128 devices in a mesh: grp: 4 (over z_hi, core), blk: 32 (over z_lo, y, x).
Axes of the slice: x: 4, y: 4, z: 4 (z_hi: 2, z_lo: 2; z = z_hi * 2 + z_lo), core: 2. Of those that a mesh axis runs over, the one named last changes fastest.
Arguments:
- raw: bfloat16 [4, 4, 4096, 256], P('grp', None, 'blk'), may hold values from -6 to 6
- raw_kin: bfloat16 [4, 4, 4, 4096], P('grp', None, None, 'blk'), may hold values from -3.2 to 20, as said below
- reader: int32 [4, 4096], P('grp', 'blk'), may hold values from 0 to 3
- event_id: int32 [4, 4096], P('grp', 'blk'), may hold values from 0 to 7, never falling along the last dimension, each value on 1 to 2048 neighbouring positions
- pre_gain: float32 [256], replicated, may hold values from 0.25 to 1.75
- w_query: bfloat16 [256, 256], replicated, may hold values from -2 to 2
- w_key: bfloat16 [256, 256], replicated, may hold values from -2 to 2
- w_value: bfloat16 [256, 256], replicated, may hold values from -0.375 to 0.375
- w_out: bfloat16 [256, 256], replicated, may hold values from -0.375 to 0.375
- post_gain: float32 [256], replicated, may hold values from 0.25 to 1.75
- pair_w1: float32 [4, 32], replicated, may hold values from -3 to 3
- pair_b1: float32 [32], replicated, may hold values from -4 to 4
- pair_w2: float32 [32, 8], replicated, may hold values from -1 to 1
Outputs:
- encoded: bfloat16 [4, 4096, 256], P('grp', 'blk')
The draws below stay inside these ranges and needn't reach their ends.
Inputs may be any that keep to these rules, and one draw needn't show every extreme that they name: `raw_kin`: rows are transverse momentum (positive), rapidity, azimuth and mass (positive). `event_id`: event numbers never fall along a group's slots; every event holds 1 to 2048 slots and some event exactly 2048.
All inputs are finite; a program needn't handle non-finite values.
Results may differ from the reference program's by a relative error of at most 0.0091.
Values may be sent and summed in bfloat16 or wider, within the bound.
A program may use at most 64 MiB of HBM per device.

```python
import math
import jax
import jax.numpy as jnp
import numpy as np
from jax import lax

D = 256
HEADS = 8
PAIR_FEAT = 4
PAIR_HID = 32
EVENTS = 8
GROUPS = 4
SLOTS = 4096
MAXLEN = 2048


def draw_raw_kin(key, part):
    shape = (GROUPS, GROUPS, SLOTS)
    trans_mom = jnp.exp(jax.random.uniform(jax.random.fold_in(key, 1), shape, jnp.float32, math.log(0.5), math.log(20.0)))
    rapidity = jax.random.uniform(jax.random.fold_in(key, 2), shape, jnp.float32, -2.5, 2.5)
    azimuth = jax.random.uniform(jax.random.fold_in(key, 3), shape, jnp.float32, -math.pi, math.pi)
    mass_val = jax.random.uniform(jax.random.fold_in(key, 4), shape, jnp.float32, 0.1, 1.0)
    return jnp.stack([trans_mom, rapidity, azimuth, mass_val], axis=2).astype(jnp.bfloat16)


def projection_parts(key):
    first = jax.random.normal(jax.random.fold_in(key, 12), (D, D), jnp.float32)
    second = jax.random.normal(jax.random.fold_in(key, 13), (D, D), jnp.float32)
    return (first, second)


def draw_w_query(key, part):
    first, second = projection_parts(key)
    value = first / math.sqrt(D)
    return jnp.clip(value, -2.0, 2.0).astype(jnp.bfloat16)


def draw_w_key(key, part):
    first, second = projection_parts(key)
    value = second / math.sqrt(D)
    return jnp.clip(value, -2.0, 2.0).astype(jnp.bfloat16)


def plant(array, own_key, low, largest):
    extent = array.shape
    place = [jax.random.randint(jax.random.fold_in(own_key, axis), (), 0, extent[axis]) for axis in range(len(extent))]
    array = array.at[tuple(place)].set(low)
    longest = extent.index(max(extent))
    place[longest] = (place[longest] + 1) % extent[longest]
    return array.at[tuple(place)].set(largest)


def steps_of(stream_key, extent, cuts, least, largest):
    level, own = 1.0, jax.random.fold_in(stream_key, 6)
    for axis_at, blocks in cuts:
        draws = jnp.exp(jax.random.uniform(jax.random.fold_in(own, axis_at), (blocks,), jnp.float32, least / len(cuts), largest / len(cuts)))
        level = level * jnp.repeat(draws, extent[axis_at] // blocks).reshape([-1 if axis == axis_at else 1 for axis in range(len(extent))])
    return level


def split_up(number_of, total, limit, lean):
    portions = [(1 << 20) // math.isqrt(rank ** lean) + 1 for rank in range(2, number_of + 1)]
    surplus, given = total - limit - (number_of - 1), [1] * (number_of - 1)
    while surplus > 0:
        movable = [i for i in range(number_of - 1) if given[i] < limit]
        mass, budget = sum([portions[i] for i in movable]), surplus
        for i in movable:
            addition = min(limit - given[i], max(1, budget * portions[i] // mass), surplus)
            given[i] = given[i] + addition
            surplus = surplus - addition
    return np.array([limit] + given)


def uneven(own_key, amount, total, reach, skew):
    if amount == 2:
        one = jax.random.randint(own_key, (), max(1, total - reach), min(reach, total - 1) + 1)
        return jnp.stack([one, total - one])
    sizes = jnp.asarray(split_up(amount, total, reach, skew), jnp.int32)
    couples = (amount - 1) // 2
    source_of, sink = sizes[1:1 + 2 * couples:2], sizes[2:2 + 2 * couples:2]
    margin = jnp.minimum(source_of - 1, reach - sink)
    shifted = jax.random.randint(jax.random.fold_in(own_key, 1), (couples,), 0, 1 << 20) % (margin + 1)
    sizes = sizes.at[1:1 + 2 * couples:2].set(source_of - shifted).at[2:2 + 2 * couples:2].set(sink + shifted)
    return sizes[jax.random.permutation(jax.random.fold_in(own_key, 2), amount)]


def normal_values(rng, extent, scale, bound, shards=(), kind=jnp.bfloat16):
    drawn = scale * jax.random.normal(rng, extent, jnp.float32)
    if shards:
        drawn = drawn * steps_of(rng, extent, shards, -0.22, 0.18)
    return jnp.clip(drawn, -bound, bound).astype(kind)


def setup_inputs(seed: int = 0) -> dict:
    streams_of = jax.random.split(jax.random.key(seed), 14)
    raw = normal_values(streams_of[0], (GROUPS, GROUPS, SLOTS, D), 1.0, 6.0, ((0, 4), (2, 32)))
    raw_kin = draw_raw_kin(jax.random.fold_in(streams_of[13], 71), 0)
    reader = plant(jax.random.randint(streams_of[2], (GROUPS, SLOTS), 0, GROUPS), jax.random.fold_in(streams_of[2], 1), 0, GROUPS - 1).astype(jnp.int32)
    event_id = jax.vmap(lambda own: jnp.searchsorted(jnp.cumsum(uneven(own, EVENTS, SLOTS, MAXLEN, 2)), jnp.arange(SLOTS), side="right"))(jax.random.split(streams_of[3], GROUPS)).reshape((GROUPS, SLOTS)).astype(jnp.int32)
    pre_gain = jnp.clip(1.0 + 0.15 * jax.random.normal(streams_of[4], (D,), jnp.float32), 0.25, 1.75)
    w_query = draw_w_query(jax.random.fold_in(streams_of[13], 71), 0)
    w_key = draw_w_key(jax.random.fold_in(streams_of[13], 71), 0)
    w_value = normal_values(streams_of[7], (D, D), D ** -0.5, 0.375)
    w_out = normal_values(streams_of[8], (D, D), D ** -0.5, 0.375)
    post_gain = jnp.clip(1.0 + 0.15 * jax.random.normal(streams_of[9], (D,), jnp.float32), 0.25, 1.75)
    pair_w1 = normal_values(streams_of[10], (PAIR_FEAT, PAIR_HID), PAIR_FEAT ** -0.5, 3.0, (), jnp.float32)
    pair_b1 = normal_values(streams_of[11], (PAIR_HID,), 1.0, 4.0, (), jnp.float32)
    pair_w2 = normal_values(streams_of[12], (PAIR_HID, HEADS), PAIR_HID ** -0.5, 1.0, (), jnp.float32)
    return dict(raw=raw, raw_kin=raw_kin, reader=reader, event_id=event_id, pre_gain=pre_gain, w_query=w_query, w_key=w_key, w_value=w_value, w_out=w_out, post_gain=post_gain, pair_w1=pair_w1, pair_b1=pair_b1, pair_w2=pair_w2)


exact_mode = lax.Precision.HIGHEST

def layer_norm(rows, gain):
    center = rows - lax.optimization_barrier(jnp.mean(rows, axis=-1, keepdims=True))
    spread = lax.optimization_barrier(jnp.mean(center * center, axis=-1, keepdims=True))
    return center * lax.rsqrt(spread + 1e-05) * gain

def particle_terms(kinematics):
    trans_mom = kinematics[0]
    rapidity = kinematics[1]
    azimuth = kinematics[2]
    mass_val = kinematics[3]
    trans_mass = jnp.sqrt(trans_mom * trans_mom + mass_val * mass_val)
    return (trans_mom, rapidity, jnp.cos(azimuth), jnp.sin(azimuth), trans_mass, mass_val * mass_val)

def pair_bias(query_terms, key_terms, pair_w1, pair_b1, pair_w2):
    q_mom, q_rap, q_cos, q_sin, q_trans, q_mass = [term[:, None] for term in query_terms]
    k_mom, k_rap, k_cos, k_sin, k_trans, k_mass = [term[None, :] for term in key_terms]
    rap_gap = q_rap - k_rap
    cos_gap = q_cos * k_cos + q_sin * k_sin
    dist_sq = rap_gap * rap_gap + 2.0 * (1.0 - cos_gap)
    low_mom = jnp.minimum(q_mom, k_mom)
    mass_sq = q_mass + k_mass + 2.0 * (q_trans * k_trans * jnp.cosh(rap_gap) - q_mom * k_mom * cos_gap)
    features = jnp.stack([jnp.log1p(dist_sq), jnp.log1p(low_mom * low_mom * dist_sq), low_mom / (q_mom + k_mom), jnp.log1p(mass_sq)])
    hidden = jax.nn.gelu(jnp.einsum('cqk,ch->hqk', features, pair_w1, precision=exact_mode) + pair_b1[:, None, None], approximate=True)
    return jnp.einsum('hqk,hn->nqk', hidden, pair_w2, precision=exact_mode)

def reference(raw, raw_kin, reader, event_id, pre_gain, w_query, w_key, w_value, w_out, post_gain, pair_w1, pair_b1, pair_w2):
    groups = raw.shape[0]
    slots = raw.shape[2]
    width = raw.shape[3]
    heads = pair_w2.shape[1]
    head_size = width // heads
    block_rows = min(256, slots)
    results = []
    for group in range(groups):
        picked = reader[group][None, :] == jnp.arange(groups, dtype=jnp.int32)[:, None]
        tokens = lax.optimization_barrier(jnp.sum(jnp.where(picked[:, :, None], raw[:, group].astype(jnp.float32), 0.0), axis=0))
        kinematics = lax.optimization_barrier(jnp.sum(jnp.where(picked[:, None, :], raw_kin[:, group].astype(jnp.float32), 0.0), axis=0))
        normed = layer_norm(tokens, pre_gain).astype(jnp.bfloat16)
        queries = jnp.dot(normed, w_query, preferred_element_type=jnp.float32).astype(jnp.bfloat16)
        keys = jnp.dot(normed, w_key, preferred_element_type=jnp.float32).astype(jnp.bfloat16)
        values = jnp.dot(normed, w_value, preferred_element_type=jnp.float32).astype(jnp.bfloat16)
        terms = particle_terms(kinematics)
        group_ids = event_id[group]
        key_heads = keys.astype(jnp.float32).T.reshape(heads, head_size, slots)
        value_heads = values.astype(jnp.float32).T.reshape(heads, head_size, slots)

        def query_block(index):
            start = (index * block_rows).astype(jnp.int32)
            block_q = lax.dynamic_slice_in_dim(queries, start, block_rows, 0).astype(jnp.float32)
            block_q = block_q.reshape(block_rows, heads, head_size)
            block_terms = tuple((lax.dynamic_slice_in_dim(term, start, block_rows, 0) for term in terms))
            block_ids = lax.dynamic_slice_in_dim(group_ids, start, block_rows, 0)
            scores = jnp.einsum('qhd,hdk->hqk', block_q, key_heads, precision=exact_mode) * head_size ** (-0.5)
            scores = scores + pair_bias(block_terms, terms, pair_w1, pair_b1, pair_w2)
            live = (block_ids[:, None] == group_ids[None, :])[None]
            top = lax.optimization_barrier(jnp.max(jnp.where(live, scores, jnp.float32(-1e+30)), axis=2))
            weights = jnp.where(live, jnp.exp(scores - top[:, :, None]), 0.0)
            totals = lax.optimization_barrier(jnp.sum(weights, axis=2))
            rounded = lax.optimization_barrier(weights.astype(jnp.bfloat16)).astype(jnp.float32)
            mixed = jnp.einsum('hqk,hdk->qhd', rounded, value_heads, precision=exact_mode)
            mixed = mixed / totals.T[:, :, None]
            return mixed.reshape(block_rows, width).astype(jnp.bfloat16)
        attended = lax.map(query_block, jnp.arange(slots // block_rows, dtype=jnp.int32)).reshape(slots, width)
        mixed_out = jnp.dot(attended, w_out, preferred_element_type=jnp.float32)
        results.append(layer_norm(mixed_out, post_gain).astype(jnp.bfloat16))
    return jnp.stack(results)
```

```python
import functools
import math

import jax
import jax.numpy as jnp
from jax import lax
from jax.experimental import pallas as pl
from jax.experimental.pallas import tpu as pltpu
from jax.sharding import PartitionSpec as P

MESH = pl.DeviceIdType.MESH
F32 = jnp.float32
BF16 = jnp.bfloat16
HIGHEST = lax.Precision.HIGHEST

KIN_ROWS = 16
GROUP = 8
UNIT = 16
TILE = 256

GELU_A = math.sqrt(2.0 / math.pi)
GELU_B = GELU_A * 0.044715
GELU_S = GELU_B ** (-1.0 / 3.0)
ALPHA = GELU_A * GELU_S
LOG2E = 1.0 / math.log(2.0)


def layer_norm(rows, gain):
    center = rows - jnp.mean(rows, axis=-1, keepdims=True)
    spread = jnp.mean(center * center, axis=-1, keepdims=True)
    return center * lax.rsqrt(spread + 1e-05) * gain


def exchange_kernel(
    n_grp,
    n_blk,
    raw_ref,
    kin_ref,
    reader_ref,
    event_ref,
    gain_ref,
    out_ref,
    inbox,
    kin_send,
    kin_in,
    block,
    send_sem,
    recv_sem,
    kin_send_sem,
    kin_recv_sem,
    all_send_sem,
    all_recv_sem,
    own_sem,
):
    g = lax.axis_index("grp")
    b = lax.axis_index("blk")
    slots = raw_ref.shape[2]
    barrier = pltpu.get_barrier_semaphore()
    for k in range(1, n_grp):
        pl.semaphore_signal(
            barrier, inc=1, device_id={"grp": lax.rem(g + k, n_grp)}, device_id_type=MESH
        )
    for k in range(1, n_blk):
        pl.semaphore_signal(
            barrier, inc=1, device_id={"blk": lax.rem(b + k, n_blk)}, device_id_type=MESH
        )
    kin_send[...] = jnp.zeros_like(kin_send)
    for k in range(n_grp):
        kin_send[k, 0:4, :] = kin_ref[0, k].astype(F32)
    pl.semaphore_wait(barrier, n_grp + n_blk - 2)

    copies = []
    for k in range(1, n_grp):
        to = lax.rem(g + k, n_grp)
        copy = pltpu.make_async_remote_copy(
            src_ref=raw_ref.at[0, to],
            dst_ref=inbox.at[n_grp - k],
            send_sem=send_sem.at[k],
            recv_sem=recv_sem.at[n_grp - k],
            device_id={"grp": to},
            device_id_type=MESH,
        )
        kin_copy = pltpu.make_async_remote_copy(
            src_ref=kin_send.at[to],
            dst_ref=kin_in.at[n_grp - k],
            send_sem=kin_send_sem.at[k],
            recv_sem=kin_recv_sem.at[n_grp - k],
            device_id={"grp": to},
            device_id_type=MESH,
        )
        copy.start()
        kin_copy.start()
        copies += [copy, kin_copy]

    reader = reader_ref[...]
    wanted = lax.rem(reader - g + n_grp, n_grp)
    column = jnp.broadcast_to(wanted, (slots, slots)).T
    kin = jnp.where(wanted == 0, kin_send[g, 0:4, :], 0.0)
    halves = [
        jnp.where(column == 0, raw_ref[0, g][:, h : h + slots].astype(F32), 0.0)
        for h in range(0, raw_ref.shape[3], slots)
    ]
    for copy in copies:
        copy.wait()
    for k in range(1, n_grp):
        kin = kin + jnp.where(wanted == k, kin_in[k, 0:4, :], 0.0)
        halves = [
            half
            + jnp.where(column == k, inbox[k][:, i * slots : (i + 1) * slots].astype(F32), 0.0)
            for i, half in enumerate(halves)
        ]
    tokens = jnp.concatenate(halves, axis=1)
    block[0:slots, :] = layer_norm(tokens, gain_ref[...]).astype(BF16)
    tail = jnp.concatenate(
        [
            jnp.concatenate(
                [kin, event_ref[...].astype(F32), jnp.zeros((KIN_ROWS - 5, slots), F32)], axis=0
            ),
            jnp.zeros((KIN_ROWS, raw_ref.shape[3] - slots), F32),
        ],
        axis=1,
    )
    block[slots : slots + KIN_ROWS, :] = tail.astype(BF16)

    own = pltpu.make_async_copy(block, out_ref.at[b], own_sem)
    own.start()

    def send(k, carry):
        pltpu.make_async_remote_copy(
            src_ref=block,
            dst_ref=out_ref.at[b],
            send_sem=all_send_sem,
            recv_sem=all_recv_sem,
            device_id={"blk": lax.rem(b + k, n_blk)},
            device_id_type=MESH,
        ).start()
        return carry

    lax.fori_loop(1, n_blk, send, 0)
    own.wait()
    every = pltpu.make_async_remote_copy(
        src_ref=out_ref.at[pl.ds(0, n_blk - 1)],
        dst_ref=out_ref.at[pl.ds(0, n_blk - 1)],
        send_sem=all_send_sem,
        recv_sem=all_recv_sem,
        device_id={"blk": lax.rem(b + 1, n_blk)},
        device_id_type=MESH,
    )
    every.wait()


def split_two(value):
    high = value.astype(BF16)
    low = (value - high.astype(F32)).astype(BF16)
    return high, low


def spread_over(weight):
    m, c = weight.shape
    up = (
        lax.broadcasted_iota(jnp.int32, (m * GROUP, m), 0) // GROUP
        == lax.broadcasted_iota(jnp.int32, (m * GROUP, m), 1)
    ).astype(F32)
    across = (
        lax.broadcasted_iota(jnp.int32, (c, c * GROUP), 1) // GROUP
        == lax.broadcasted_iota(jnp.int32, (c, c * GROUP), 0)
    ).astype(F32)
    tall = jnp.dot(up, weight, precision=HIGHEST, preferred_element_type=F32)
    wide = jnp.dot(tall, across, precision=HIGHEST, preferred_element_type=F32)
    same = (
        lax.broadcasted_iota(jnp.int32, (m * GROUP, c * GROUP), 0) % GROUP
        == lax.broadcasted_iota(jnp.int32, (m * GROUP, c * GROUP), 1) % GROUP
    )
    return jnp.where(same, wide, 0.0)


def attend_kernel(
    heads,
    x_ref,
    wq_ref,
    wk_ref,
    wv_ref,
    wo_ref,
    gain_ref,
    w1_ref,
    b1_ref,
    w2_ref,
    out_ref,
    kt_ref,
    v_ref,
    terms,
    q_terms,
    q_ref,
    qm_ref,
    s_ref,
    acc_ref,
    att_ref,
    wfirst,
    wsecond,
):
    n_blk = x_ref.shape[0]
    own_rows = out_ref.shape[0]
    width = out_ref.shape[1]
    head_size = width // heads
    hid = w1_ref.shape[1]
    feats = w1_ref.shape[0]
    per_tile = TILE // own_rows
    b = lax.axis_index("blk")
    root = math.sqrt(head_size)

    w1 = w1_ref[...]
    b1 = b1_ref[...]
    w2 = w2_ref[...]
    first = jnp.concatenate([w1, b1, jnp.zeros((8 - feats - 1, hid), F32)], axis=0)
    line = jnp.dot(first, w2, precision=HIGHEST, preferred_element_type=F32) * (0.5 * root)
    stacked = jnp.concatenate([first.T * (1.0 / GELU_S), line.T], axis=0)
    big = spread_over(stacked)
    high, low = split_two(big)
    part = feats * GROUP
    wfirst[:, 0:part] = high[:, 0:part]
    wfirst[:, part : 2 * part] = high[:, 0:part]
    wfirst[:, 2 * part : 3 * part] = low[:, 0:part]
    wfirst[:, 3 * part : 3 * part + GROUP] = high[:, part : part + GROUP]
    wfirst[:, 3 * part + GROUP : 3 * part + 2 * GROUP] = low[:, part : part + GROUP]
    wsecond[...] = spread_over(w2.T * (0.5 * root * GELU_S)).astype(BF16)

    tab = x_ref[:, own_rows : own_rows + 8, 0:own_rows].astype(F32)
    mom, rap, azi, mass, ids = [tab[:, i, :] for i in range(5)]
    trans = jnp.sqrt(mom * mom + mass * mass)
    grow = jnp.exp(rap)
    shrink = jnp.exp(-rap)
    for i, term in enumerate(
        [mom, rap, jnp.cos(azi), jnp.sin(azi), trans * grow, trans * shrink, mass * mass, ids]
    ):
        terms[i] = term
    for i in range(8):
        q_terms[i] = jnp.broadcast_to(terms[i, pl.ds(b, 1), :], (own_rows, own_rows)).T

    q_ref[...] = jnp.dot(
        x_ref[b, 0:own_rows, :], wq_ref[...], preferred_element_type=F32
    )

    n_units = own_rows // UNIT
    lows = []
    ends = []
    for u in range(n_units):
        begin = q_terms[7, pl.ds(u * UNIT, 1), :]
        finish = q_terms[7, pl.ds(u * UNIT + UNIT - 1, 1), :]
        lows.append(jnp.sum((ids < begin).astype(jnp.int32)) // TILE)
        ends.append((jnp.sum((ids <= finish).astype(jnp.int32)) + TILE - 1) // TILE)

    wkt = wk_ref[...].astype(F32).T.astype(BF16)

    def project(t, carry):
        for i in range(per_tile):
            rows = x_ref[t * per_tile + i, 0:own_rows, :]
            start = pl.multiple_of(t * TILE + i * own_rows, own_rows)
            kt_ref[:, pl.ds(start, own_rows)] = lax.dot_general(
                wkt, rows, (((1,), (1,)), ((), ())), preferred_element_type=F32
            ).astype(BF16)
            v_ref[pl.ds(start, own_rows), :] = jnp.dot(
                rows, wv_ref[...], preferred_element_type=F32
            ).astype(BF16)
        return carry

    lax.fori_loop(lows[0], ends[-1], project, 0)

    lane_head = lax.broadcasted_iota(jnp.int32, (GROUP, width), 1) // head_size
    groups = UNIT // GROUP
    rows_g = heads * GROUP

    for u in range(n_units):
        for g in range(groups):
            base = u * UNIT + g * GROUP
            rows = q_ref[pl.ds(base, GROUP), :]
            qm_ref[g * rows_g : (g + 1) * rows_g, :] = jnp.concatenate(
                [jnp.where(lane_head == h, rows, 0.0) for h in range(heads)], axis=0
            ).astype(BF16)

        def score(t, run_max, u=u):
            start = pl.multiple_of(t * TILE, TILE)
            products = jnp.dot(
                qm_ref[...], kt_ref[:, pl.ds(start, TILE)], preferred_element_type=F32
            )
            parts = []
            for g in range(groups):
                base = u * UNIT + g * GROUP
                qt = [q_terms[i, pl.ds(base, GROUP), :] for i in range(8)]
                columns = []
                lives = []
                for i in range(per_tile):
                    kt = [terms[j, pl.ds(t * per_tile + i, 1), :] for j in range(8)]
                    gap = qt[1] - kt[1]
                    cos_gap = qt[2] * kt[2] + qt[3] * kt[3]
                    dist = gap * gap + (2.0 - 2.0 * cos_gap)
                    small = jnp.minimum(qt[0], kt[0])
                    msq = (
                        qt[6]
                        + kt[6]
                        + (qt[4] * kt[5] + qt[5] * kt[4] - 2.0 * (qt[0] * kt[0] * cos_gap))
                    )
                    f = [
                        jnp.log(1.0 + dist),
                        jnp.log(1.0 + small * small * dist),
                        small / (qt[0] + kt[0]),
                        jnp.log(1.0 + msq),
                    ]
                    f = jnp.concatenate(f, axis=0)
                    fh, fl = split_two(f)
                    columns.append(
                        jnp.concatenate([fh, fl, fh, jnp.ones((2 * GROUP, own_rows), BF16)], axis=0)
                    )
                    lives.append(qt[7] == kt[7])
                x = jnp.concatenate(columns, axis=1)
                z = jnp.dot(wfirst[...], x, preferred_element_type=F32)
                inner = z[0 : hid * GROUP].astype(BF16)
                turn = jnp.tanh(inner * (ALPHA + inner * inner))
                bias = (
                    jnp.dot(wsecond[...], inner * turn, preferred_element_type=F32)
                    + z[hid * GROUP :]
                )
                s = products[g * rows_g : (g + 1) * rows_g] + bias
                live = jnp.concatenate(lives, axis=1)
                s = jnp.where(live[None], s.reshape(heads, GROUP, TILE), -1e30)
                parts.append(s.reshape(rows_g, TILE))
            s = jnp.concatenate(parts, axis=0)
            s_ref[:, pl.ds(start, TILE)] = s
            for i in range(0, TILE, 128):
                run_max = jnp.maximum(run_max, s[:, i : i + 128])
            return run_max

        run_max = lax.fori_loop(
            lows[u], ends[u], score, jnp.full((groups * rows_g, 128), -1e30, F32)
        )
        top = jnp.max(run_max, axis=1, keepdims=True)
        acc_ref[...] = jnp.zeros_like(acc_ref)

        def gather(t, total):
            start = pl.multiple_of(t * TILE, TILE)
            weight = jnp.exp2((s_ref[:, pl.ds(start, TILE)] - top) * (LOG2E / root))
            acc_ref[...] += jnp.dot(
                weight.astype(BF16), v_ref[pl.ds(start, TILE), :], preferred_element_type=F32
            )
            for i in range(0, TILE, 128):
                total = total + weight[:, i : i + 128]
            return total

        total = lax.fori_loop(
            lows[u], ends[u], gather, jnp.zeros((groups * rows_g, 128), F32)
        )
        total = jnp.sum(total, axis=1, keepdims=True)
        for g in range(groups):
            out = jnp.zeros((GROUP, width), F32)
            for h in range(heads):
                at = g * rows_g + h * GROUP
                scaled = acc_ref[at : at + GROUP, :] / total[at : at + GROUP]
                out = jnp.where(lane_head == h, scaled, out)
            att_ref[u * UNIT + g * GROUP : u * UNIT + (g + 1) * GROUP, :] = out

    mixed = jnp.dot(att_ref[...].astype(BF16), wo_ref[...], preferred_element_type=F32)
    out_ref[...] = layer_norm(mixed, gain_ref[...]).astype(BF16)


def shards(
    n_grp,
    n_blk,
    raw,
    raw_kin,
    reader,
    event_id,
    pre_gain,
    w_query,
    w_key,
    w_value,
    w_out,
    post_gain,
    pair_w1,
    pair_b1,
    pair_w2,
):
    slots, width = raw.shape[2], raw.shape[3]
    heads = pair_w2.shape[1]
    vmem = pl.BlockSpec(memory_space=pltpu.VMEM)
    gathered = pl.pallas_call(
        functools.partial(exchange_kernel, n_grp, n_blk),
        out_shape=jax.ShapeDtypeStruct((n_blk, slots + KIN_ROWS, width), BF16),
        in_specs=[vmem] * 5,
        out_specs=pl.BlockSpec(memory_space=pl.ANY),
        scratch_shapes=[
            pltpu.VMEM((n_grp, slots, width), BF16),
            pltpu.VMEM((n_grp, 8, slots), F32),
            pltpu.VMEM((n_grp, 8, slots), F32),
            pltpu.VMEM((slots + KIN_ROWS, width), BF16),
            pltpu.SemaphoreType.DMA((n_grp,)),
            pltpu.SemaphoreType.DMA((n_grp,)),
            pltpu.SemaphoreType.DMA((n_grp,)),
            pltpu.SemaphoreType.DMA((n_grp,)),
            pltpu.SemaphoreType.DMA,
            pltpu.SemaphoreType.DMA,
            pltpu.SemaphoreType.DMA,
        ],
        compiler_params=pltpu.CompilerParams(collective_id=0, has_side_effects=True),
        name="exchange",
    )(raw, raw_kin, reader, event_id, pre_gain[None])

    keys = n_blk * slots
    feats, hid = pair_w1.shape
    rows_u = heads * UNIT
    encoded = pl.pallas_call(
        functools.partial(attend_kernel, heads),
        out_shape=jax.ShapeDtypeStruct((slots, width), BF16),
        in_specs=[vmem] * 9,
        out_specs=vmem,
        scratch_shapes=[
            pltpu.VMEM((width, keys), BF16),
            pltpu.VMEM((keys, width), BF16),
            pltpu.VMEM((8, n_blk, slots), F32),
            pltpu.VMEM((8, slots, slots), F32),
            pltpu.VMEM((slots, width), F32),
            pltpu.VMEM((rows_u, width), BF16),
            pltpu.VMEM((rows_u, keys), F32),
            pltpu.VMEM((rows_u, width), F32),
            pltpu.VMEM((slots, width), F32),
            pltpu.VMEM(((hid + heads) * GROUP, (3 * feats + 2) * GROUP), BF16),
            pltpu.VMEM((heads * GROUP, hid * GROUP), BF16),
        ],
        compiler_params=pltpu.CompilerParams(vmem_limit_bytes=40 * 1024 * 1024),
        name="attend",
    )(
        gathered,
        w_query,
        w_key,
        w_value,
        w_out,
        post_gain[None],
        pair_w1,
        pair_b1[None],
        pair_w2,
    )
    return encoded[None]


def solution(mesh):
    in_specs = (
        P("grp", None, "blk", None),
        P("grp", None, None, "blk"),
        P("grp", "blk"),
        P("grp", "blk"),
        P(),
        P(),
        P(),
        P(),
        P(),
        P(),
        P(),
        P(),
        P(),
    )
    out_specs = P("grp", "blk", None)
    body = functools.partial(shards, mesh.shape["grp"], mesh.shape["blk"])
    return jax.shard_map(body, mesh=mesh, in_specs=in_specs, out_specs=out_specs, check_vma=False)
```

```python
import functools
import math

import jax
import jax.numpy as jnp
from jax import lax
from jax.experimental import pallas as pl
from jax.experimental.pallas import tpu as pltpu
from jax.sharding import PartitionSpec as P

MESH = pl.DeviceIdType.MESH
F32 = jnp.float32
BF16 = jnp.bfloat16
HIGHEST = lax.Precision.HIGHEST

KIN_ROWS = 16
GROUP = 8
UNIT = 16
TILE = 256

GELU_A = math.sqrt(2.0 / math.pi)
GELU_B = GELU_A * 0.044715
GELU_S = GELU_B ** (-1.0 / 3.0)
ALPHA = GELU_A * GELU_S
LOG2E = 1.0 / math.log(2.0)


def layer_norm(rows, gain):
    center = rows - jnp.mean(rows, axis=-1, keepdims=True)
    spread = jnp.mean(center * center, axis=-1, keepdims=True)
    return center * lax.rsqrt(spread + 1e-05) * gain


def exchange_kernel(
    n_grp,
    n_blk,
    raw_ref,
    kin_ref,
    reader_ref,
    event_ref,
    gain_ref,
    out_ref,
    inbox,
    kin_send,
    kin_in,
    block,
    send_sem,
    recv_sem,
    kin_send_sem,
    kin_recv_sem,
    all_send_sem,
    all_recv_sem,
    own_sem,
):
    g = lax.axis_index("grp")
    b = lax.axis_index("blk")
    slots = raw_ref.shape[2]
    barrier = pltpu.get_barrier_semaphore()
    for k in range(1, n_grp):
        pl.semaphore_signal(
            barrier, inc=1, device_id={"grp": lax.rem(g + k, n_grp)}, device_id_type=MESH
        )
    for k in range(1, n_blk):
        pl.semaphore_signal(
            barrier, inc=1, device_id={"blk": lax.rem(b + k, n_blk)}, device_id_type=MESH
        )
    kin_send[...] = jnp.zeros_like(kin_send)
    for k in range(n_grp):
        kin_send[k, 0:4, :] = kin_ref[0, k].astype(F32)
    pl.semaphore_wait(barrier, n_grp + n_blk - 2)

    copies = []
    for k in range(1, n_grp):
        to = lax.rem(g + k, n_grp)
        copy = pltpu.make_async_remote_copy(
            src_ref=raw_ref.at[0, to],
            dst_ref=inbox.at[n_grp - k],
            send_sem=send_sem.at[k],
            recv_sem=recv_sem.at[n_grp - k],
            device_id={"grp": to},
            device_id_type=MESH,
        )
        kin_copy = pltpu.make_async_remote_copy(
            src_ref=kin_send.at[to],
            dst_ref=kin_in.at[n_grp - k],
            send_sem=kin_send_sem.at[k],
            recv_sem=kin_recv_sem.at[n_grp - k],
            device_id={"grp": to},
            device_id_type=MESH,
        )
        copy.start()
        kin_copy.start()
        copies += [copy, kin_copy]

    reader = reader_ref[...]
    wanted = lax.rem(reader - g + n_grp, n_grp)
    column = jnp.broadcast_to(wanted, (slots, slots)).T
    kin = jnp.where(wanted == 0, kin_send[g, 0:4, :], 0.0)
    halves = [
        jnp.where(column == 0, raw_ref[0, g][:, h : h + slots].astype(F32), 0.0)
        for h in range(0, raw_ref.shape[3], slots)
    ]
    for copy in copies:
        copy.wait()
    for k in range(1, n_grp):
        kin = kin + jnp.where(wanted == k, kin_in[k, 0:4, :], 0.0)
        halves = [
            half
            + jnp.where(column == k, inbox[k][:, i * slots : (i + 1) * slots].astype(F32), 0.0)
            for i, half in enumerate(halves)
        ]
    tokens = jnp.concatenate(halves, axis=1)
    block[0:slots, :] = layer_norm(tokens, gain_ref[...]).astype(BF16)
    tail = jnp.concatenate(
        [
            jnp.concatenate(
                [kin, event_ref[...].astype(F32), jnp.zeros((KIN_ROWS - 5, slots), F32)], axis=0
            ),
            jnp.zeros((KIN_ROWS, raw_ref.shape[3] - slots), F32),
        ],
        axis=1,
    )
    block[slots : slots + KIN_ROWS, :] = tail.astype(BF16)

    own = pltpu.make_async_copy(block, out_ref.at[b], own_sem)
    own.start()

    def send(k, carry):
        pltpu.make_async_remote_copy(
            src_ref=block,
            dst_ref=out_ref.at[b],
            send_sem=all_send_sem,
            recv_sem=all_recv_sem,
            device_id={"blk": lax.rem(b + k, n_blk)},
            device_id_type=MESH,
        ).start()
        return carry

    lax.fori_loop(1, n_blk, send, 0)
    own.wait()
    every = pltpu.make_async_remote_copy(
        src_ref=out_ref.at[pl.ds(0, n_blk - 1)],
        dst_ref=out_ref.at[pl.ds(0, n_blk - 1)],
        send_sem=all_send_sem,
        recv_sem=all_recv_sem,
        device_id={"blk": lax.rem(b + 1, n_blk)},
        device_id_type=MESH,
    )
    every.wait()


def split_two(value):
    high = value.astype(BF16)
    low = (value - high.astype(F32)).astype(BF16)
    return high, low


def spread_over(weight):
    m, c = weight.shape
    up = (
        lax.broadcasted_iota(jnp.int32, (m * GROUP, m), 0) // GROUP
        == lax.broadcasted_iota(jnp.int32, (m * GROUP, m), 1)
    ).astype(F32)
    across = (
        lax.broadcasted_iota(jnp.int32, (c, c * GROUP), 1) // GROUP
        == lax.broadcasted_iota(jnp.int32, (c, c * GROUP), 0)
    ).astype(F32)
    tall = jnp.dot(up, weight, precision=HIGHEST, preferred_element_type=F32)
    wide = jnp.dot(tall, across, precision=HIGHEST, preferred_element_type=F32)
    same = (
        lax.broadcasted_iota(jnp.int32, (m * GROUP, c * GROUP), 0) % GROUP
        == lax.broadcasted_iota(jnp.int32, (m * GROUP, c * GROUP), 1) % GROUP
    )
    return jnp.where(same, wide, 0.0)


def attend_kernel(
    heads,
    x_ref,
    wq_ref,
    wk_ref,
    wv_ref,
    wo_ref,
    gain_ref,
    w1_ref,
    b1_ref,
    w2_ref,
    out_ref,
    kt_ref,
    v_ref,
    terms,
    q_terms,
    qm_ref,
    s_ref,
    top_ref,
    total_ref,
    acc_ref,
    att_ref,
    wfirst,
    wline,
    wsecond,
    fresh,
    aged,
    turned,
    weight_ref,
    limits,
):
    own_rows, width = out_ref.shape
    head_size = width // heads
    feats, hid = w1_ref.shape
    per_tile = TILE // own_rows
    b = lax.axis_index("blk")
    root = math.sqrt(head_size)
    groups = UNIT // GROUP
    rows_g = heads * GROUP
    rows_u = groups * rows_g
    n_units = own_rows // UNIT

    w1 = w1_ref[...]
    b1 = b1_ref[...]
    w2 = w2_ref[...]
    first = jnp.concatenate([w1, b1, jnp.zeros((8 - feats - 1, hid), F32)], axis=0)
    line = jnp.dot(first, w2, precision=HIGHEST, preferred_element_type=F32) * (0.5 * root)
    part = feats * GROUP

    def lay(ref, weight):
        high, low = split_two(spread_over(weight))
        ref[:, 0:part] = high[:, 0:part]
        ref[:, part : 2 * part] = high[:, 0:part]
        ref[:, 2 * part : 3 * part] = low[:, 0:part]
        ref[:, 3 * part : 3 * part + GROUP] = high[:, part : part + GROUP]
        ref[:, 3 * part + GROUP : 3 * part + 2 * GROUP] = low[:, part : part + GROUP]

    lay(wfirst, first.T * (1.0 / GELU_S))
    lay(wline, line.T)
    wsecond[...] = spread_over(w2.T * (0.5 * root * GELU_S)).astype(BF16)

    tab = x_ref[:, own_rows : own_rows + 8, 0:own_rows].astype(F32)
    mom, rap, azi, mass, ids = [tab[:, i, :] for i in range(5)]
    trans = jnp.sqrt(mom * mom + mass * mass)
    grow = jnp.exp(rap)
    shrink = jnp.exp(-rap)
    for i, term in enumerate(
        [mom, rap, jnp.cos(azi), jnp.sin(azi), trans * grow, trans * shrink, mass * mass, ids]
    ):
        terms[i] = term
    for i in range(8):
        q_terms[i] = jnp.broadcast_to(terms[i, pl.ds(b, 1), :], (own_rows, own_rows)).T

    for u in range(n_units):
        begin = q_terms[7, pl.ds(u * UNIT, 1), :]
        finish = q_terms[7, pl.ds(u * UNIT + UNIT - 1, 1), :]
        limits[0, u] = jnp.sum((ids < begin).astype(jnp.int32)) // TILE
        limits[1, u] = (jnp.sum((ids <= finish).astype(jnp.int32)) + TILE - 1) // TILE

    wkt = wk_ref[...].astype(F32).T.astype(BF16)

    def project(t, carry):
        for i in range(per_tile):
            rows = x_ref[t * per_tile + i, 0:own_rows, :]
            start = pl.multiple_of(t * TILE + i * own_rows, own_rows)
            kt_ref[:, pl.ds(start, own_rows)] = lax.dot_general(
                wkt, rows, (((1,), (1,)), ((), ())), preferred_element_type=F32
            ).astype(BF16)
            v_ref[pl.ds(start, own_rows), :] = jnp.dot(
                rows, wv_ref[...], preferred_element_type=F32
            ).astype(BF16)
        return carry

    lax.fori_loop(limits[0, 0], limits[1, n_units - 1], project, 0)

    lane_head = lax.broadcasted_iota(jnp.int32, (GROUP, width), 1) // head_size
    queries = jnp.dot(x_ref[b, 0:own_rows, :], wq_ref[...], preferred_element_type=F32)
    for base in range(0, own_rows, GROUP):
        rows = queries[base : base + GROUP]
        qm_ref[base * heads : base * heads + rows_g, :] = jnp.concatenate(
            [jnp.where(lane_head == h, rows, 0.0) for h in range(heads)], axis=0
        ).astype(BF16)

    top_ref[...] = jnp.full_like(top_ref, -1e30)
    total_ref[...] = jnp.zeros_like(total_ref)
    acc_ref[...] = jnp.zeros_like(acc_ref)

    def following(u, t):
        more = t + 1 < limits[1, u]
        then = jnp.where(more, u, jnp.minimum(u + 1, n_units - 1))
        return then, jnp.where(more, t + 1, limits[0, then])

    steps = limits[1, 0] - limits[0, 0]
    for u in range(1, n_units):
        steps = steps + limits[1, u] - limits[0, u]

    def features(u, t):
        for g in range(groups):
            base = pl.multiple_of(u * UNIT + g * GROUP, GROUP)
            qt = [q_terms[i, pl.ds(base, GROUP), :] for i in range(7)]
            columns = []
            for i in range(per_tile):
                kt = [terms[j, pl.ds(t * per_tile + i, 1), :] for j in range(7)]
                gap = qt[1] - kt[1]
                cos_gap = qt[2] * kt[2] + qt[3] * kt[3]
                dist = gap * gap + (2.0 - 2.0 * cos_gap)
                small = jnp.minimum(qt[0], kt[0])
                msq = (
                    qt[6]
                    + kt[6]
                    + (qt[4] * kt[5] + qt[5] * kt[4] - 2.0 * (qt[0] * kt[0] * cos_gap))
                )
                f = [
                    jnp.log(1.0 + dist),
                    jnp.log(1.0 + small * small * dist),
                    small / (qt[0] + kt[0]),
                    jnp.log(1.0 + msq),
                ]
                fh, fl = split_two(jnp.concatenate(f, axis=0))
                columns.append(
                    jnp.concatenate([fh, fl, fh, jnp.ones((2 * GROUP, own_rows), BF16)], axis=0)
                )
            fresh[g] = jnp.concatenate(columns, axis=1)

    def gelus():
        for g in range(groups):
            x = fresh[g]
            aged[g] = x
            inner = jnp.dot(wfirst[...], x, preferred_element_type=F32).astype(BF16)
            turned[g] = inner * jnp.tanh(inner * (ALPHA + inner * inner))

    def scores(u, t, away):
        start = pl.multiple_of(t * TILE, TILE)
        first_row = pl.multiple_of(u * rows_u, rows_u)
        products = jnp.dot(
            qm_ref[pl.ds(first_row, rows_u), :],
            kt_ref[:, pl.ds(start, TILE)],
            preferred_element_type=F32,
        )
        for g in range(groups):
            base = pl.multiple_of(u * UNIT + g * GROUP, GROUP)
            bias = jnp.dot(wsecond[...], turned[g], preferred_element_type=F32) + jnp.dot(
                wline[...], aged[g], preferred_element_type=F32
            )
            s = products[g * rows_g : (g + 1) * rows_g] + bias
            own = q_terms[7, pl.ds(base, GROUP), :] + away
            live = jnp.concatenate(
                [own == terms[7, pl.ds(t * per_tile + i, 1), :] for i in range(per_tile)], axis=1
            )
            s = jnp.where(live[None], s.reshape(heads, GROUP, TILE), -1e30).reshape(rows_g, TILE)
            at = pl.ds(pl.multiple_of(first_row + g * rows_g, rows_g), rows_g)
            s_ref[at, pl.ds(start, TILE)] = s
            run_max = top_ref[at, :]
            for i in range(0, TILE, 128):
                run_max = jnp.maximum(run_max, s[:, i : i + 128])
            top_ref[at, :] = run_max

    def score_step(i, carry):
        u0, t0, u1, t1, u2, t2 = carry
        scores(u2, t2, jnp.where(i >= 2, 0.0, 100.0))
        gelus()
        features(u0, t0)
        return (*following(u0, t0), u0, t0, u1, t1)

    zero = jnp.int32(0)
    t_first = limits[0, 0]
    _, _, u1, t1, u2, t2 = lax.fori_loop(
        0, steps, score_step, (zero, t_first, zero, t_first, zero, t_first)
    )
    scores(u2, t2, jnp.where(steps >= 2, 0.0, 100.0))
    gelus()
    scores(u1, t1, 0.0)

    for u in range(n_units):
        at = slice(u * rows_u, (u + 1) * rows_u)
        top_ref[at, :] = jnp.broadcast_to(
            jnp.max(top_ref[at, :], axis=1, keepdims=True), (rows_u, 128)
        )

    weight_ref[...] = jnp.zeros_like(weight_ref)

    def apply(u, t):
        at = pl.ds(pl.multiple_of(u * rows_u, rows_u), rows_u)
        acc_ref[at, :] += jnp.dot(
            weight_ref[...],
            v_ref[pl.ds(pl.multiple_of(t * TILE, TILE), TILE), :],
            preferred_element_type=F32,
        )

    def weigh(u, t):
        at = pl.ds(pl.multiple_of(u * rows_u, rows_u), rows_u)
        top = top_ref[at, :]
        total = total_ref[at, :]
        for i in range(0, TILE, 128):
            cols = pl.ds(pl.multiple_of(t * TILE + i, 128), 128)
            weight = jnp.exp2((s_ref[at, cols] - top) * (LOG2E / root))
            total = total + weight
            weight_ref[:, i : i + 128] = weight.astype(BF16)
        total_ref[at, :] = total

    def value_step(i, carry):
        u0, t0, u1, t1 = carry
        apply(u1, t1)
        weigh(u0, t0)
        return (*following(u0, t0), u0, t0)

    _, _, u1, t1 = lax.fori_loop(0, steps, value_step, (zero, t_first, zero, t_first))
    apply(u1, t1)

    for base in range(0, own_rows, GROUP):
        at = base * heads
        total = 1.0 / jnp.sum(total_ref[at : at + rows_g, :], axis=1, keepdims=True)
        out = jnp.zeros((GROUP, width), F32)
        for h in range(heads):
            rows = slice(at + h * GROUP, at + (h + 1) * GROUP)
            scaled = acc_ref[rows, :] * total[h * GROUP : (h + 1) * GROUP]
            out = jnp.where(lane_head == h, scaled, out)
        att_ref[base : base + GROUP, :] = out

    mixed = jnp.dot(att_ref[...].astype(BF16), wo_ref[...], preferred_element_type=F32)
    out_ref[...] = layer_norm(mixed, gain_ref[...]).astype(BF16)


def shards(
    n_grp,
    n_blk,
    raw,
    raw_kin,
    reader,
    event_id,
    pre_gain,
    w_query,
    w_key,
    w_value,
    w_out,
    post_gain,
    pair_w1,
    pair_b1,
    pair_w2,
):
    slots, width = raw.shape[2], raw.shape[3]
    heads = pair_w2.shape[1]
    vmem = pl.BlockSpec(memory_space=pltpu.VMEM)
    gathered = pl.pallas_call(
        functools.partial(exchange_kernel, n_grp, n_blk),
        out_shape=jax.ShapeDtypeStruct((n_blk, slots + KIN_ROWS, width), BF16),
        in_specs=[vmem] * 5,
        out_specs=pl.BlockSpec(memory_space=pl.ANY),
        scratch_shapes=[
            pltpu.VMEM((n_grp, slots, width), BF16),
            pltpu.VMEM((n_grp, 8, slots), F32),
            pltpu.VMEM((n_grp, 8, slots), F32),
            pltpu.VMEM((slots + KIN_ROWS, width), BF16),
            pltpu.SemaphoreType.DMA((n_grp,)),
            pltpu.SemaphoreType.DMA((n_grp,)),
            pltpu.SemaphoreType.DMA((n_grp,)),
            pltpu.SemaphoreType.DMA((n_grp,)),
            pltpu.SemaphoreType.DMA,
            pltpu.SemaphoreType.DMA,
            pltpu.SemaphoreType.DMA,
        ],
        compiler_params=pltpu.CompilerParams(collective_id=0, has_side_effects=True),
        name="exchange",
    )(raw, raw_kin, reader, event_id, pre_gain[None])

    keys = n_blk * slots
    feats, hid = pair_w1.shape
    groups = UNIT // GROUP
    rows_all = heads * slots
    mixing = (3 * feats + 2) * GROUP
    encoded = pl.pallas_call(
        functools.partial(attend_kernel, heads),
        out_shape=jax.ShapeDtypeStruct((slots, width), BF16),
        in_specs=[vmem] * 9,
        out_specs=vmem,
        scratch_shapes=[
            pltpu.VMEM((width, keys), BF16),
            pltpu.VMEM((keys, width), BF16),
            pltpu.VMEM((8, n_blk, slots), F32),
            pltpu.VMEM((8, slots, slots), F32),
            pltpu.VMEM((rows_all, width), BF16),
            pltpu.VMEM((rows_all, keys), F32),
            pltpu.VMEM((rows_all, 128), F32),
            pltpu.VMEM((rows_all, 128), F32),
            pltpu.VMEM((rows_all, width), F32),
            pltpu.VMEM((slots, width), F32),
            pltpu.VMEM((hid * GROUP, mixing), BF16),
            pltpu.VMEM((heads * GROUP, mixing), BF16),
            pltpu.VMEM((heads * GROUP, hid * GROUP), BF16),
            pltpu.VMEM((groups, mixing, TILE), BF16),
            pltpu.VMEM((groups, mixing, TILE), BF16),
            pltpu.VMEM((groups, hid * GROUP, TILE), BF16),
            pltpu.VMEM((heads * UNIT, TILE), BF16),
            pltpu.SMEM((2, slots // UNIT), jnp.int32),
        ],
        compiler_params=pltpu.CompilerParams(vmem_limit_bytes=40 * 1024 * 1024),
        name="attend",
    )(
        gathered,
        w_query,
        w_key,
        w_value,
        w_out,
        post_gain[None],
        pair_w1,
        pair_b1[None],
        pair_w2,
    )
    return encoded[None]


def solution(mesh):
    in_specs = (
        P("grp", None, "blk", None),
        P("grp", None, None, "blk"),
        P("grp", "blk"),
        P("grp", "blk"),
        P(),
        P(),
        P(),
        P(),
        P(),
        P(),
        P(),
        P(),
        P(),
    )
    out_specs = P("grp", "blk", None)
    body = functools.partial(shards, mesh.shape["grp"], mesh.shape["blk"])
    return jax.shard_map(body, mesh=mesh, in_specs=in_specs, out_specs=out_specs, check_vma=False)
```

```python
import functools
import math

import jax
import jax.numpy as jnp
from jax import lax
from jax.experimental import pallas as pl
from jax.experimental.pallas import tpu as pltpu
from jax.sharding import PartitionSpec as P

MESH = pl.DeviceIdType.MESH
F32 = jnp.float32
BF16 = jnp.bfloat16
HIGHEST = lax.Precision.HIGHEST

KIN_ROWS = 16
GROUP = 8
UNIT = 16
TILE = 256
STRIDE = 3

GELU_A = math.sqrt(2.0 / math.pi)
GELU_B = GELU_A * 0.044715
GELU_S = GELU_B ** (-1.0 / 3.0)
ALPHA = GELU_A * GELU_S
LOG2E = 1.0 / math.log(2.0)


def layer_norm(rows, gain):
    center = rows - jnp.mean(rows, axis=-1, keepdims=True)
    spread = jnp.mean(center * center, axis=-1, keepdims=True)
    return center * lax.rsqrt(spread + 1e-05) * gain


def mesh_place(cube):
    _, ny, nx = cube
    b = lax.axis_index("blk")
    return b // (ny * nx), lax.rem(b // nx, ny), lax.rem(b, nx)


def exchange_kernel(
    n_grp,
    cube,
    raw_ref,
    kin_ref,
    reader_ref,
    event_ref,
    gain_ref,
    pair_ref,
    keys_ref,
    inbox,
    kin_send,
    kin_in,
    block,
    other,
    payload,
    send_sem,
    recv_sem,
    kin_send_sem,
    kin_recv_sem,
    link_send,
    link_recv,
    own_sem,
):
    nz, ny, nx = cube
    g = lax.axis_index("grp")
    z, y, x = mesh_place(cube)
    slots = raw_ref.shape[2]
    width = raw_ref.shape[3]
    half = slots // nz

    def blk(z, y, x):
        return {"blk": (z * ny + y) * nx + x}

    partners = [{"grp": lax.rem(g + k, n_grp)} for k in range(1, n_grp)]
    partners.append(blk(1 - z, y, x))
    partners += [blk(z, lax.rem(y + k, ny), x) for k in range(1, ny)]
    partners += [blk(z, y, lax.rem(x + k, nx)) for k in range(1, nx)]
    barrier = pltpu.get_barrier_semaphore()
    for partner in partners:
        pl.semaphore_signal(barrier, inc=1, device_id=partner, device_id_type=MESH)
    kin_send[...] = jnp.zeros_like(kin_send)
    for k in range(n_grp):
        kin_send[k, 0:4, :] = kin_ref[0, k].astype(F32)
    pl.semaphore_wait(barrier, len(partners))

    copies = []
    for k in range(1, n_grp):
        to = lax.rem(g + k, n_grp)
        for src, dst, ssem, rsem in (
            (raw_ref.at[0, to], inbox.at[n_grp - k], send_sem, recv_sem),
            (kin_send.at[to], kin_in.at[n_grp - k], kin_send_sem, kin_recv_sem),
        ):
            copy = pltpu.make_async_remote_copy(
                src_ref=src,
                dst_ref=dst,
                send_sem=ssem.at[k],
                recv_sem=rsem.at[n_grp - k],
                device_id={"grp": to},
                device_id_type=MESH,
            )
            copy.start()
            copies.append(copy)

    wanted = lax.rem(reader_ref[...] - g + n_grp, n_grp)
    column = jnp.broadcast_to(wanted, (slots, slots)).T
    kin = jnp.where(wanted == 0, kin_send[g, 0:4, :], 0.0)
    sides = [
        jnp.where(column == 0, raw_ref[0, g][:, h : h + slots].astype(F32), 0.0)
        for h in range(0, width, slots)
    ]
    for copy in copies:
        copy.wait()
    for k in range(1, n_grp):
        kin = kin + jnp.where(wanted == k, kin_in[k, 0:4, :], 0.0)
        sides = [
            side
            + jnp.where(column == k, inbox[k][:, i * slots : (i + 1) * slots].astype(F32), 0.0)
            for i, side in enumerate(sides)
        ]
    tokens = jnp.concatenate(sides, axis=1)
    block[0:slots, :] = layer_norm(tokens, gain_ref[...]).astype(BF16)
    tail = jnp.concatenate(
        [kin, event_ref[...].astype(F32), jnp.zeros((8 - 5, slots), F32)], axis=0
    )
    tail = jnp.concatenate([tail, tail], axis=0)
    block[slots : slots + KIN_ROWS, :] = jnp.concatenate([tail, tail], axis=1).astype(BF16)

    def push(slot, src, dst, to):
        copy = pltpu.make_async_remote_copy(
            src_ref=src,
            dst_ref=dst,
            send_sem=link_send.at[slot],
            recv_sem=link_recv.at[slot],
            device_id=to,
            device_id_type=MESH,
        )
        copy.start()
        return copy

    mine = pl.ds(pl.multiple_of(z * half, half), half)
    theirs = pl.ds(pl.multiple_of((1 - z) * half, half), half)
    ends = pl.ds(slots, KIN_ROWS)
    near = blk(1 - z, y, x)
    first = [
        push(0, block.at[theirs], other.at[theirs], near),
        push(1, block.at[ends], other.at[ends], near),
    ]
    rest = push(2, block.at[mine], other.at[mine], near)
    for copy in first:
        copy.wait()

    mine_own = block[mine, :]
    mine_other = other[mine, :]
    payload[0:half, :] = jnp.where(z == 0, mine_own, mine_other)
    payload[half : 2 * half, :] = jnp.where(z == 0, mine_other, mine_own)
    ends_own = block[ends, :].astype(F32)
    ends_other = other[ends, :].astype(F32)
    part = lax.broadcasted_iota(jnp.int32, (KIN_ROWS, width), 0) // 8
    lane = lax.broadcasted_iota(jnp.int32, (KIN_ROWS, width), 1) // half
    both = jnp.where(part == z, ends_own, ends_other)
    swapped = jnp.concatenate([both[:, half:], both[:, :half]], axis=1)
    both = jnp.where(lax.rem(lane, 2) == z, both, swapped)
    payload[slots : slots + KIN_ROWS, :] = jnp.where(lane == x, both, 0.0).astype(BF16)

    own = pltpu.make_async_copy(payload, keys_ref.at[y, x], own_sem.at[0])
    own.start()
    rows = (pl.ds(0, half), pl.ds(half, half + KIN_ROWS))
    along = []
    for i, k in enumerate((1, 3, 2)):
        along.append(
            push(
                3 + i,
                payload.at[rows[0]],
                keys_ref.at[y, x, rows[0]],
                blk(z, y, lax.rem(x + k, nx)),
            )
        )
        along.append(
            push(
                6 + i,
                payload.at[rows[1]],
                keys_ref.at[y, x, rows[1]],
                blk(z, lax.rem(y + k, ny), x),
            )
        )
    own.wait()
    for copy in along:
        copy.wait()
    line_x = keys_ref.at[y, :, rows[0]]
    line_y = keys_ref.at[:, x, rows[1]]
    last = []
    for i, k in enumerate((1, 3, 2)):
        last.append(push(9 + i, line_x, line_x, blk(z, lax.rem(y + k, ny), x)))
        last.append(push(12 + i, line_y, line_y, blk(z, y, lax.rem(x + k, nx))))
    rest.wait()
    pair = [
        pltpu.make_async_copy(block, pair_ref.at[z], own_sem.at[1]),
        pltpu.make_async_copy(other, pair_ref.at[1 - z], own_sem.at[2]),
    ]
    for copy in pair:
        copy.start()
    for copy in pair + last:
        copy.wait()


def split_two(value):
    high = value.astype(BF16)
    low = (value - high.astype(F32)).astype(BF16)
    return high, low


def spread_over(weight):
    m, c = weight.shape
    up = (
        lax.broadcasted_iota(jnp.int32, (m * GROUP, m), 0) // GROUP
        == lax.broadcasted_iota(jnp.int32, (m * GROUP, m), 1)
    ).astype(F32)
    across = (
        lax.broadcasted_iota(jnp.int32, (c, c * GROUP), 1) // GROUP
        == lax.broadcasted_iota(jnp.int32, (c, c * GROUP), 0)
    ).astype(F32)
    tall = jnp.dot(up, weight, precision=HIGHEST, preferred_element_type=F32)
    wide = jnp.dot(tall, across, precision=HIGHEST, preferred_element_type=F32)
    same = (
        lax.broadcasted_iota(jnp.int32, (m * GROUP, c * GROUP), 0) % GROUP
        == lax.broadcasted_iota(jnp.int32, (m * GROUP, c * GROUP), 1) % GROUP
    )
    return jnp.where(same, wide, 0.0)


def attend_kernel(
    heads,
    pair_hbm,
    keys_hbm,
    wq_ref,
    wk_ref,
    wv_ref,
    w1_ref,
    b1_ref,
    w2_ref,
    out_ref,
    level_ref,
    pair_ref,
    keys_ref,
    load_sem,
    kt_ref,
    v_ref,
    terms,
    q_terms,
    qm_ref,
    s_ref,
    top_ref,
    total_ref,
    acc_ref,
    wfirst,
    wsecond,
    fresh,
    hidden,
    linear,
    turned,
    weight_ref,
    held_ref,
    limits,
):
    loads = [
        pltpu.make_async_copy(pair_hbm, pair_ref, load_sem.at[0]),
        pltpu.make_async_copy(keys_hbm, keys_ref, load_sem.at[1]),
    ]
    for load in loads:
        load.start()
    nz, slots, width = out_ref.shape
    ny, nx = keys_ref.shape[0:2]
    half = slots // nz
    own_rows = nz * slots
    head_size = width // heads
    feats, hid = w1_ref.shape
    root = math.sqrt(head_size)
    groups = UNIT // GROUP
    rows_g = heads * GROUP
    rows_u = groups * rows_g
    n_units = own_rows // UNIT
    n_tiles = nz * ny

    w1 = w1_ref[...]
    b1 = b1_ref[...]
    w2 = w2_ref[...]
    first = jnp.concatenate([w1, b1, jnp.zeros((8 - feats - 1, hid), F32)], axis=0)
    line = jnp.dot(first, w2, precision=HIGHEST, preferred_element_type=F32) * (0.5 * root)
    part = feats * GROUP

    stacked = jnp.concatenate([first.T * (1.0 / GELU_S), line.T], axis=0)
    high, low = split_two(spread_over(stacked))
    wfirst[:, 0:part] = high[:, 0:part]
    wfirst[:, part : 2 * part] = high[:, 0:part]
    wfirst[:, 2 * part : 3 * part] = low[:, 0:part]
    wfirst[:, 3 * part : 3 * part + GROUP] = high[:, part : part + GROUP]
    wfirst[:, 3 * part + GROUP : 3 * part + 2 * GROUP] = low[:, part : part + GROUP]
    wsecond[...] = spread_over(w2.T * (0.5 * root * GELU_S)).astype(BF16)

    for load in loads:
        load.wait()

    def terms_of(mom, rap, azi, mass, ids):
        trans = jnp.sqrt(mom * mom + mass * mass)
        return (
            mom,
            rap,
            jnp.cos(azi),
            jnp.sin(azi),
            trans * jnp.exp(rap),
            trans * jnp.exp(-rap),
            mass * mass,
            ids,
        )

    ends = []
    for yy in range(ny):
        end = keys_ref[yy, 0, slots : slots + KIN_ROWS, :].astype(F32)
        for xx in range(1, nx):
            end = end + keys_ref[yy, xx, slots : slots + KIN_ROWS, :].astype(F32)
        ends.append(end)
    raw_terms = [
        jnp.concatenate(
            [ends[yy][zz * 8 + i : zz * 8 + i + 1] for zz in range(nz) for yy in range(ny)], axis=0
        )
        for i in range(5)
    ]
    ids = raw_terms[4]
    for i, term in enumerate(terms_of(*raw_terms)):
        for k in range(TILE // 128):
            terms[i, k] = term[:, k * 128 : (k + 1) * 128]
    ends = [pair_ref[zz, slots : slots + KIN_ROWS, 0:slots].astype(F32) for zz in range(nz)]
    raw_terms = [
        jnp.concatenate([ends[zz][i : i + 1] for zz in range(nz)], axis=0) for i in range(5)
    ]
    for i, term in enumerate(terms_of(*raw_terms)):
        for zz in range(nz):
            q_terms[i, zz * slots : (zz + 1) * slots, :] = jnp.broadcast_to(
                term[zz : zz + 1], (slots, slots)
            ).T

    for u in range(n_units):
        begin = q_terms[7, u * UNIT : u * UNIT + 1, 0:1]
        finish = q_terms[7, u * UNIT + UNIT - 1 : u * UNIT + UNIT, 0:1]
        start = jnp.minimum(jnp.sum((ids < begin).astype(jnp.int32)) // TILE, n_tiles - 1)
        limits[0, u] = start
        limits[1, u] = jnp.maximum(
            (jnp.sum((ids <= finish).astype(jnp.int32)) + TILE - 1) // TILE, start + 1
        )

    wkt = wk_ref[...].astype(F32).T.astype(BF16)
    for yy in range(ny):
        for zz in range(nz):
            rows = jnp.concatenate(
                [keys_ref[yy, xx, zz * half : (zz + 1) * half, :] for xx in range(nx)], axis=0
            )
            at = slice((zz * ny + yy) * TILE, (zz * ny + yy + 1) * TILE)
            kt_ref[:, at] = lax.dot_general(
                wkt, rows, (((1,), (1,)), ((), ())), preferred_element_type=F32
            ).astype(BF16)
            v_ref[at, :] = jnp.dot(rows, wv_ref[...], preferred_element_type=F32).astype(BF16)
    for k in range(STRIDE - 1):
        v_ref[(n_tiles + k) * TILE : (n_tiles + k + 1) * TILE, :] = jnp.zeros((TILE, width), BF16)

    lane_head = lax.broadcasted_iota(jnp.int32, (GROUP, width), 1) // head_size
    for zz in range(nz):
        queries = jnp.dot(pair_ref[zz, 0:slots, :], wq_ref[...], preferred_element_type=F32)
        for base in range(0, slots, GROUP):
            rows = queries[base : base + GROUP]
            at = (zz * slots + base) * heads
            qm_ref[at : at + rows_g, :] = jnp.concatenate(
                [jnp.where(lane_head == h, rows, 0.0) for h in range(heads)], axis=0
            ).astype(BF16)

    top_ref[...] = jnp.full_like(top_ref, -1e30)
    total_ref[...] = jnp.zeros_like(total_ref)
    acc_ref[...] = jnp.zeros_like(acc_ref)

    def following(u, t):
        more = t + 1 < limits[1, u]
        then = jnp.where(more, u, jnp.minimum(u + 1, n_units - 1))
        return then, jnp.where(more, t + 1, limits[0, then])

    steps = limits[1, 0] - limits[0, 0]
    for u in range(1, n_units):
        steps = steps + limits[1, u] - limits[0, u]

    def features(p, u, t):
        for g in range(groups):
            base = pl.multiple_of(u * UNIT + g * GROUP, GROUP)
            qt = [q_terms[i, pl.ds(base, GROUP), :] for i in range(7)]
            columns = []
            for i in range(TILE // 128):
                kt = [terms[j, i, pl.ds(t, 1), :] for j in range(7)]
                gap = qt[1] - kt[1]
                cos_gap = qt[2] * kt[2] + qt[3] * kt[3]
                dist = gap * gap + (2.0 - 2.0 * cos_gap)
                small = jnp.minimum(qt[0], kt[0])
                msq = (
                    qt[6]
                    + kt[6]
                    + (qt[4] * kt[5] + qt[5] * kt[4] - 2.0 * (qt[0] * kt[0] * cos_gap))
                )
                f = [
                    jnp.log(1.0 + dist),
                    jnp.log(1.0 + small * small * dist),
                    small / (qt[0] + kt[0]),
                    jnp.log(1.0 + msq),
                ]
                fh, fl = split_two(jnp.concatenate(f, axis=0))
                columns.append(
                    jnp.concatenate([fh, fl, fh, jnp.ones((2 * GROUP, 128), BF16)], axis=0)
                )
            fresh[p, g] = jnp.concatenate(columns, axis=1)

    def hiddens(p):
        for g in range(groups):
            z = jnp.dot(wfirst[...], fresh[p, g], preferred_element_type=F32)
            hidden[p, g] = z[0 : hid * GROUP].astype(BF16)
            linear[p, g] = z[hid * GROUP :]

    def gelus(p):
        for g in range(groups):
            inner = hidden[p, g]
            turned[p, g] = inner * jnp.tanh(inner * (ALPHA + inner * inner))

    def scores(p, u, t, away):
        start = pl.multiple_of(t * TILE, TILE)
        first_row = pl.multiple_of(u * rows_u, rows_u)
        products = jnp.dot(
            qm_ref[pl.ds(first_row, rows_u), :],
            kt_ref[:, pl.ds(start, TILE)],
            preferred_element_type=F32,
        )
        for g in range(groups):
            base = pl.multiple_of(u * UNIT + g * GROUP, GROUP)
            bias = jnp.dot(wsecond[...], turned[p, g], preferred_element_type=F32)
            s = products[g * rows_g : (g + 1) * rows_g] + (bias + linear[p, g])
            own = q_terms[7, pl.ds(base, GROUP), :] + away
            live = jnp.concatenate(
                [own == terms[7, i, pl.ds(t, 1), :] for i in range(TILE // 128)], axis=1
            )
            s = jnp.where(live[None], s.reshape(heads, GROUP, TILE), -1e30).reshape(rows_g, TILE)
            at = pl.ds(pl.multiple_of(first_row + g * rows_g, rows_g), rows_g)
            s_ref[at, pl.ds(start, TILE)] = s
            run_max = top_ref[at, :]
            for i in range(0, TILE, 128):
                run_max = jnp.maximum(run_max, s[:, i : i + 128])
            top_ref[at, :] = run_max

    def score_steps(i, carry):
        for p in range(2):
            u0, t0, u1, t1, u2, t2, u3, t3 = carry
            scores(1 - p, u3, t3, jnp.where(2 * i + p >= 3, 0.0, 100.0))
            hiddens(1 - p)
            gelus(p)
            features(p, u0, t0)
            carry = (*following(u0, t0), u0, t0, u1, t1, u2, t2)
        return carry

    zero = jnp.int32(0)
    t_first = limits[0, 0]
    lax.fori_loop(0, (steps + 4) // 2, score_steps, (zero, t_first) * 4)

    for u in range(n_units):
        at = slice(u * rows_u, (u + 1) * rows_u)
        top_ref[at, :] = jnp.broadcast_to(
            jnp.max(top_ref[at, :], axis=1, keepdims=True), (rows_u, 128)
        )

    for u in range(n_units):
        for k in range(STRIDE - 1):
            start = pl.multiple_of((limits[1, u] + k) * TILE, TILE)
            s_ref[u * rows_u : (u + 1) * rows_u, pl.ds(start, TILE)] = jnp.full(
                (rows_u, TILE), -1e30, F32
            )
    weight_ref[...] = jnp.zeros_like(weight_ref)
    span = STRIDE * TILE

    def stride_on(u, t):
        more = t + STRIDE < limits[1, u]
        then = jnp.where(more, u, jnp.minimum(u + 1, n_units - 1))
        return then, jnp.where(more, t + STRIDE, limits[0, then])

    def apply(u, t):
        at = pl.ds(pl.multiple_of(u * rows_u, rows_u), rows_u)
        acc_ref[at, :] += jnp.dot(
            weight_ref[...],
            v_ref[pl.ds(pl.multiple_of(t * TILE, TILE), span), :],
            preferred_element_type=F32,
        )

    def weigh(u, t):
        at = pl.ds(pl.multiple_of(u * rows_u, rows_u), rows_u)
        top = top_ref[at, :]
        total = total_ref[at, :]
        for i in range(0, span, 128):
            cols = pl.ds(pl.multiple_of(t * TILE + i, 128), 128)
            weight = jnp.exp2((s_ref[at, cols] - top) * (LOG2E / root))
            total = total + weight
            weight_ref[:, i : i + 128] = weight.astype(BF16)
        total_ref[at, :] = total

    def value_step(i, carry):
        u0, t0, u1, t1 = carry
        apply(u1, t1)
        weigh(u0, t0)
        return (*stride_on(u0, t0), u0, t0)

    strides = zero
    for u in range(n_units):
        strides = strides + (limits[1, u] - limits[0, u] + STRIDE - 1) // STRIDE
    _, _, u1, t1 = lax.fori_loop(0, strides, value_step, (zero, t_first, zero, t_first))
    apply(u1, t1)

    lane = lax.broadcasted_iota(jnp.int32, (rows_g, slots), 1)
    row = lax.rem(lax.broadcasted_iota(jnp.int32, (rows_g, slots), 0), GROUP)
    for zz in range(nz):
        level = jnp.zeros((rows_g, slots), F32)
        for base in range(0, slots, GROUP):
            at = (zz * slots + base) * heads
            total = jnp.sum(total_ref[at : at + rows_g, :], axis=1, keepdims=True)
            level = jnp.where(
                lane == base + row,
                top_ref[at : at + rows_g, :] * (LOG2E / root) + jnp.log(total) * LOG2E,
                level,
            )
            total = 1.0 / total
            out = jnp.zeros((GROUP, width), F32)
            for h in range(heads):
                rows = slice(at + h * GROUP, at + (h + 1) * GROUP)
                scaled = acc_ref[rows, :] * total[h * GROUP : (h + 1) * GROUP]
                out = jnp.where(lane_head == h, scaled, out)
            held_ref[base : base + GROUP, :] = out
        out_ref[zz] = held_ref[...].astype(BF16)
        level_ref[zz] = jnp.sum(level.reshape(heads, GROUP, slots), axis=1)


def finish_kernel(
    cube,
    part_ref,
    level_ref,
    wo_ref,
    gain_ref,
    out_ref,
    part_in,
    level_in,
    send_sem,
    recv_sem,
):
    _, ny, nx = cube
    z, y, x = mesh_place(cube)
    near = {"blk": ((1 - z) * ny + y) * nx + x}
    heads = level_ref.shape[1]
    width = part_ref.shape[2]
    barrier = pltpu.get_barrier_semaphore()
    pl.semaphore_signal(barrier, inc=1, device_id=near, device_id_type=MESH)
    pl.semaphore_wait(barrier, 1)
    copies = [
        pltpu.make_async_remote_copy(
            src_ref=src,
            dst_ref=dst,
            send_sem=send_sem.at[i],
            recv_sem=recv_sem.at[i],
            device_id=near,
            device_id_type=MESH,
        )
        for i, (src, dst) in enumerate(
            [(part_ref.at[1 - z], part_in), (level_ref.at[1 - z], level_in)]
        )
    ]
    for copy in copies:
        copy.start()
    spread = (
        lax.broadcasted_iota(jnp.int32, (heads, width), 1) // (width // heads)
        == lax.broadcasted_iota(jnp.int32, (heads, width), 0)
    ).astype(F32)
    for copy in copies:
        copy.wait()
    share = 1.0 / (1.0 + jnp.exp2(level_in[...] - level_ref[z]))
    share = jnp.dot(share.T, spread, precision=HIGHEST, preferred_element_type=F32)
    theirs = part_in[...].astype(F32)
    attended = theirs + share * (part_ref[z].astype(F32) - theirs)
    mixed = jnp.dot(attended.astype(BF16), wo_ref[...], preferred_element_type=F32)
    out_ref[...] = layer_norm(mixed, gain_ref[...]).astype(BF16)


def shards(
    n_grp,
    cube,
    raw,
    raw_kin,
    reader,
    event_id,
    pre_gain,
    w_query,
    w_key,
    w_value,
    w_out,
    post_gain,
    pair_w1,
    pair_b1,
    pair_w2,
):
    slots, width = raw.shape[2], raw.shape[3]
    heads = pair_w2.shape[1]
    nz, ny, nx = cube
    vmem = pl.BlockSpec(memory_space=pltpu.VMEM)
    free = pl.BlockSpec(memory_space=pl.ANY)
    dma = pltpu.SemaphoreType.DMA
    tall = slots + KIN_ROWS
    pair, keys = pl.pallas_call(
        functools.partial(exchange_kernel, n_grp, cube),
        out_shape=(
            jax.ShapeDtypeStruct((nz, tall, width), BF16),
            jax.ShapeDtypeStruct((ny, nx, tall, width), BF16),
        ),
        in_specs=[vmem] * 5,
        out_specs=(free, free),
        scratch_shapes=[
            pltpu.VMEM((n_grp, slots, width), BF16),
            pltpu.VMEM((n_grp, 8, slots), F32),
            pltpu.VMEM((n_grp, 8, slots), F32),
            pltpu.VMEM((tall, width), BF16),
            pltpu.VMEM((tall, width), BF16),
            pltpu.VMEM((tall, width), BF16),
            dma((n_grp,)),
            dma((n_grp,)),
            dma((n_grp,)),
            dma((n_grp,)),
            dma((15,)),
            dma((15,)),
            dma((3,)),
        ],
        compiler_params=pltpu.CompilerParams(collective_id=0, has_side_effects=True),
        name="exchange",
    )(raw, raw_kin, reader, event_id, pre_gain[None])

    own_rows = nz * slots
    n_tiles = nz * ny
    feats, hid = pair_w1.shape
    groups = UNIT // GROUP
    rows_all = heads * own_rows
    mixing = (3 * feats + 2) * GROUP
    part, level = pl.pallas_call(
        functools.partial(attend_kernel, heads),
        out_shape=(
            jax.ShapeDtypeStruct((nz, slots, width), BF16),
            jax.ShapeDtypeStruct((nz, heads, slots), F32),
        ),
        in_specs=[free, free] + [vmem] * 6,
        out_specs=(vmem, vmem),
        scratch_shapes=[
            pltpu.VMEM((nz, tall, width), BF16),
            pltpu.VMEM((ny, nx, tall, width), BF16),
            dma((2,)),
            pltpu.VMEM((width, n_tiles * TILE), BF16),
            pltpu.VMEM(((n_tiles + STRIDE - 1) * TILE, width), BF16),
            pltpu.VMEM((8, TILE // 128, n_tiles, 128), F32),
            pltpu.VMEM((8, own_rows, slots), F32),
            pltpu.VMEM((rows_all, width), BF16),
            pltpu.VMEM((rows_all, (n_tiles + STRIDE - 1) * TILE), F32),
            pltpu.VMEM((rows_all, 128), F32),
            pltpu.VMEM((rows_all, 128), F32),
            pltpu.VMEM((rows_all, width), F32),
            pltpu.VMEM(((hid + heads) * GROUP, mixing), BF16),
            pltpu.VMEM((heads * GROUP, hid * GROUP), BF16),
            pltpu.VMEM((2, groups, mixing, TILE), BF16),
            pltpu.VMEM((2, groups, hid * GROUP, TILE), BF16),
            pltpu.VMEM((2, groups, heads * GROUP, TILE), F32),
            pltpu.VMEM((2, groups, hid * GROUP, TILE), BF16),
            pltpu.VMEM((heads * UNIT, STRIDE * TILE), BF16),
            pltpu.VMEM((slots, width), F32),
            pltpu.SMEM((2, own_rows // UNIT), jnp.int32),
        ],
        compiler_params=pltpu.CompilerParams(vmem_limit_bytes=52 * 1024 * 1024),
        name="attend",
    )(pair, keys, w_query, w_key, w_value, pair_w1, pair_b1[None], pair_w2)

    encoded = pl.pallas_call(
        functools.partial(finish_kernel, cube),
        out_shape=jax.ShapeDtypeStruct((slots, width), BF16),
        in_specs=[vmem] * 4,
        out_specs=vmem,
        scratch_shapes=[
            pltpu.VMEM((slots, width), BF16),
            pltpu.VMEM((heads, slots), F32),
            dma((2,)),
            dma((2,)),
        ],
        compiler_params=pltpu.CompilerParams(collective_id=1, has_side_effects=True),
        name="finish",
    )(part, level, w_out, post_gain[None])
    return encoded[None]


def solution(mesh):
    in_specs = (
        P("grp", None, "blk", None),
        P("grp", None, None, "blk"),
        P("grp", "blk"),
        P("grp", "blk"),
        P(),
        P(),
        P(),
        P(),
        P(),
        P(),
        P(),
        P(),
        P(),
    )
    out_specs = P("grp", "blk", None)
    cube = (2, 4, mesh.shape["blk"] // 8)
    body = functools.partial(shards, mesh.shape["grp"], cube)
    return jax.shard_map(body, mesh=mesh, in_specs=in_specs, out_specs=out_specs, check_vma=False)
```

```python
import functools
import math

import jax
import jax.numpy as jnp
from jax import lax
from jax.experimental import pallas as pl
from jax.experimental.pallas import tpu as pltpu
from jax.sharding import PartitionSpec as P

MESH = pl.DeviceIdType.MESH
F32 = jnp.float32
BF16 = jnp.bfloat16
HIGHEST = lax.Precision.HIGHEST

KIN_ROWS = 16
GROUP = 8
UNIT = 16
TILE = 256
STRIDE = 3

GELU_A = math.sqrt(2.0 / math.pi)
GELU_B = GELU_A * 0.044715
GELU_S = GELU_B ** (-1.0 / 3.0)
ALPHA = GELU_A * GELU_S
LOG2E = 1.0 / math.log(2.0)


def layer_norm(rows, gain):
    center = rows - jnp.mean(rows, axis=-1, keepdims=True)
    spread = jnp.mean(center * center, axis=-1, keepdims=True)
    return center * lax.rsqrt(spread + 1e-05) * gain


def mesh_place(cube):
    _, ny, nx = cube
    b = lax.axis_index("blk")
    return b // (ny * nx), lax.rem(b // nx, ny), lax.rem(b, nx)


def exchange_kernel(
    n_grp,
    cube,
    raw_ref,
    kin_ref,
    reader_ref,
    event_ref,
    gain_ref,
    pair_ref,
    keys_ref,
    inbox,
    kin_send,
    kin_in,
    block,
    other,
    payload,
    send_sem,
    recv_sem,
    kin_send_sem,
    kin_recv_sem,
    link_send,
    link_recv,
    own_sem,
):
    nz, ny, nx = cube
    g = lax.axis_index("grp")
    z, y, x = mesh_place(cube)
    slots = raw_ref.shape[2]
    width = raw_ref.shape[3]
    half = slots // nz

    def blk(z, y, x):
        return {"blk": (z * ny + y) * nx + x}

    partners = [{"grp": lax.rem(g + k, n_grp)} for k in range(1, n_grp)]
    partners.append(blk(1 - z, y, x))
    partners += [blk(z, lax.rem(y + k, ny), x) for k in range(1, ny)]
    partners += [blk(z, y, lax.rem(x + k, nx)) for k in range(1, nx)]
    barrier = pltpu.get_barrier_semaphore()
    for partner in partners:
        pl.semaphore_signal(barrier, inc=1, device_id=partner, device_id_type=MESH)
    kin_send[...] = jnp.zeros_like(kin_send)
    for k in range(n_grp):
        kin_send[k, 0:4, :] = kin_ref[0, k].astype(F32)
    pl.semaphore_wait(barrier, len(partners))

    copies = []
    for k in range(1, n_grp):
        to = lax.rem(g + k, n_grp)
        for src, dst, ssem, rsem in (
            (raw_ref.at[0, to], inbox.at[n_grp - k], send_sem, recv_sem),
            (kin_send.at[to], kin_in.at[n_grp - k], kin_send_sem, kin_recv_sem),
        ):
            copy = pltpu.make_async_remote_copy(
                src_ref=src,
                dst_ref=dst,
                send_sem=ssem.at[k],
                recv_sem=rsem.at[n_grp - k],
                device_id={"grp": to},
                device_id_type=MESH,
            )
            copy.start()
            copies.append(copy)

    wanted = lax.rem(reader_ref[...] - g + n_grp, n_grp)
    column = jnp.broadcast_to(wanted, (slots, slots)).T
    kin = jnp.where(wanted == 0, kin_send[g, 0:4, :], 0.0)
    sides = [
        jnp.where(column == 0, raw_ref[0, g][:, h : h + slots].astype(F32), 0.0)
        for h in range(0, width, slots)
    ]
    for copy in copies:
        copy.wait()
    for k in range(1, n_grp):
        kin = kin + jnp.where(wanted == k, kin_in[k, 0:4, :], 0.0)
        sides = [
            side
            + jnp.where(column == k, inbox[k][:, i * slots : (i + 1) * slots].astype(F32), 0.0)
            for i, side in enumerate(sides)
        ]
    tokens = jnp.concatenate(sides, axis=1)
    block[0:slots, :] = layer_norm(tokens, gain_ref[...]).astype(BF16)
    tail = jnp.concatenate(
        [kin, event_ref[...].astype(F32), jnp.zeros((8 - 5, slots), F32)], axis=0
    )
    tail = jnp.concatenate([tail, tail], axis=0)
    block[slots : slots + KIN_ROWS, :] = jnp.concatenate([tail, tail], axis=1).astype(BF16)

    def push(slot, src, dst, to):
        copy = pltpu.make_async_remote_copy(
            src_ref=src,
            dst_ref=dst,
            send_sem=link_send.at[slot],
            recv_sem=link_recv.at[slot],
            device_id=to,
            device_id_type=MESH,
        )
        copy.start()
        return copy

    mine = pl.ds(pl.multiple_of(z * half, half), half)
    theirs = pl.ds(pl.multiple_of((1 - z) * half, half), half)
    ends = pl.ds(slots, KIN_ROWS)
    near = blk(1 - z, y, x)
    first = [
        push(0, block.at[theirs], other.at[theirs], near),
        push(1, block.at[ends], other.at[ends], near),
    ]
    rest = push(2, block.at[mine], other.at[mine], near)
    for copy in first:
        copy.wait()

    mine_own = block[mine, :]
    mine_other = other[mine, :]
    payload[0:half, :] = jnp.where(z == 0, mine_own, mine_other)
    payload[half : 2 * half, :] = jnp.where(z == 0, mine_other, mine_own)
    ends_own = block[ends, :].astype(F32)
    ends_other = other[ends, :].astype(F32)
    part = lax.broadcasted_iota(jnp.int32, (KIN_ROWS, width), 0) // 8
    lane = lax.broadcasted_iota(jnp.int32, (KIN_ROWS, width), 1) // half
    both = jnp.where(part == z, ends_own, ends_other)
    swapped = jnp.concatenate([both[:, half:], both[:, :half]], axis=1)
    both = jnp.where(lax.rem(lane, 2) == z, both, swapped)
    payload[slots : slots + KIN_ROWS, :] = jnp.where(lane == x, both, 0.0).astype(BF16)

    own = pltpu.make_async_copy(payload, keys_ref.at[y, x], own_sem.at[0])
    own.start()
    rows = (pl.ds(0, half), pl.ds(half, half + KIN_ROWS))
    along = []
    for i, k in enumerate((1, 3, 2)):
        along.append(
            push(
                3 + i,
                payload.at[rows[0]],
                keys_ref.at[y, x, rows[0]],
                blk(z, y, lax.rem(x + k, nx)),
            )
        )
        along.append(
            push(
                6 + i,
                payload.at[rows[1]],
                keys_ref.at[y, x, rows[1]],
                blk(z, lax.rem(y + k, ny), x),
            )
        )
    own.wait()
    for copy in along:
        copy.wait()
    line_x = keys_ref.at[y, :, rows[0]]
    line_y = keys_ref.at[:, x, rows[1]]
    last = []
    for i, k in enumerate((1, 3, 2)):
        last.append(push(9 + i, line_x, line_x, blk(z, lax.rem(y + k, ny), x)))
        last.append(push(12 + i, line_y, line_y, blk(z, y, lax.rem(x + k, nx))))
    rest.wait()
    pair = [
        pltpu.make_async_copy(block, pair_ref.at[z], own_sem.at[1]),
        pltpu.make_async_copy(other, pair_ref.at[1 - z], own_sem.at[2]),
    ]
    for copy in pair:
        copy.start()
    for copy in pair + last:
        copy.wait()


def split_two(value):
    high = value.astype(BF16)
    low = (value - high.astype(F32)).astype(BF16)
    return high, low


def spread_over(weight):
    m, c = weight.shape
    up = (
        lax.broadcasted_iota(jnp.int32, (m * GROUP, m), 0) // GROUP
        == lax.broadcasted_iota(jnp.int32, (m * GROUP, m), 1)
    ).astype(F32)
    across = (
        lax.broadcasted_iota(jnp.int32, (c, c * GROUP), 1) // GROUP
        == lax.broadcasted_iota(jnp.int32, (c, c * GROUP), 0)
    ).astype(F32)
    tall = jnp.dot(up, weight, precision=HIGHEST, preferred_element_type=F32)
    wide = jnp.dot(tall, across, precision=HIGHEST, preferred_element_type=F32)
    same = (
        lax.broadcasted_iota(jnp.int32, (m * GROUP, c * GROUP), 0) % GROUP
        == lax.broadcasted_iota(jnp.int32, (m * GROUP, c * GROUP), 1) % GROUP
    )
    return jnp.where(same, wide, 0.0)


def attend_kernel(
    heads,
    pair_hbm,
    keys_hbm,
    wq_ref,
    wk_ref,
    wv_ref,
    w1_ref,
    b1_ref,
    w2t_ref,
    out_ref,
    level_ref,
    pair_ref,
    keys_ref,
    load_sem,
    kt_ref,
    v_ref,
    terms,
    q_terms,
    qm_ref,
    s_ref,
    top_ref,
    total_ref,
    acc_ref,
    wfirst,
    wsecond,
    fresh,
    hidden,
    linear,
    turned,
    weight_ref,
    held_ref,
    ranges,
    limits,
):
    loads = [
        pltpu.make_async_copy(pair_hbm, pair_ref, load_sem.at[0]),
        pltpu.make_async_copy(keys_hbm, keys_ref, load_sem.at[1]),
    ]
    for load in loads:
        load.start()
    nz, slots, width = out_ref.shape
    ny, nx = keys_ref.shape[0:2]
    half = slots // nz
    own_rows = nz * slots
    head_size = width // heads
    feats, hid = w1_ref.shape
    root = math.sqrt(head_size)
    groups = UNIT // GROUP
    rows_g = heads * GROUP
    rows_u = groups * rows_g
    n_units = own_rows // UNIT
    n_tiles = nz * ny

    w1 = w1_ref[...]
    b1 = b1_ref[...]
    w2t = w2t_ref[...]
    first = jnp.concatenate([w1, b1, jnp.zeros((8 - feats - 1, hid), F32)], axis=0)
    line = lax.dot_general(
        w2t, first, (((1,), (1,)), ((), ())), precision=HIGHEST, preferred_element_type=F32
    ) * (0.5 * root)
    part = feats * GROUP

    stacked = jnp.concatenate([first.T * (1.0 / GELU_S), line], axis=0)
    high, low = split_two(spread_over(stacked))
    wfirst[:, 0:part] = high[:, 0:part]
    wfirst[:, part : 2 * part] = high[:, 0:part]
    wfirst[:, 2 * part : 3 * part] = low[:, 0:part]
    wfirst[:, 3 * part : 3 * part + GROUP] = high[:, part : part + GROUP]
    wfirst[:, 3 * part + GROUP : 3 * part + 2 * GROUP] = low[:, part : part + GROUP]
    wsecond[...] = spread_over(w2t * (0.5 * root * GELU_S)).astype(BF16)

    for load in loads:
        load.wait()

    def terms_of(mom, rap, azi, mass, ids):
        trans = jnp.sqrt(mom * mom + mass * mass)
        return (
            mom,
            rap,
            jnp.cos(azi),
            jnp.sin(azi),
            trans * jnp.exp(rap),
            trans * jnp.exp(-rap),
            mass * mass,
            ids,
        )

    ends = []
    for yy in range(ny):
        end = keys_ref[yy, 0, slots : slots + KIN_ROWS, :].astype(F32)
        for xx in range(1, nx):
            end = end + keys_ref[yy, xx, slots : slots + KIN_ROWS, :].astype(F32)
        ends.append(end)
    raw_terms = [
        jnp.concatenate(
            [ends[yy][zz * 8 + i : zz * 8 + i + 1] for zz in range(nz) for yy in range(ny)], axis=0
        )
        for i in range(5)
    ]
    ids = raw_terms[4]
    for i, term in enumerate(terms_of(*raw_terms)):
        for k in range(TILE // 128):
            terms[i, k] = term[:, k * 128 : (k + 1) * 128]
    ends = [pair_ref[zz, slots : slots + KIN_ROWS, 0:slots].astype(F32) for zz in range(nz)]
    raw_terms = [
        jnp.concatenate([ends[zz][i : i + 1] for zz in range(nz)], axis=0) for i in range(5)
    ]
    for i, term in enumerate(terms_of(*raw_terms)):
        for zz in range(nz):
            q_terms[i, zz * slots : (zz + 1) * slots, :] = jnp.broadcast_to(
                term[zz : zz + 1], (slots, slots)
            ).T

    counts = []
    for row in (0, UNIT - 1):
        bound = q_terms[7, pl.ds(row, n_units, stride=UNIT), :]
        count = jnp.zeros((n_units, 128), F32)
        for t in range(n_tiles):
            for k in range(TILE // 128):
                key = terms[7, k, t : t + 1, :]
                count = count + jnp.where(key < bound if row == 0 else key <= bound, 1.0, 0.0)
        counts.append(jnp.sum(count, axis=1, keepdims=True).astype(jnp.int32))
    start = jnp.minimum(counts[0] // TILE, n_tiles - 1)
    stop = jnp.maximum((counts[1] + (TILE - 1)) // TILE, start + 1)
    ranges[0] = jnp.broadcast_to(start, (n_units, 128))
    ranges[1] = jnp.broadcast_to(stop, (n_units, 128))
    to_scalars = pltpu.make_async_copy(ranges, limits, load_sem.at[2])
    to_scalars.start()

    wkt = wk_ref[...].astype(F32).T.astype(BF16)
    for yy in range(ny):
        for zz in range(nz):
            rows = jnp.concatenate(
                [keys_ref[yy, xx, zz * half : (zz + 1) * half, :] for xx in range(nx)], axis=0
            )
            at = slice((zz * ny + yy) * TILE, (zz * ny + yy + 1) * TILE)
            kt_ref[:, at] = lax.dot_general(
                wkt, rows, (((1,), (1,)), ((), ())), preferred_element_type=F32
            ).astype(BF16)
            v_ref[at, :] = jnp.dot(rows, wv_ref[...], preferred_element_type=F32).astype(BF16)
    for k in range(STRIDE - 1):
        v_ref[(n_tiles + k) * TILE : (n_tiles + k + 1) * TILE, :] = jnp.zeros((TILE, width), BF16)

    lane_head = lax.broadcasted_iota(jnp.int32, (GROUP, width), 1) // head_size
    for zz in range(nz):
        queries = jnp.dot(pair_ref[zz, 0:slots, :], wq_ref[...], preferred_element_type=F32)
        for base in range(0, slots, GROUP):
            rows = queries[base : base + GROUP]
            at = (zz * slots + base) * heads
            qm_ref[at : at + rows_g, :] = jnp.concatenate(
                [jnp.where(lane_head == h, rows, 0.0) for h in range(heads)], axis=0
            ).astype(BF16)

    top_ref[...] = jnp.full_like(top_ref, -1e30)
    total_ref[...] = jnp.zeros_like(total_ref)
    acc_ref[...] = jnp.zeros_like(acc_ref)

    to_scalars.wait()

    def following(u, t):
        more = t + 1 < limits[1, u, 0]
        then = jnp.where(more, u, jnp.minimum(u + 1, n_units - 1))
        return then, jnp.where(more, t + 1, limits[0, then, 0])

    steps = limits[1, 0, 0] - limits[0, 0, 0]
    for u in range(1, n_units):
        steps = steps + limits[1, u, 0] - limits[0, u, 0]

    def features(p, u, t):
        for g in range(groups):
            base = pl.multiple_of(u * UNIT + g * GROUP, GROUP)
            qt = [q_terms[i, pl.ds(base, GROUP), :] for i in range(7)]
            columns = []
            for i in range(TILE // 128):
                kt = [terms[j, i, pl.ds(t, 1), :] for j in range(7)]
                gap = qt[1] - kt[1]
                cos_gap = qt[2] * kt[2] + qt[3] * kt[3]
                dist = gap * gap + (2.0 - 2.0 * cos_gap)
                small = jnp.minimum(qt[0], kt[0])
                msq = (
                    qt[6]
                    + kt[6]
                    + (qt[4] * kt[5] + qt[5] * kt[4] - 2.0 * (qt[0] * kt[0] * cos_gap))
                )
                f = [
                    jnp.log(1.0 + dist),
                    jnp.log(1.0 + small * small * dist),
                    small / (qt[0] + kt[0]),
                    jnp.log(1.0 + msq),
                ]
                fh, fl = split_two(jnp.concatenate(f, axis=0))
                columns.append(
                    jnp.concatenate([fh, fl, fh, jnp.ones((2 * GROUP, 128), BF16)], axis=0)
                )
            fresh[p, g] = jnp.concatenate(columns, axis=1)

    def hiddens(p):
        for g in range(groups):
            z = jnp.dot(wfirst[...], fresh[p, g], preferred_element_type=F32)
            hidden[p, g] = z[0 : hid * GROUP].astype(BF16)
            linear[p, g] = z[hid * GROUP :]

    def gelus(p):
        for g in range(groups):
            inner = hidden[p, g]
            turned[p, g] = inner * jnp.tanh(inner * (ALPHA + inner * inner))

    def scores(p, u, t, away):
        start = pl.multiple_of(t * TILE, TILE)
        first_row = pl.multiple_of(u * rows_u, rows_u)
        products = jnp.dot(
            qm_ref[pl.ds(first_row, rows_u), :],
            kt_ref[:, pl.ds(start, TILE)],
            preferred_element_type=F32,
        )
        for g in range(groups):
            base = pl.multiple_of(u * UNIT + g * GROUP, GROUP)
            bias = jnp.dot(wsecond[...], turned[p, g], preferred_element_type=F32)
            s = products[g * rows_g : (g + 1) * rows_g] + (bias + linear[p, g])
            own = q_terms[7, pl.ds(base, GROUP), :] + away
            live = jnp.concatenate(
                [own == terms[7, i, pl.ds(t, 1), :] for i in range(TILE // 128)], axis=1
            )
            s = jnp.where(live[None], s.reshape(heads, GROUP, TILE), -1e30).reshape(rows_g, TILE)
            at = pl.ds(pl.multiple_of(first_row + g * rows_g, rows_g), rows_g)
            s_ref[at, pl.ds(start, TILE)] = s
            run_max = top_ref[at, :]
            for i in range(0, TILE, 128):
                run_max = jnp.maximum(run_max, s[:, i : i + 128])
            top_ref[at, :] = run_max

    def score_steps(i, carry):
        for p in range(2):
            u0, t0, u1, t1, u2, t2, u3, t3 = carry
            scores(1 - p, u3, t3, jnp.where(2 * i + p >= 3, 0.0, 100.0))
            hiddens(1 - p)
            gelus(p)
            features(p, u0, t0)
            carry = (*following(u0, t0), u0, t0, u1, t1, u2, t2)
        return carry

    zero = jnp.int32(0)
    t_first = limits[0, 0, 0]
    lax.fori_loop(0, (steps + 4) // 2, score_steps, (zero, t_first) * 4)

    for u in range(n_units):
        at = slice(u * rows_u, (u + 1) * rows_u)
        top_ref[at, :] = jnp.broadcast_to(
            jnp.max(top_ref[at, :], axis=1, keepdims=True), (rows_u, 128)
        )

    for u in range(n_units):
        for k in range(STRIDE - 1):
            start = pl.multiple_of((limits[1, u, 0] + k) * TILE, TILE)
            s_ref[u * rows_u : (u + 1) * rows_u, pl.ds(start, TILE)] = jnp.full(
                (rows_u, TILE), -1e30, F32
            )
    weight_ref[...] = jnp.zeros_like(weight_ref)
    span = STRIDE * TILE

    def stride_on(u, t):
        more = t + STRIDE < limits[1, u, 0]
        then = jnp.where(more, u, jnp.minimum(u + 1, n_units - 1))
        return then, jnp.where(more, t + STRIDE, limits[0, then, 0])

    def apply(u, t):
        at = pl.ds(pl.multiple_of(u * rows_u, rows_u), rows_u)
        acc_ref[at, :] += jnp.dot(
            weight_ref[...],
            v_ref[pl.ds(pl.multiple_of(t * TILE, TILE), span), :],
            preferred_element_type=F32,
        )

    def weigh(u, t):
        at = pl.ds(pl.multiple_of(u * rows_u, rows_u), rows_u)
        top = top_ref[at, :]
        total = total_ref[at, :]
        for i in range(0, span, 128):
            cols = pl.ds(pl.multiple_of(t * TILE + i, 128), 128)
            weight = jnp.exp2((s_ref[at, cols] - top) * (LOG2E / root))
            total = total + weight
            weight_ref[:, i : i + 128] = weight.astype(BF16)
        total_ref[at, :] = total

    def value_step(i, carry):
        u0, t0, u1, t1 = carry
        apply(u1, t1)
        weigh(u0, t0)
        return (*stride_on(u0, t0), u0, t0)

    strides = zero
    for u in range(n_units):
        strides = strides + (limits[1, u, 0] - limits[0, u, 0] + STRIDE - 1) // STRIDE
    _, _, u1, t1 = lax.fori_loop(0, strides, value_step, (zero, t_first, zero, t_first))
    apply(u1, t1)

    lane = lax.broadcasted_iota(jnp.int32, (rows_g, slots), 1)
    row = lax.rem(lax.broadcasted_iota(jnp.int32, (rows_g, slots), 0), GROUP)
    for zz in range(nz):
        level = jnp.zeros((rows_g, slots), F32)
        for base in range(0, slots, GROUP):
            at = (zz * slots + base) * heads
            total = jnp.sum(total_ref[at : at + rows_g, :], axis=1, keepdims=True)
            level = jnp.where(
                lane == base + row,
                top_ref[at : at + rows_g, :] * (LOG2E / root) + jnp.log(total) * LOG2E,
                level,
            )
            total = 1.0 / total
            out = jnp.zeros((GROUP, width), F32)
            for h in range(heads):
                rows = slice(at + h * GROUP, at + (h + 1) * GROUP)
                scaled = acc_ref[rows, :] * total[h * GROUP : (h + 1) * GROUP]
                out = jnp.where(lane_head == h, scaled, out)
            held_ref[base : base + GROUP, :] = out
        out_ref[zz] = held_ref[...].astype(BF16)
        level_ref[zz] = jnp.sum(level.reshape(heads, GROUP, slots), axis=1)


def finish_kernel(
    cube,
    part_ref,
    level_ref,
    wo_ref,
    gain_ref,
    out_ref,
    part_in,
    level_in,
    send_sem,
    recv_sem,
):
    _, ny, nx = cube
    z, y, x = mesh_place(cube)
    near = {"blk": ((1 - z) * ny + y) * nx + x}
    heads = level_ref.shape[1]
    width = part_ref.shape[2]
    barrier = pltpu.get_barrier_semaphore()
    pl.semaphore_signal(barrier, inc=1, device_id=near, device_id_type=MESH)
    pl.semaphore_wait(barrier, 1)
    copies = [
        pltpu.make_async_remote_copy(
            src_ref=src,
            dst_ref=dst,
            send_sem=send_sem.at[i],
            recv_sem=recv_sem.at[i],
            device_id=near,
            device_id_type=MESH,
        )
        for i, (src, dst) in enumerate(
            [(part_ref.at[1 - z], part_in), (level_ref.at[1 - z], level_in)]
        )
    ]
    for copy in copies:
        copy.start()
    spread = (
        lax.broadcasted_iota(jnp.int32, (heads, width), 1) // (width // heads)
        == lax.broadcasted_iota(jnp.int32, (heads, width), 0)
    ).astype(F32)
    for copy in copies:
        copy.wait()
    share = 1.0 / (1.0 + jnp.exp2(level_in[...] - level_ref[z]))
    share = jnp.dot(share.T, spread, precision=HIGHEST, preferred_element_type=F32)
    theirs = part_in[...].astype(F32)
    attended = theirs + share * (part_ref[z].astype(F32) - theirs)
    mixed = jnp.dot(attended.astype(BF16), wo_ref[...], preferred_element_type=F32)
    out_ref[...] = layer_norm(mixed, gain_ref[...]).astype(BF16)


def shards(
    n_grp,
    cube,
    raw,
    raw_kin,
    reader,
    event_id,
    pre_gain,
    w_query,
    w_key,
    w_value,
    w_out,
    post_gain,
    pair_w1,
    pair_b1,
    pair_w2,
):
    slots, width = raw.shape[2], raw.shape[3]
    heads = pair_w2.shape[1]
    nz, ny, nx = cube
    vmem = pl.BlockSpec(memory_space=pltpu.VMEM)
    free = pl.BlockSpec(memory_space=pl.ANY)
    dma = pltpu.SemaphoreType.DMA
    tall = slots + KIN_ROWS
    pair, keys = pl.pallas_call(
        functools.partial(exchange_kernel, n_grp, cube),
        out_shape=(
            jax.ShapeDtypeStruct((nz, tall, width), BF16),
            jax.ShapeDtypeStruct((ny, nx, tall, width), BF16),
        ),
        in_specs=[vmem] * 5,
        out_specs=(free, free),
        scratch_shapes=[
            pltpu.VMEM((n_grp, slots, width), BF16),
            pltpu.VMEM((n_grp, 8, slots), F32),
            pltpu.VMEM((n_grp, 8, slots), F32),
            pltpu.VMEM((tall, width), BF16),
            pltpu.VMEM((tall, width), BF16),
            pltpu.VMEM((tall, width), BF16),
            dma((n_grp,)),
            dma((n_grp,)),
            dma((n_grp,)),
            dma((n_grp,)),
            dma((15,)),
            dma((15,)),
            dma((3,)),
        ],
        compiler_params=pltpu.CompilerParams(collective_id=0, has_side_effects=True),
        name="exchange",
    )(raw, raw_kin, reader, event_id, pre_gain[None])

    own_rows = nz * slots
    n_tiles = nz * ny
    feats, hid = pair_w1.shape
    groups = UNIT // GROUP
    rows_all = heads * own_rows
    mixing = (3 * feats + 2) * GROUP
    part, level = pl.pallas_call(
        functools.partial(attend_kernel, heads),
        out_shape=(
            jax.ShapeDtypeStruct((nz, slots, width), BF16),
            jax.ShapeDtypeStruct((nz, heads, slots), F32),
        ),
        in_specs=[free, free] + [vmem] * 6,
        out_specs=(vmem, vmem),
        scratch_shapes=[
            pltpu.VMEM((nz, tall, width), BF16),
            pltpu.VMEM((ny, nx, tall, width), BF16),
            dma((3,)),
            pltpu.VMEM((width, n_tiles * TILE), BF16),
            pltpu.VMEM(((n_tiles + STRIDE - 1) * TILE, width), BF16),
            pltpu.VMEM((8, TILE // 128, n_tiles, 128), F32),
            pltpu.VMEM((8, own_rows, slots), F32),
            pltpu.VMEM((rows_all, width), BF16),
            pltpu.VMEM((rows_all, (n_tiles + STRIDE - 1) * TILE), F32),
            pltpu.VMEM((rows_all, 128), F32),
            pltpu.VMEM((rows_all, 128), F32),
            pltpu.VMEM((rows_all, width), F32),
            pltpu.VMEM(((hid + heads) * GROUP, mixing), BF16),
            pltpu.VMEM((heads * GROUP, hid * GROUP), BF16),
            pltpu.VMEM((2, groups, mixing, TILE), BF16),
            pltpu.VMEM((2, groups, hid * GROUP, TILE), BF16),
            pltpu.VMEM((2, groups, heads * GROUP, TILE), F32),
            pltpu.VMEM((2, groups, hid * GROUP, TILE), BF16),
            pltpu.VMEM((heads * UNIT, STRIDE * TILE), BF16),
            pltpu.VMEM((slots, width), F32),
            pltpu.VMEM((2, own_rows // UNIT, 128), jnp.int32),
            pltpu.SMEM((2, own_rows // UNIT, 128), jnp.int32),
        ],
        compiler_params=pltpu.CompilerParams(vmem_limit_bytes=63 * 1024 * 1024),
        name="attend",
    )(pair, keys, w_query, w_key, w_value, pair_w1, pair_b1[None], pair_w2.T)

    encoded = pl.pallas_call(
        functools.partial(finish_kernel, cube),
        out_shape=jax.ShapeDtypeStruct((slots, width), BF16),
        in_specs=[vmem] * 4,
        out_specs=vmem,
        scratch_shapes=[
            pltpu.VMEM((slots, width), BF16),
            pltpu.VMEM((heads, slots), F32),
            dma((2,)),
            dma((2,)),
        ],
        compiler_params=pltpu.CompilerParams(collective_id=1, has_side_effects=True),
        name="finish",
    )(part, level, w_out, post_gain[None])
    return encoded[None]


def solution(mesh):
    in_specs = (
        P("grp", None, "blk", None),
        P("grp", None, None, "blk"),
        P("grp", "blk"),
        P("grp", "blk"),
        P(),
        P(),
        P(),
        P(),
        P(),
        P(),
        P(),
        P(),
        P(),
    )
    out_specs = P("grp", "blk", None)
    cube = (2, 4, mesh.shape["blk"] // 8)
    body = functools.partial(shards, mesh.shape["grp"], cube)
    return jax.shard_map(body, mesh=mesh, in_specs=in_specs, out_specs=out_specs, check_vma=False)
```

```python
import functools
import math

import jax
import jax.numpy as jnp
from jax import lax
from jax.experimental import pallas as pl
from jax.experimental.pallas import tpu as pltpu
from jax.sharding import PartitionSpec as P

MESH = pl.DeviceIdType.MESH
F32 = jnp.float32
BF16 = jnp.bfloat16
HIGHEST = lax.Precision.HIGHEST

KIN_ROWS = 16
GROUP = 8
UNIT = 16
TILE = 256
SCORE_STEPS = 6
VALUE_STEPS = 8

GELU_A = math.sqrt(2.0 / math.pi)
GELU_B = GELU_A * 0.044715
GELU_S = GELU_B ** (-1.0 / 3.0)
ALPHA = GELU_A * GELU_S
LOG2E = 1.0 / math.log(2.0)


def layer_norm(rows, gain):
    center = rows - jnp.mean(rows, axis=-1, keepdims=True)
    spread = jnp.mean(center * center, axis=-1, keepdims=True)
    return center * lax.rsqrt(spread + 1e-05) * gain


def mesh_place(cube):
    _, ny, nx = cube
    b = lax.axis_index("blk")
    return b // (ny * nx), lax.rem(b // nx, ny), lax.rem(b, nx)


def exchange_kernel(
    n_grp,
    cube,
    raw_ref,
    kin_ref,
    reader_ref,
    event_ref,
    gain_ref,
    w1_ref,
    b1_ref,
    w2t_ref,
    pair_ref,
    keys_ref,
    wfirst,
    wsecond,
    inbox,
    kin_send,
    kin_in,
    block,
    other,
    payload,
    send_sem,
    recv_sem,
    kin_send_sem,
    kin_recv_sem,
    link_send,
    link_recv,
    own_sem,
):
    nz, ny, nx = cube
    g = lax.axis_index("grp")
    z, y, x = mesh_place(cube)
    slots = raw_ref.shape[2]
    width = raw_ref.shape[3]
    half = slots // nz

    def blk(z, y, x):
        return {"blk": (z * ny + y) * nx + x}

    partners = [{"grp": lax.rem(g + k, n_grp)} for k in range(1, n_grp)]
    partners.append(blk(1 - z, y, x))
    partners += [blk(z, lax.rem(y + k, ny), x) for k in range(1, ny)]
    partners += [blk(z, y, lax.rem(x + k, nx)) for k in range(1, nx)]
    barrier = pltpu.get_barrier_semaphore()
    for partner in partners:
        pl.semaphore_signal(barrier, inc=1, device_id=partner, device_id_type=MESH)
    load = pltpu.make_async_copy(raw_ref.at[0, g], inbox.at[0], own_sem.at[0])
    load.start()
    kin_send[...] = jnp.zeros_like(kin_send)
    for k in range(n_grp):
        kin_send[k, 0:4, :] = kin_ref[0, k].astype(F32)
    pl.semaphore_wait(barrier, len(partners))

    copies = []
    for k in range(1, n_grp):
        to = lax.rem(g + k, n_grp)
        for src, dst, ssem, rsem in (
            (raw_ref.at[0, to], inbox.at[n_grp - k], send_sem, recv_sem),
            (kin_send.at[to], kin_in.at[n_grp - k], kin_send_sem, kin_recv_sem),
        ):
            copy = pltpu.make_async_remote_copy(
                src_ref=src,
                dst_ref=dst,
                send_sem=ssem.at[k],
                recv_sem=rsem.at[n_grp - k],
                device_id={"grp": to},
                device_id_type=MESH,
            )
            copy.start()
            copies.append(copy)

    pair_weights(w1_ref[...], b1_ref[...], w2t_ref[...], width // w2t_ref.shape[0], wfirst, wsecond)
    wanted = lax.rem(reader_ref[...] - g + n_grp, n_grp)
    load.wait()
    column = jnp.broadcast_to(wanted, (slots, slots)).T
    kin = jnp.where(wanted == 0, kin_send[g, 0:4, :], 0.0)
    sides = [
        jnp.where(column == 0, inbox[0][:, h : h + slots].astype(F32), 0.0)
        for h in range(0, width, slots)
    ]
    for copy in copies:
        copy.wait()
    for k in range(1, n_grp):
        kin = kin + jnp.where(wanted == k, kin_in[k, 0:4, :], 0.0)
        sides = [
            side
            + jnp.where(column == k, inbox[k][:, i * slots : (i + 1) * slots].astype(F32), 0.0)
            for i, side in enumerate(sides)
        ]
    tokens = jnp.concatenate(sides, axis=1)
    block[0:slots, :] = layer_norm(tokens, gain_ref[...]).astype(BF16)
    tail = jnp.concatenate(
        [kin, event_ref[...].astype(F32), jnp.zeros((8 - 5, slots), F32)], axis=0
    )
    tail = jnp.concatenate([tail, tail], axis=0)
    block[slots : slots + KIN_ROWS, :] = jnp.concatenate([tail, tail], axis=1).astype(BF16)

    def push(slot, src, dst, to):
        copy = pltpu.make_async_remote_copy(
            src_ref=src,
            dst_ref=dst,
            send_sem=link_send.at[slot],
            recv_sem=link_recv.at[slot],
            device_id=to,
            device_id_type=MESH,
        )
        copy.start()
        return copy

    mine = pl.ds(pl.multiple_of(z * half, half), half)
    theirs = pl.ds(pl.multiple_of((1 - z) * half, half), half)
    ends = pl.ds(slots, KIN_ROWS)
    near = blk(1 - z, y, x)
    first = [
        push(0, block.at[theirs], other.at[theirs], near),
        push(1, block.at[ends], other.at[ends], near),
    ]
    rows_own = pl.ds(pl.multiple_of(z * (half + KIN_ROWS), 16), half)
    rows_other = pl.ds(pl.multiple_of((1 - z) * half, 16), half + KIN_ROWS)
    x_peers = [blk(z, y, lax.rem(x + k, nx)) for k in (1, nx - 1, 2)]
    y_peers = [blk(z, lax.rem(y + k, ny), x) for k in (1, ny - 1, 2)]
    own_x = [
        push(3 + i, block.at[mine], keys_ref.at[y, x, rows_own], peer)
        for i, peer in enumerate(x_peers)
    ]
    own_here = pltpu.make_async_copy(block.at[mine], keys_ref.at[y, x, rows_own], own_sem.at[0])
    own_here.start()
    for copy in first:
        copy.wait()

    ends_own = block[ends, :].astype(F32)
    ends_other = other[ends, :].astype(F32)
    part = lax.broadcasted_iota(jnp.int32, (KIN_ROWS, width), 0) // 8
    lane = lax.broadcasted_iota(jnp.int32, (KIN_ROWS, width), 1) // half
    both = jnp.where(part == z, ends_own, ends_other)
    swapped = jnp.concatenate([both[:, half:], both[:, :half]], axis=1)
    both = jnp.where(lax.rem(lane, 2) == z, both, swapped)
    payload[pl.ds(pl.multiple_of(z * half, 16), KIN_ROWS), :] = jnp.where(
        lane == x, both, 0.0
    ).astype(BF16)
    payload[pl.ds(pl.multiple_of((1 - z) * KIN_ROWS, 16), half), :] = other[mine, :]
    other_y = [
        push(6 + i, payload, keys_ref.at[y, x, rows_other], peer)
        for i, peer in enumerate(y_peers)
    ]
    other_here = pltpu.make_async_copy(payload, keys_ref.at[y, x, rows_other], own_sem.at[1])
    other_here.start()
    rest = push(2, block.at[mine], other.at[mine], near)

    def line(slot, view, peers):
        lower, upper = view(0), view(1)
        right, left = peers[0], peers[1]
        return (
            [push(slot, lower, lower, right), push(slot + 1, upper, upper, left)],
            [push(slot + 2, upper, upper, right), push(slot + 3, lower, lower, left)],
        )

    def view_x(yy):
        return lambda part: keys_ref.at[yy, pl.ds(part * (nx // 2), nx // 2), rows_own]

    def view_y(xx):
        return lambda part: keys_ref.at[pl.ds(part * (ny // 2), ny // 2), xx, rows_other]

    own_here.wait()
    for copy in own_x:
        copy.wait()
    lines_x = line(9, view_x(y), y_peers)
    other_here.wait()
    for copy in other_y:
        copy.wait()
    lines_y = line(15, view_y(x), x_peers)
    onward = []
    for slot, lines, view, place, size, peers in (
        (13, lines_x, view_x, y, ny, y_peers),
        (19, lines_y, view_y, x, nx, x_peers),
    ):
        for copy in lines[0]:
            copy.wait()
        lower = view(lax.rem(place + size - 1, size))(0)
        upper = view(lax.rem(place + 1, size))(1)
        onward += [push(slot, lower, lower, peers[0]), push(slot + 1, upper, upper, peers[1])]
    rest.wait()
    pair = [
        pltpu.make_async_copy(block, pair_ref.at[z], own_sem.at[0]),
        pltpu.make_async_copy(other, pair_ref.at[1 - z], own_sem.at[1]),
    ]
    for copy in pair:
        copy.start()
    for copy in pair + lines_x[1] + lines_y[1] + onward:
        copy.wait()


def split_two(value):
    high = value.astype(BF16)
    low = (value - high.astype(F32)).astype(BF16)
    return high, low


def spread_over(weight):
    m, c = weight.shape
    up = (
        lax.broadcasted_iota(jnp.int32, (m * GROUP, m), 0) // GROUP
        == lax.broadcasted_iota(jnp.int32, (m * GROUP, m), 1)
    ).astype(F32)
    across = (
        lax.broadcasted_iota(jnp.int32, (c, c * GROUP), 1) // GROUP
        == lax.broadcasted_iota(jnp.int32, (c, c * GROUP), 0)
    ).astype(F32)
    tall = jnp.dot(up, weight, precision=HIGHEST, preferred_element_type=F32)
    wide = jnp.dot(tall, across, precision=HIGHEST, preferred_element_type=F32)
    same = (
        lax.broadcasted_iota(jnp.int32, (m * GROUP, c * GROUP), 0) % GROUP
        == lax.broadcasted_iota(jnp.int32, (m * GROUP, c * GROUP), 1) % GROUP
    )
    return jnp.where(same, wide, 0.0)


def pair_weights(w1, b1, w2t, head_size, wfirst, wsecond):
    feats, hid = w1.shape
    root = math.sqrt(head_size)
    first = jnp.concatenate([w1, b1, jnp.zeros((8 - feats - 1, hid), F32)], axis=0)
    line = lax.dot_general(
        w2t, first, (((1,), (1,)), ((), ())), precision=HIGHEST, preferred_element_type=F32
    ) * (0.5 * root)
    part = feats * GROUP

    stacked = jnp.concatenate([first.T * (1.0 / GELU_S), line], axis=0)
    high, low = split_two(spread_over(stacked))
    wfirst[:, 0:part] = high[:, 0:part]
    wfirst[:, part : 2 * part] = high[:, 0:part]
    wfirst[:, 2 * part : 3 * part] = low[:, 0:part]
    wfirst[:, 3 * part : 3 * part + GROUP] = high[:, part : part + GROUP]
    wfirst[:, 3 * part + GROUP : 3 * part + 2 * GROUP] = low[:, part : part + GROUP]
    wsecond[...] = spread_over(w2t * (0.5 * root * GELU_S)).astype(BF16)


def attend_kernel(
    heads,
    pair_hbm,
    keys_hbm,
    wq_ref,
    wk_ref,
    wv_ref,
    wfirst,
    wsecond,
    out_ref,
    level_ref,
    pair_ref,
    keys_ref,
    load_sem,
    kt_ref,
    v_ref,
    terms,
    q_terms,
    qm_ref,
    s_ref,
    top_ref,
    total_ref,
    acc_ref,
    fresh,
    hidden,
    linear,
    turned,
    weight_ref,
    held_ref,
    ranges,
    limits,
):
    loads = [
        pltpu.make_async_copy(pair_hbm, pair_ref, load_sem.at[0]),
        pltpu.make_async_copy(keys_hbm, keys_ref, load_sem.at[1]),
    ]
    for load in loads:
        load.start()
    nz, slots, width = out_ref.shape
    ny, nx = keys_ref.shape[0:2]
    half = slots // nz
    own_rows = nz * slots
    head_size = width // heads
    hid = wsecond.shape[1] // GROUP
    root = math.sqrt(head_size)
    groups = UNIT // GROUP
    rows_g = heads * GROUP
    rows_u = groups * rows_g
    n_units = own_rows // UNIT
    n_tiles = nz * ny

    for load in loads:
        load.wait()

    def terms_of(mom, rap, azi, mass, ids):
        trans = jnp.sqrt(mom * mom + mass * mass)
        return (
            mom,
            rap,
            jnp.cos(azi),
            jnp.sin(azi),
            trans * jnp.exp(rap),
            trans * jnp.exp(-rap),
            mass * mass,
            ids,
        )

    ends = []
    for yy in range(ny):
        end = keys_ref[yy, 0, half : half + KIN_ROWS, :].astype(F32)
        for xx in range(1, nx):
            end = end + keys_ref[yy, xx, half : half + KIN_ROWS, :].astype(F32)
        ends.append(end)
    raw_terms = [
        jnp.concatenate(
            [ends[yy][zz * 8 + i : zz * 8 + i + 1] for zz in range(nz) for yy in range(ny)], axis=0
        )
        for i in range(5)
    ]
    ids = raw_terms[4]
    for i, term in enumerate(terms_of(*raw_terms)):
        for k in range(TILE // 128):
            terms[i, k] = term[:, k * 128 : (k + 1) * 128]
    ends = [pair_ref[zz, slots : slots + KIN_ROWS, 0:slots].astype(F32) for zz in range(nz)]
    raw_terms = [
        jnp.concatenate([ends[zz][i : i + 1] for zz in range(nz)], axis=0) for i in range(5)
    ]
    for i, term in enumerate(terms_of(*raw_terms)):
        for zz in range(nz):
            q_terms[i, zz * slots : (zz + 1) * slots, :] = jnp.broadcast_to(
                term[zz : zz + 1], (slots, slots)
            ).T

    counts = []
    for row in (0, UNIT - 1):
        bound = q_terms[7, pl.ds(row, n_units, stride=UNIT), :]
        count = jnp.zeros((n_units, 128), F32)
        for t in range(n_tiles):
            for k in range(TILE // 128):
                key = terms[7, k, t : t + 1, :]
                count = count + jnp.where(key < bound if row == 0 else key <= bound, 1.0, 0.0)
        counts.append(jnp.sum(count, axis=1, keepdims=True).astype(jnp.int32))
    start = jnp.minimum(counts[0] // TILE, n_tiles - 1)
    stop = jnp.maximum((counts[1] + (TILE - 1)) // TILE, start + 1)
    ranges[0] = jnp.broadcast_to(start, (n_units, 128))
    ranges[1] = jnp.broadcast_to(stop, (n_units, 128))
    to_scalars = pltpu.make_async_copy(ranges, limits, load_sem.at[2])
    to_scalars.start()

    wkt = wk_ref[...].astype(F32).T.astype(BF16)
    for yy in range(ny):
        for zz in range(nz):
            rows = jnp.concatenate(
                [
                    keys_ref[yy, xx, zz * (half + KIN_ROWS) : zz * (half + KIN_ROWS) + half, :]
                    for xx in range(nx)
                ],
                axis=0,
            )
            at = slice((zz * ny + yy) * TILE, (zz * ny + yy + 1) * TILE)
            kt_ref[:, at] = lax.dot_general(
                wkt, rows, (((1,), (1,)), ((), ())), preferred_element_type=F32
            ).astype(BF16)
            v_ref[at, :] = jnp.dot(rows, wv_ref[...], preferred_element_type=F32).astype(BF16)

    lane_head = lax.broadcasted_iota(jnp.int32, (GROUP, width), 1) // head_size
    for zz in range(nz):
        queries = jnp.dot(pair_ref[zz, 0:slots, :], wq_ref[...], preferred_element_type=F32)
        for base in range(0, slots, GROUP):
            rows = queries[base : base + GROUP]
            at = (zz * slots + base) * heads
            qm_ref[at : at + rows_g, :] = jnp.concatenate(
                [jnp.where(lane_head == h, rows, 0.0) for h in range(heads)], axis=0
            ).astype(BF16)

    top_ref[...] = jnp.full_like(top_ref, -1e30)
    total_ref[...] = jnp.zeros_like(total_ref)
    acc_ref[...] = jnp.zeros_like(acc_ref)

    to_scalars.wait()

    def following(u, t):
        more = t + 1 < limits[1, u, 0]
        then = jnp.where(more, u, jnp.minimum(u + 1, n_units - 1))
        return then, jnp.where(more, t + 1, limits[0, then, 0])

    steps = limits[1, 0, 0] - limits[0, 0, 0]
    for u in range(1, n_units):
        steps = steps + limits[1, u, 0] - limits[0, u, 0]

    def features(p, u, t):
        for g in range(groups):
            base = pl.multiple_of(u * UNIT + g * GROUP, GROUP)
            qt = [q_terms[i, pl.ds(base, GROUP), :] for i in range(7)]
            columns = []
            for i in range(TILE // 128):
                kt = [terms[j, i, pl.ds(t, 1), :] for j in range(7)]
                gap = qt[1] - kt[1]
                cos_gap = qt[2] * kt[2] + qt[3] * kt[3]
                dist = gap * gap + (2.0 - 2.0 * cos_gap)
                small = jnp.minimum(qt[0], kt[0])
                msq = (
                    qt[6]
                    + kt[6]
                    + (qt[4] * kt[5] + qt[5] * kt[4] - 2.0 * (qt[0] * kt[0] * cos_gap))
                )
                f = [
                    jnp.log(1.0 + dist),
                    jnp.log(1.0 + small * small * dist),
                    small / (qt[0] + kt[0]),
                    jnp.log(1.0 + msq),
                ]
                fh, fl = split_two(jnp.concatenate(f, axis=0))
                columns.append(
                    jnp.concatenate([fh, fl, fh, jnp.ones((2 * GROUP, 128), BF16)], axis=0)
                )
            fresh[p, g] = jnp.concatenate(columns, axis=1)

    def hiddens(p):
        for g in range(groups):
            z = jnp.dot(wfirst[...], fresh[p, g], preferred_element_type=F32)
            hidden[p, g] = z[0 : hid * GROUP].astype(BF16)
            linear[p, g] = z[hid * GROUP :]

    def gelus(p):
        for g in range(groups):
            inner = hidden[p, g]
            turned[p, g] = inner * jnp.tanh(inner * (ALPHA + inner * inner))

    def scores(p, u, t, away):
        start = pl.multiple_of(t * TILE, TILE)
        first_row = pl.multiple_of(u * rows_u, rows_u)
        products = jnp.dot(
            qm_ref[pl.ds(first_row, rows_u), :],
            kt_ref[:, pl.ds(start, TILE)],
            preferred_element_type=F32,
        )
        for g in range(groups):
            base = pl.multiple_of(u * UNIT + g * GROUP, GROUP)
            bias = jnp.dot(wsecond[...], turned[p, g], preferred_element_type=F32)
            s = products[g * rows_g : (g + 1) * rows_g] + (bias + linear[p, g])
            own = q_terms[7, pl.ds(base, GROUP), :] + away
            live = jnp.concatenate(
                [own == terms[7, i, pl.ds(t, 1), :] for i in range(TILE // 128)], axis=1
            )
            s = jnp.where(live[None], s.reshape(heads, GROUP, TILE), -1e30).reshape(rows_g, TILE)
            at = pl.ds(pl.multiple_of(first_row + g * rows_g, rows_g), rows_g)
            s_ref[at, pl.ds(start, TILE)] = s
            run_max = top_ref[at, :]
            for i in range(0, TILE, 128):
                run_max = jnp.maximum(run_max, s[:, i : i + 128])
            top_ref[at, :] = run_max

    def score_steps(i, carry):
        for k in range(SCORE_STEPS):
            p = k % 2
            u0, t0, u1, t1, u2, t2, u3, t3 = carry
            scores(1 - p, u3, t3, jnp.where(SCORE_STEPS * i + k >= 3, 0.0, 100.0))
            hiddens(1 - p)
            gelus(p)
            features(p, u0, t0)
            carry = (*following(u0, t0), u0, t0, u1, t1, u2, t2)
        return carry

    zero = jnp.int32(0)
    t_first = limits[0, 0, 0]
    lax.fori_loop(0, (steps + SCORE_STEPS + 2) // SCORE_STEPS, score_steps, (zero, t_first) * 4)

    for u in range(n_units):
        at = slice(u * rows_u, (u + 1) * rows_u)
        top_ref[at, :] = jnp.broadcast_to(
            jnp.max(top_ref[at, :], axis=1, keepdims=True), (rows_u, 128)
        )

    weight_ref[...] = jnp.zeros_like(weight_ref)

    def apply(p, u, t):
        at = pl.ds(pl.multiple_of(u * rows_u, rows_u), rows_u)
        acc_ref[at, :] += jnp.dot(
            weight_ref[p],
            v_ref[pl.ds(pl.multiple_of(t * TILE, TILE), TILE), :],
            preferred_element_type=F32,
        )

    def weigh(p, u, t, above):
        at = pl.ds(pl.multiple_of(u * rows_u, rows_u), rows_u)
        top = top_ref[at, :] + above
        total = total_ref[at, :]
        for i in range(0, TILE, 128):
            cols = pl.ds(pl.multiple_of(t * TILE + i, 128), 128)
            weight = jnp.exp2((s_ref[at, cols] - top) * (LOG2E / root))
            total = total + weight
            weight_ref[p, :, i : i + 128] = weight.astype(BF16)
        total_ref[at, :] = total

    def value_steps(i, carry):
        for k in range(VALUE_STEPS):
            u0, t0, u1, t1 = carry
            apply(1 - k % 2, u1, t1)
            weigh(k % 2, u0, t0, jnp.where(VALUE_STEPS * i + k < steps, 0.0, 1e32))
            carry = (*following(u0, t0), u0, t0)
        return carry

    lax.fori_loop(0, (steps + VALUE_STEPS) // VALUE_STEPS, value_steps, (zero, t_first) * 2)

    lane = lax.broadcasted_iota(jnp.int32, (rows_g, slots), 1)
    row = lax.rem(lax.broadcasted_iota(jnp.int32, (rows_g, slots), 0), GROUP)
    for zz in range(nz):
        level = jnp.zeros((rows_g, slots), F32)
        for base in range(0, slots, GROUP):
            at = (zz * slots + base) * heads
            total = jnp.sum(total_ref[at : at + rows_g, :], axis=1, keepdims=True)
            level = jnp.where(
                lane == base + row,
                top_ref[at : at + rows_g, :] * (LOG2E / root) + jnp.log(total) * LOG2E,
                level,
            )
            total = 1.0 / total
            out = jnp.zeros((GROUP, width), F32)
            for h in range(heads):
                rows = slice(at + h * GROUP, at + (h + 1) * GROUP)
                scaled = acc_ref[rows, :] * total[h * GROUP : (h + 1) * GROUP]
                out = jnp.where(lane_head == h, scaled, out)
            held_ref[base : base + GROUP, :] = out
        out_ref[zz] = held_ref[...].astype(BF16)
        level_ref[zz] = jnp.sum(level.reshape(heads, GROUP, slots), axis=1)


def finish_kernel(
    cube,
    part_ref,
    level_ref,
    wo_ref,
    gain_ref,
    out_ref,
    part_in,
    level_in,
    part_own,
    wo_own,
    send_sem,
    recv_sem,
    load_sem,
):
    _, ny, nx = cube
    z, y, x = mesh_place(cube)
    near = {"blk": ((1 - z) * ny + y) * nx + x}
    heads = level_ref.shape[1]
    width = part_ref.shape[2]
    barrier = pltpu.get_barrier_semaphore()
    pl.semaphore_signal(barrier, inc=1, device_id=near, device_id_type=MESH)
    loads = [
        pltpu.make_async_copy(part_ref.at[z], part_own, load_sem.at[0]),
        pltpu.make_async_copy(wo_ref, wo_own, load_sem.at[1]),
    ]
    for load in loads:
        load.start()
    pl.semaphore_wait(barrier, 1)
    copies = [
        pltpu.make_async_remote_copy(
            src_ref=src,
            dst_ref=dst,
            send_sem=send_sem.at[i],
            recv_sem=recv_sem.at[i],
            device_id=near,
            device_id_type=MESH,
        )
        for i, (src, dst) in enumerate(
            [(part_ref.at[1 - z], part_in), (level_ref.at[1 - z], level_in)]
        )
    ]
    for copy in copies:
        copy.start()
    spread = (
        lax.broadcasted_iota(jnp.int32, (heads, width), 1) // (width // heads)
        == lax.broadcasted_iota(jnp.int32, (heads, width), 0)
    ).astype(F32)
    for copy in loads + copies:
        copy.wait()
    share = 1.0 / (1.0 + jnp.exp2(level_in[...] - level_ref[z]))
    share = jnp.dot(share.T, spread, precision=HIGHEST, preferred_element_type=F32)
    theirs = part_in[...].astype(F32)
    attended = theirs + share * (part_own[...].astype(F32) - theirs)
    mixed = jnp.dot(attended.astype(BF16), wo_own[...], preferred_element_type=F32)
    out_ref[...] = layer_norm(mixed, gain_ref[...]).astype(BF16)


def shards(
    n_grp,
    cube,
    raw,
    raw_kin,
    reader,
    event_id,
    pre_gain,
    w_query,
    w_key,
    w_value,
    w_out,
    post_gain,
    pair_w1,
    pair_b1,
    pair_w2,
):
    slots, width = raw.shape[2], raw.shape[3]
    heads = pair_w2.shape[1]
    nz, ny, nx = cube
    vmem = pl.BlockSpec(memory_space=pltpu.VMEM)
    free = pl.BlockSpec(memory_space=pl.ANY)
    dma = pltpu.SemaphoreType.DMA
    tall = slots + KIN_ROWS
    feats, hid = pair_w1.shape
    mixing = (3 * feats + 2) * GROUP
    pair, keys, first, second = pl.pallas_call(
        functools.partial(exchange_kernel, n_grp, cube),
        out_shape=(
            jax.ShapeDtypeStruct((nz, tall, width), BF16),
            jax.ShapeDtypeStruct((ny, nx, tall, width), BF16),
            jax.ShapeDtypeStruct(((hid + heads) * GROUP, mixing), BF16),
            jax.ShapeDtypeStruct((heads * GROUP, hid * GROUP), BF16),
        ),
        in_specs=[free] + [vmem] * 7,
        out_specs=(free, free, vmem, vmem),
        scratch_shapes=[
            pltpu.VMEM((n_grp, slots, width), BF16),
            pltpu.VMEM((n_grp, 8, slots), F32),
            pltpu.VMEM((n_grp, 8, slots), F32),
            pltpu.VMEM((tall, width), BF16),
            pltpu.VMEM((tall, width), BF16),
            pltpu.VMEM((slots // nz + KIN_ROWS, width), BF16),
            dma((n_grp,)),
            dma((n_grp,)),
            dma((n_grp,)),
            dma((n_grp,)),
            dma((21,)),
            dma((21,)),
            dma((2,)),
        ],
        compiler_params=pltpu.CompilerParams(collective_id=0, has_side_effects=True),
        name="exchange",
    )(
        raw,
        raw_kin,
        reader,
        event_id,
        pre_gain[None],
        pair_w1,
        pair_b1[None],
        pair_w2.T,
    )

    own_rows = nz * slots
    n_tiles = nz * ny
    groups = UNIT // GROUP
    rows_all = heads * own_rows
    part, level = pl.pallas_call(
        functools.partial(attend_kernel, heads),
        out_shape=(
            jax.ShapeDtypeStruct((nz, slots, width), BF16),
            jax.ShapeDtypeStruct((nz, heads, slots), F32),
        ),
        in_specs=[free, free] + [vmem] * 5,
        out_specs=(vmem, vmem),
        scratch_shapes=[
            pltpu.VMEM((nz, tall, width), BF16),
            pltpu.VMEM((ny, nx, tall, width), BF16),
            dma((3,)),
            pltpu.VMEM((width, n_tiles * TILE), BF16),
            pltpu.VMEM((n_tiles * TILE, width), BF16),
            pltpu.VMEM((8, TILE // 128, n_tiles, 128), F32),
            pltpu.VMEM((8, own_rows, slots), F32),
            pltpu.VMEM((rows_all, width), BF16),
            pltpu.VMEM((rows_all, n_tiles * TILE), F32),
            pltpu.VMEM((rows_all, 128), F32),
            pltpu.VMEM((rows_all, 128), F32),
            pltpu.VMEM((rows_all, width), F32),
            pltpu.VMEM((2, groups, mixing, TILE), BF16),
            pltpu.VMEM((2, groups, hid * GROUP, TILE), BF16),
            pltpu.VMEM((2, groups, heads * GROUP, TILE), F32),
            pltpu.VMEM((2, groups, hid * GROUP, TILE), BF16),
            pltpu.VMEM((2, heads * UNIT, TILE), BF16),
            pltpu.VMEM((slots, width), F32),
            pltpu.VMEM((2, own_rows // UNIT, 128), jnp.int32),
            pltpu.SMEM((2, own_rows // UNIT, 128), jnp.int32),
        ],
        compiler_params=pltpu.CompilerParams(vmem_limit_bytes=63 * 1024 * 1024),
        name="attend",
    )(pair, keys, w_query, w_key, w_value, first, second)

    encoded = pl.pallas_call(
        functools.partial(finish_kernel, cube),
        out_shape=jax.ShapeDtypeStruct((slots, width), BF16),
        in_specs=[free, vmem, free, vmem],
        out_specs=vmem,
        scratch_shapes=[
            pltpu.VMEM((slots, width), BF16),
            pltpu.VMEM((heads, slots), F32),
            pltpu.VMEM((slots, width), BF16),
            pltpu.VMEM((width, width), BF16),
            dma((2,)),
            dma((2,)),
            dma((2,)),
        ],
        compiler_params=pltpu.CompilerParams(collective_id=1, has_side_effects=True),
        name="finish",
    )(part, level, w_out, post_gain[None])
    return encoded[None]


def solution(mesh):
    in_specs = (
        P("grp", None, "blk", None),
        P("grp", None, None, "blk"),
        P("grp", "blk"),
        P("grp", "blk"),
        P(),
        P(),
        P(),
        P(),
        P(),
        P(),
        P(),
        P(),
        P(),
    )
    out_specs = P("grp", "blk", None)
    cube = (2, 4, mesh.shape["blk"] // 8)
    body = functools.partial(shards, mesh.shape["grp"], cube)
    return jax.shard_map(body, mesh=mesh, in_specs=in_specs, out_specs=out_specs, check_vma=False)
```

```python
import functools
import math

import jax
import jax.numpy as jnp
from jax import lax
from jax.experimental import pallas as pl
from jax.experimental.pallas import tpu as pltpu
from jax.sharding import PartitionSpec as P

MESH = pl.DeviceIdType.MESH
F32 = jnp.float32
BF16 = jnp.bfloat16
HIGHEST = lax.Precision.HIGHEST

KIN_ROWS = 16
GROUP = 8
UNIT = 16
TILE = 256
SCORE_STEPS = 6
VALUE_STEPS = 8

GELU_A = math.sqrt(2.0 / math.pi)
GELU_B = GELU_A * 0.044715
GELU_S = GELU_B ** (-1.0 / 3.0)
ALPHA = GELU_A * GELU_S
LOG2E = 1.0 / math.log(2.0)


def layer_norm(rows, gain):
    center = rows - jnp.mean(rows, axis=-1, keepdims=True)
    spread = jnp.mean(center * center, axis=-1, keepdims=True)
    return center * lax.rsqrt(spread + 1e-05) * gain


def mesh_place(cube):
    _, ny, nx = cube
    b = lax.axis_index("blk")
    return b // (ny * nx), lax.rem(b // nx, ny), lax.rem(b, nx)


def exchange_kernel(
    n_grp,
    cube,
    raw_ref,
    kin_hbm,
    reader_hbm,
    event_hbm,
    gain_hbm,
    w1_hbm,
    b1_hbm,
    w2t_hbm,
    pair_ref,
    keys_ref,
    first_hbm,
    second_hbm,
    kin_ref,
    reader_ref,
    event_ref,
    gain_ref,
    w1_ref,
    b1_ref,
    w2t_ref,
    wfirst,
    wsecond,
    load_sem,
    inbox,
    kin_send,
    kin_in,
    block,
    mine,
    theirs,
    send_sem,
    recv_sem,
    kin_send_sem,
    kin_recv_sem,
    link_send,
    link_recv,
    own_sem,
):
    nz, ny, nx = cube
    g = lax.axis_index("grp")
    z, y, x = mesh_place(cube)
    slots = raw_ref.shape[2]
    width = raw_ref.shape[3]
    half = slots // nz

    def blk(z, y, x):
        return {"blk": (z * ny + y) * nx + x}

    partners = [{"grp": lax.rem(g + k, n_grp)} for k in range(1, n_grp)]
    x_peers = [blk(z, y, lax.rem(x + k, nx)) for k in range(1, nx)]
    y_peers = [blk(z, lax.rem(y + k, ny), x) for k in range(1, ny)]
    across = [blk(1 - z, lax.rem(y + k, ny), x) for k in range(ny)]
    partners += x_peers + y_peers + across
    barrier = pltpu.get_barrier_semaphore()
    for partner in partners:
        pl.semaphore_signal(barrier, inc=1, device_id=partner, device_id_type=MESH)
    loads = [
        pltpu.make_async_copy(src, dst, load_sem.at[i])
        for i, (src, dst) in enumerate(
            [
                (kin_hbm, kin_ref),
                (reader_hbm, reader_ref),
                (event_hbm, event_ref),
                (gain_hbm, gain_ref),
                (w1_hbm, w1_ref),
                (b1_hbm, b1_ref),
                (w2t_hbm, w2t_ref),
                (raw_ref.at[0, g], inbox.at[0]),
            ]
        )
    ]
    for load in loads:
        load.start()
    loads[0].wait()
    kin_send[...] = jnp.zeros_like(kin_send)
    for k in range(n_grp):
        kin_send[k, 0:4, :] = kin_ref[0, k].astype(F32)
    pl.semaphore_wait(barrier, len(partners))

    copies = []
    for k in range(1, n_grp):
        to = lax.rem(g + k, n_grp)
        for src, dst, ssem, rsem in (
            (raw_ref.at[0, to], inbox.at[n_grp - k], send_sem, recv_sem),
            (kin_send.at[to], kin_in.at[n_grp - k], kin_send_sem, kin_recv_sem),
        ):
            copy = pltpu.make_async_remote_copy(
                src_ref=src,
                dst_ref=dst,
                send_sem=ssem.at[k],
                recv_sem=rsem.at[n_grp - k],
                device_id={"grp": to},
                device_id_type=MESH,
            )
            copy.start()
            copies.append(copy)

    for load in loads[1:]:
        load.wait()
    pair_weights(w1_ref[...], b1_ref[...], w2t_ref[...], width // w2t_ref.shape[0], wfirst, wsecond)
    wanted = lax.rem(reader_ref[...] - g + n_grp, n_grp)
    stores = [
        pltpu.make_async_copy(wfirst, first_hbm, load_sem.at[0]),
        pltpu.make_async_copy(wsecond, second_hbm, load_sem.at[1]),
    ]
    for store in stores:
        store.start()
    column = jnp.broadcast_to(wanted, (slots, slots)).T
    kin = jnp.where(wanted == 0, kin_send[g, 0:4, :], 0.0)
    sides = [
        jnp.where(column == 0, inbox[0][:, h : h + slots].astype(F32), 0.0)
        for h in range(0, width, slots)
    ]
    for copy in copies:
        copy.wait()
    for k in range(1, n_grp):
        kin = kin + jnp.where(wanted == k, kin_in[k, 0:4, :], 0.0)
        sides = [
            side
            + jnp.where(column == k, inbox[k][:, i * slots : (i + 1) * slots].astype(F32), 0.0)
            for i, side in enumerate(sides)
        ]
    tokens = jnp.concatenate(sides, axis=1)
    normed = layer_norm(tokens, gain_ref[...]).astype(BF16)
    block[0:slots, :] = normed
    tail = jnp.concatenate(
        [kin, event_ref[...].astype(F32), jnp.zeros((KIN_ROWS - 5, slots), F32)], axis=0
    )
    double = jnp.concatenate([tail, tail], axis=1)
    swapped = jnp.concatenate([double[:, half:], double[:, :half]], axis=1)
    block[slots : slots + KIN_ROWS, :] = double.astype(BF16)
    lane = lax.broadcasted_iota(jnp.int32, (KIN_ROWS, width), 1) // half
    even = lax.rem(lane, 2)
    rows_z = jnp.where(z == 0, normed[0:half], normed[half : 2 * half])
    rows_not = jnp.where(z == 0, normed[half : 2 * half], normed[0:half])
    for ref, rows, side in ((mine, rows_z, z), (theirs, rows_not, 1 - z)):
        ref[0:half, :] = rows
        placed = jnp.where(even == side, double, swapped)
        ref[half : half + KIN_ROWS, :] = jnp.where(lane == x, placed, 0.0).astype(BF16)

    def push(slot, src, dst, to):
        copy = pltpu.make_async_remote_copy(
            src_ref=src,
            dst_ref=dst,
            send_sem=link_send.at[slot],
            recv_sem=link_recv.at[slot],
            device_id=to,
            device_id_type=MESH,
        )
        copy.start()
        return copy

    other_y = [push(k, theirs, keys_ref.at[y, x, z], peer) for k, peer in enumerate(across)]
    own_x = [push(4 + k, mine, keys_ref.at[y, x, z], peer) for k, peer in enumerate(x_peers)]
    moves = [push(7 + k, mine, keys_ref.at[y, x, z], peer) for k, peer in enumerate(y_peers)]
    moves.append(push(10, block, pair_ref.at[z], across[0]))
    own_here = pltpu.make_async_copy(mine, keys_ref.at[y, x, z], own_sem.at[0])
    own_here.start()
    pair_here = pltpu.make_async_copy(block, pair_ref.at[z], own_sem.at[1])
    pair_here.start()
    slot = 11
    near_x = [(own_x[k - 1], keys_ref.at[y, lax.rem(x - k + nx, nx), z], y_peers) for k in (1, 3, 2)]
    near_y = [
        (other_y[k], keys_ref.at[lax.rem(y - k + ny, ny), x, 1 - z], x_peers) for k in (0, 1, 3, 2)
    ]
    for copy, piece, peers in near_x[0:2] + near_y[0:3] + near_x[2:] + near_y[3:]:
        copy.wait_recv()
        for peer in peers:
            moves.append(push(slot, piece, piece, peer))
            slot += 1
    for copy in [own_here, pair_here] + stores:
        copy.wait()
    for copy in other_y + own_x:
        copy.wait_send()
    for copy in moves:
        copy.wait()


def split_two(value):
    high = value.astype(BF16)
    low = (value - high.astype(F32)).astype(BF16)
    return high, low


def spread_over(weight):
    m, c = weight.shape
    up = (
        lax.broadcasted_iota(jnp.int32, (m * GROUP, m), 0) // GROUP
        == lax.broadcasted_iota(jnp.int32, (m * GROUP, m), 1)
    ).astype(F32)
    across = (
        lax.broadcasted_iota(jnp.int32, (c, c * GROUP), 1) // GROUP
        == lax.broadcasted_iota(jnp.int32, (c, c * GROUP), 0)
    ).astype(F32)
    tall = jnp.dot(up, weight, precision=HIGHEST, preferred_element_type=F32)
    wide = jnp.dot(tall, across, precision=HIGHEST, preferred_element_type=F32)
    same = (
        lax.broadcasted_iota(jnp.int32, (m * GROUP, c * GROUP), 0) % GROUP
        == lax.broadcasted_iota(jnp.int32, (m * GROUP, c * GROUP), 1) % GROUP
    )
    return jnp.where(same, wide, 0.0)


def pair_weights(w1, b1, w2t, head_size, wfirst, wsecond):
    feats, hid = w1.shape
    root = math.sqrt(head_size)
    first = jnp.concatenate([w1, b1, jnp.zeros((8 - feats - 1, hid), F32)], axis=0)
    line = lax.dot_general(
        w2t, first, (((1,), (1,)), ((), ())), precision=HIGHEST, preferred_element_type=F32
    ) * (0.5 * root)
    part = feats * GROUP

    stacked = jnp.concatenate([first.T * (1.0 / GELU_S), line], axis=0)
    high, low = split_two(spread_over(stacked))
    wfirst[:, 0:part] = high[:, 0:part]
    wfirst[:, part : 2 * part] = high[:, 0:part]
    wfirst[:, 2 * part : 3 * part] = low[:, 0:part]
    wfirst[:, 3 * part : 3 * part + GROUP] = high[:, part : part + GROUP]
    wfirst[:, 3 * part + GROUP : 3 * part + 2 * GROUP] = low[:, part : part + GROUP]
    wsecond[...] = spread_over(w2t * (0.5 * root * GELU_S)).astype(BF16)


def attend_kernel(
    heads,
    pair_hbm,
    keys_hbm,
    wq_hbm,
    wk_hbm,
    wv_hbm,
    first_hbm,
    second_hbm,
    out_ref,
    level_ref,
    pair_ref,
    keys_ref,
    wq_ref,
    wk_ref,
    wv_ref,
    wfirst,
    wsecond,
    load_sem,
    kt_ref,
    v_ref,
    terms,
    q_terms,
    qm_ref,
    s_ref,
    top_ref,
    total_ref,
    acc_ref,
    fresh,
    hidden,
    linear,
    turned,
    weight_ref,
    held_ref,
    ranges,
    limits,
):
    loads = [
        pltpu.make_async_copy(src, dst, load_sem.at[i])
        for i, (src, dst) in enumerate(
            [
                (keys_hbm, keys_ref),
                (pair_hbm, pair_ref),
                (wk_hbm, wk_ref),
                (wv_hbm, wv_ref),
                (wq_hbm, wq_ref),
                (first_hbm, wfirst),
                (second_hbm, wsecond),
            ]
        )
    ]
    for load in loads:
        load.start()
    nz, slots, width = out_ref.shape
    ny, nx = keys_ref.shape[0:2]
    half = slots // nz
    own_rows = nz * slots
    head_size = width // heads
    hid = wsecond.shape[1] // GROUP
    root = math.sqrt(head_size)
    groups = UNIT // GROUP
    rows_g = heads * GROUP
    rows_u = groups * rows_g
    n_units = own_rows // UNIT
    n_tiles = nz * ny

    for load in loads:
        load.wait()

    def terms_of(mom, rap, azi, mass, ids):
        trans = jnp.sqrt(mom * mom + mass * mass)
        return (
            mom,
            rap,
            jnp.cos(azi),
            jnp.sin(azi),
            trans * jnp.exp(rap),
            trans * jnp.exp(-rap),
            mass * mass,
            ids,
        )

    ends = []
    for zz in range(nz):
        for yy in range(ny):
            end = keys_ref[yy, 0, zz, half : half + KIN_ROWS, :].astype(F32)
            for xx in range(1, nx):
                end = end + keys_ref[yy, xx, zz, half : half + KIN_ROWS, :].astype(F32)
            ends.append(end)
    raw_terms = [jnp.concatenate([end[i : i + 1] for end in ends], axis=0) for i in range(5)]
    ids = raw_terms[4]
    for i, term in enumerate(terms_of(*raw_terms)):
        for k in range(TILE // 128):
            terms[i, k] = term[:, k * 128 : (k + 1) * 128]
    ends = [pair_ref[zz, slots : slots + KIN_ROWS, 0:slots].astype(F32) for zz in range(nz)]
    raw_terms = [
        jnp.concatenate([ends[zz][i : i + 1] for zz in range(nz)], axis=0) for i in range(5)
    ]
    for i, term in enumerate(terms_of(*raw_terms)):
        for zz in range(nz):
            q_terms[i, zz * slots : (zz + 1) * slots, :] = jnp.broadcast_to(
                term[zz : zz + 1], (slots, slots)
            ).T

    counts = []
    for row in (0, UNIT - 1):
        bound = q_terms[7, pl.ds(row, n_units, stride=UNIT), :]
        count = jnp.zeros((n_units, 128), F32)
        for t in range(n_tiles):
            for k in range(TILE // 128):
                key = terms[7, k, t : t + 1, :]
                count = count + jnp.where(key < bound if row == 0 else key <= bound, 1.0, 0.0)
        counts.append(jnp.sum(count, axis=1, keepdims=True).astype(jnp.int32))
    start = jnp.minimum(counts[0] // TILE, n_tiles - 1)
    stop = jnp.maximum((counts[1] + (TILE - 1)) // TILE, start + 1)
    ranges[0] = jnp.broadcast_to(start, (n_units, 128))
    ranges[1] = jnp.broadcast_to(stop, (n_units, 128))
    to_scalars = pltpu.make_async_copy(ranges, limits, load_sem.at[7])
    to_scalars.start()

    wkt = wk_ref[...].astype(F32).T.astype(BF16)
    for yy in range(ny):
        for zz in range(nz):
            rows = jnp.concatenate(
                [keys_ref[yy, xx, zz, 0:half, :] for xx in range(nx)], axis=0
            )
            at = slice((zz * ny + yy) * TILE, (zz * ny + yy + 1) * TILE)
            kt_ref[:, at] = lax.dot_general(
                wkt, rows, (((1,), (1,)), ((), ())), preferred_element_type=F32
            ).astype(BF16)
            v_ref[at, :] = jnp.dot(rows, wv_ref[...], preferred_element_type=F32).astype(BF16)

    lane_head = lax.broadcasted_iota(jnp.int32, (GROUP, width), 1) // head_size
    for zz in range(nz):
        queries = jnp.dot(pair_ref[zz, 0:slots, :], wq_ref[...], preferred_element_type=F32)
        for base in range(0, slots, GROUP):
            rows = queries[base : base + GROUP]
            at = (zz * slots + base) * heads
            qm_ref[at : at + rows_g, :] = jnp.concatenate(
                [jnp.where(lane_head == h, rows, 0.0) for h in range(heads)], axis=0
            ).astype(BF16)

    top_ref[...] = jnp.full_like(top_ref, -1e30)
    total_ref[...] = jnp.zeros_like(total_ref)
    acc_ref[...] = jnp.zeros_like(acc_ref)

    to_scalars.wait()

    def following(u, t):
        more = t + 1 < limits[1, u, 0]
        then = jnp.where(more, u, jnp.minimum(u + 1, n_units - 1))
        return then, jnp.where(more, t + 1, limits[0, then, 0])

    steps = limits[1, 0, 0] - limits[0, 0, 0]
    for u in range(1, n_units):
        steps = steps + limits[1, u, 0] - limits[0, u, 0]

    def features(p, u, t):
        for g in range(groups):
            base = pl.multiple_of(u * UNIT + g * GROUP, GROUP)
            qt = [q_terms[i, pl.ds(base, GROUP), :] for i in range(7)]
            columns = []
            for i in range(TILE // 128):
                kt = [terms[j, i, pl.ds(t, 1), :] for j in range(7)]
                gap = qt[1] - kt[1]
                cos_gap = qt[2] * kt[2] + qt[3] * kt[3]
                dist = gap * gap + (2.0 - 2.0 * cos_gap)
                small = jnp.minimum(qt[0], kt[0])
                msq = (
                    qt[6]
                    + kt[6]
                    + (qt[4] * kt[5] + qt[5] * kt[4] - 2.0 * (qt[0] * kt[0] * cos_gap))
                )
                f = [
                    jnp.log(1.0 + dist),
                    jnp.log(1.0 + small * small * dist),
                    small / (qt[0] + kt[0]),
                    jnp.log(1.0 + msq),
                ]
                fh, fl = split_two(jnp.concatenate(f, axis=0))
                columns.append(
                    jnp.concatenate([fh, fl, fh, jnp.ones((2 * GROUP, 128), BF16)], axis=0)
                )
            fresh[p, g] = jnp.concatenate(columns, axis=1)

    def hiddens(p):
        for g in range(groups):
            z = jnp.dot(wfirst[...], fresh[p, g], preferred_element_type=F32)
            hidden[p, g] = z[0 : hid * GROUP].astype(BF16)
            linear[p, g] = z[hid * GROUP :]

    def gelus(p):
        for g in range(groups):
            inner = hidden[p, g]
            turned[p, g] = inner * jnp.tanh(inner * (ALPHA + inner * inner))

    def scores(p, u, t, away):
        start = pl.multiple_of(t * TILE, TILE)
        first_row = pl.multiple_of(u * rows_u, rows_u)
        products = jnp.dot(
            qm_ref[pl.ds(first_row, rows_u), :],
            kt_ref[:, pl.ds(start, TILE)],
            preferred_element_type=F32,
        )
        for g in range(groups):
            base = pl.multiple_of(u * UNIT + g * GROUP, GROUP)
            bias = jnp.dot(wsecond[...], turned[p, g], preferred_element_type=F32)
            s = products[g * rows_g : (g + 1) * rows_g] + (bias + linear[p, g])
            own = q_terms[7, pl.ds(base, GROUP), :] + away
            live = jnp.concatenate(
                [own == terms[7, i, pl.ds(t, 1), :] for i in range(TILE // 128)], axis=1
            )
            s = jnp.where(live[None], s.reshape(heads, GROUP, TILE), -1e30).reshape(rows_g, TILE)
            at = pl.ds(pl.multiple_of(first_row + g * rows_g, rows_g), rows_g)
            s_ref[at, pl.ds(start, TILE)] = s
            run_max = top_ref[at, :]
            for i in range(0, TILE, 128):
                run_max = jnp.maximum(run_max, s[:, i : i + 128])
            top_ref[at, :] = run_max

    def score_steps(i, carry):
        for k in range(SCORE_STEPS):
            p = k % 2
            u0, t0, u1, t1, u2, t2, u3, t3 = carry
            scores(1 - p, u3, t3, jnp.where(SCORE_STEPS * i + k >= 3, 0.0, 100.0))
            hiddens(1 - p)
            gelus(p)
            features(p, u0, t0)
            carry = (*following(u0, t0), u0, t0, u1, t1, u2, t2)
        return carry

    zero = jnp.int32(0)
    t_first = limits[0, 0, 0]
    lax.fori_loop(0, (steps + SCORE_STEPS + 2) // SCORE_STEPS, score_steps, (zero, t_first) * 4)

    for u in range(n_units):
        at = slice(u * rows_u, (u + 1) * rows_u)
        top_ref[at, :] = jnp.broadcast_to(
            jnp.max(top_ref[at, :], axis=1, keepdims=True), (rows_u, 128)
        )

    weight_ref[...] = jnp.zeros_like(weight_ref)

    def apply(p, u, t):
        at = pl.ds(pl.multiple_of(u * rows_u, rows_u), rows_u)
        acc_ref[at, :] += jnp.dot(
            weight_ref[p],
            v_ref[pl.ds(pl.multiple_of(t * TILE, TILE), TILE), :],
            preferred_element_type=F32,
        )

    def weigh(p, u, t, above):
        at = pl.ds(pl.multiple_of(u * rows_u, rows_u), rows_u)
        top = top_ref[at, :] + above
        total = total_ref[at, :]
        for i in range(0, TILE, 128):
            cols = pl.ds(pl.multiple_of(t * TILE + i, 128), 128)
            weight = jnp.exp2((s_ref[at, cols] - top) * (LOG2E / root))
            total = total + weight
            weight_ref[p, :, i : i + 128] = weight.astype(BF16)
        total_ref[at, :] = total

    def value_steps(i, carry):
        for k in range(VALUE_STEPS):
            u0, t0, u1, t1 = carry
            apply(1 - k % 2, u1, t1)
            weigh(k % 2, u0, t0, jnp.where(VALUE_STEPS * i + k < steps, 0.0, 1e32))
            carry = (*following(u0, t0), u0, t0)
        return carry

    lax.fori_loop(0, (steps + VALUE_STEPS) // VALUE_STEPS, value_steps, (zero, t_first) * 2)

    lane = lax.broadcasted_iota(jnp.int32, (rows_g, slots), 1)
    row = lax.rem(lax.broadcasted_iota(jnp.int32, (rows_g, slots), 0), GROUP)
    for zz in range(nz):
        level = jnp.zeros((rows_g, slots), F32)
        for base in range(0, slots, GROUP):
            at = (zz * slots + base) * heads
            total = jnp.sum(total_ref[at : at + rows_g, :], axis=1, keepdims=True)
            level = jnp.where(
                lane == base + row,
                top_ref[at : at + rows_g, :] * (LOG2E / root) + jnp.log(total) * LOG2E,
                level,
            )
            total = 1.0 / total
            out = jnp.zeros((GROUP, width), F32)
            for h in range(heads):
                rows = slice(at + h * GROUP, at + (h + 1) * GROUP)
                scaled = acc_ref[rows, :] * total[h * GROUP : (h + 1) * GROUP]
                out = jnp.where(lane_head == h, scaled, out)
            held_ref[base : base + GROUP, :] = out
        out_ref[zz] = held_ref[...].astype(BF16)
        level_ref[zz] = jnp.sum(level.reshape(heads, GROUP, slots), axis=1)


def finish_kernel(
    cube,
    part_ref,
    level_ref,
    wo_ref,
    gain_ref,
    out_ref,
    part_in,
    level_in,
    part_own,
    level_own,
    wo_own,
    gain_own,
    send_sem,
    recv_sem,
    load_sem,
):
    _, ny, nx = cube
    z, y, x = mesh_place(cube)
    near = {"blk": ((1 - z) * ny + y) * nx + x}
    heads = level_ref.shape[1]
    width = part_ref.shape[2]
    barrier = pltpu.get_barrier_semaphore()
    pl.semaphore_signal(barrier, inc=1, device_id=near, device_id_type=MESH)
    loads = [
        pltpu.make_async_copy(part_ref.at[z], part_own, load_sem.at[0]),
        pltpu.make_async_copy(level_ref.at[z], level_own, load_sem.at[1]),
        pltpu.make_async_copy(wo_ref, wo_own, load_sem.at[2]),
        pltpu.make_async_copy(gain_ref, gain_own, load_sem.at[3]),
    ]
    for load in loads:
        load.start()
    pl.semaphore_wait(barrier, 1)
    copies = [
        pltpu.make_async_remote_copy(
            src_ref=src,
            dst_ref=dst,
            send_sem=send_sem.at[i],
            recv_sem=recv_sem.at[i],
            device_id=near,
            device_id_type=MESH,
        )
        for i, (src, dst) in enumerate(
            [(part_ref.at[1 - z], part_in), (level_ref.at[1 - z], level_in)]
        )
    ]
    for copy in copies:
        copy.start()
    spread = (
        lax.broadcasted_iota(jnp.int32, (heads, width), 1) // (width // heads)
        == lax.broadcasted_iota(jnp.int32, (heads, width), 0)
    ).astype(F32)
    for copy in loads + copies:
        copy.wait()
    share = 1.0 / (1.0 + jnp.exp2(level_in[...] - level_own[...]))
    share = jnp.dot(share.T, spread, precision=HIGHEST, preferred_element_type=F32)
    theirs = part_in[...].astype(F32)
    attended = theirs + share * (part_own[...].astype(F32) - theirs)
    mixed = jnp.dot(attended.astype(BF16), wo_own[...], preferred_element_type=F32)
    out_ref[...] = layer_norm(mixed, gain_own[...]).astype(BF16)


def shards(
    n_grp,
    cube,
    raw,
    raw_kin,
    reader,
    event_id,
    pre_gain,
    w_query,
    w_key,
    w_value,
    w_out,
    post_gain,
    pair_w1,
    pair_b1,
    pair_w2,
):
    slots, width = raw.shape[2], raw.shape[3]
    heads = pair_w2.shape[1]
    nz, ny, nx = cube
    vmem = pl.BlockSpec(memory_space=pltpu.VMEM)
    free = pl.BlockSpec(memory_space=pl.ANY)
    dma = pltpu.SemaphoreType.DMA
    tall = slots + KIN_ROWS
    part_rows = slots // nz + KIN_ROWS
    feats, hid = pair_w1.shape
    mixing = (3 * feats + 2) * GROUP
    pair, keys, first, second = pl.pallas_call(
        functools.partial(exchange_kernel, n_grp, cube),
        out_shape=(
            jax.ShapeDtypeStruct((nz, tall, width), BF16),
            jax.ShapeDtypeStruct((ny, nx, nz, part_rows, width), BF16),
            jax.ShapeDtypeStruct(((hid + heads) * GROUP, mixing), BF16),
            jax.ShapeDtypeStruct((heads * GROUP, hid * GROUP), BF16),
        ),
        in_specs=[free] * 8,
        out_specs=(free,) * 4,
        scratch_shapes=[
            pltpu.VMEM(raw_kin.shape, BF16),
            pltpu.VMEM(reader.shape, jnp.int32),
            pltpu.VMEM(event_id.shape, jnp.int32),
            pltpu.VMEM((1, width), F32),
            pltpu.VMEM((feats, hid), F32),
            pltpu.VMEM((1, hid), F32),
            pltpu.VMEM((heads, hid), F32),
            pltpu.VMEM(((hid + heads) * GROUP, mixing), BF16),
            pltpu.VMEM((heads * GROUP, hid * GROUP), BF16),
            dma((8,)),
            pltpu.VMEM((n_grp, slots, width), BF16),
            pltpu.VMEM((n_grp, 8, slots), F32),
            pltpu.VMEM((n_grp, 8, slots), F32),
            pltpu.VMEM((tall, width), BF16),
            pltpu.VMEM((part_rows, width), BF16),
            pltpu.VMEM((part_rows, width), BF16),
            dma((n_grp,)),
            dma((n_grp,)),
            dma((n_grp,)),
            dma((n_grp,)),
            dma((32,)),
            dma((32,)),
            dma((2,)),
        ],
        compiler_params=pltpu.CompilerParams(collective_id=0, has_side_effects=True),
        name="exchange",
    )(
        raw,
        raw_kin,
        reader,
        event_id,
        pre_gain[None],
        pair_w1,
        pair_b1[None],
        pair_w2.T,
    )

    own_rows = nz * slots
    n_tiles = nz * ny
    groups = UNIT // GROUP
    rows_all = heads * own_rows
    part, level = pl.pallas_call(
        functools.partial(attend_kernel, heads),
        out_shape=(
            jax.ShapeDtypeStruct((nz, slots, width), BF16),
            jax.ShapeDtypeStruct((nz, heads, slots), F32),
        ),
        in_specs=[free] * 7,
        out_specs=(vmem, vmem),
        scratch_shapes=[
            pltpu.VMEM((nz, tall, width), BF16),
            pltpu.VMEM((ny, nx, nz, part_rows, width), BF16),
            pltpu.VMEM((width, width), BF16),
            pltpu.VMEM((width, width), BF16),
            pltpu.VMEM((width, width), BF16),
            pltpu.VMEM(((hid + heads) * GROUP, mixing), BF16),
            pltpu.VMEM((heads * GROUP, hid * GROUP), BF16),
            dma((8,)),
            pltpu.VMEM((width, n_tiles * TILE), BF16),
            pltpu.VMEM((n_tiles * TILE, width), BF16),
            pltpu.VMEM((8, TILE // 128, n_tiles, 128), F32),
            pltpu.VMEM((8, own_rows, slots), F32),
            pltpu.VMEM((rows_all, width), BF16),
            pltpu.VMEM((rows_all, n_tiles * TILE), F32),
            pltpu.VMEM((rows_all, 128), F32),
            pltpu.VMEM((rows_all, 128), F32),
            pltpu.VMEM((rows_all, width), F32),
            pltpu.VMEM((2, groups, mixing, TILE), BF16),
            pltpu.VMEM((2, groups, hid * GROUP, TILE), BF16),
            pltpu.VMEM((2, groups, heads * GROUP, TILE), F32),
            pltpu.VMEM((2, groups, hid * GROUP, TILE), BF16),
            pltpu.VMEM((2, heads * UNIT, TILE), BF16),
            pltpu.VMEM((slots, width), F32),
            pltpu.VMEM((2, own_rows // UNIT, 128), jnp.int32),
            pltpu.SMEM((2, own_rows // UNIT, 128), jnp.int32),
        ],
        compiler_params=pltpu.CompilerParams(vmem_limit_bytes=63 * 1024 * 1024),
        name="attend",
    )(pair, keys, w_query, w_key, w_value, first, second)

    encoded = pl.pallas_call(
        functools.partial(finish_kernel, cube),
        out_shape=jax.ShapeDtypeStruct((slots, width), BF16),
        in_specs=[free] * 4,
        out_specs=vmem,
        scratch_shapes=[
            pltpu.VMEM((slots, width), BF16),
            pltpu.VMEM((heads, slots), F32),
            pltpu.VMEM((slots, width), BF16),
            pltpu.VMEM((heads, slots), F32),
            pltpu.VMEM((width, width), BF16),
            pltpu.VMEM((1, width), F32),
            dma((2,)),
            dma((2,)),
            dma((4,)),
        ],
        compiler_params=pltpu.CompilerParams(collective_id=1, has_side_effects=True),
        name="finish",
    )(part, level, w_out, post_gain[None])
    return encoded[None]


def solution(mesh):
    in_specs = (
        P("grp", None, "blk", None),
        P("grp", None, None, "blk"),
        P("grp", "blk"),
        P("grp", "blk"),
        P(),
        P(),
        P(),
        P(),
        P(),
        P(),
        P(),
        P(),
        P(),
    )
    out_specs = P("grp", "blk", None)
    cube = (2, 4, mesh.shape["blk"] // 8)
    body = functools.partial(shards, mesh.shape["grp"], cube)
    return jax.shard_map(body, mesh=mesh, in_specs=in_specs, out_specs=out_specs, check_vma=False)
```

```python
import functools
import math

import jax
import jax.numpy as jnp
from jax import lax
from jax.experimental import pallas as pl
from jax.experimental.pallas import tpu as pltpu
from jax.sharding import PartitionSpec as P

MESH = pl.DeviceIdType.MESH
F32 = jnp.float32
BF16 = jnp.bfloat16
HIGHEST = lax.Precision.HIGHEST

KIN_ROWS = 16
GROUP = 8
UNIT = 16
TILE = 256
SCORE_STEPS = 6
VALUE_STEPS = 8

GELU_A = math.sqrt(2.0 / math.pi)
GELU_B = GELU_A * 0.044715
GELU_S = GELU_B ** (-1.0 / 3.0)
ALPHA = GELU_A * GELU_S
LOG2E = 1.0 / math.log(2.0)


def layer_norm(rows, gain):
    center = rows - jnp.mean(rows, axis=-1, keepdims=True)
    spread = jnp.mean(center * center, axis=-1, keepdims=True)
    return center * lax.rsqrt(spread + 1e-05) * gain


def mesh_place(cube):
    _, ny, nx = cube
    b = lax.axis_index("blk")
    return b // (ny * nx), lax.rem(b // nx, ny), lax.rem(b, nx)


def exchange_kernel(
    n_grp,
    cube,
    raw_ref,
    kin_hbm,
    reader_hbm,
    event_hbm,
    gain_hbm,
    w1_hbm,
    b1_hbm,
    w2t_hbm,
    pair_ref,
    keys_ref,
    first_hbm,
    second_hbm,
    kin_ref,
    reader_ref,
    event_ref,
    gain_ref,
    w1_ref,
    b1_ref,
    w2t_ref,
    wfirst,
    wsecond,
    load_sem,
    inbox,
    kin_send,
    kin_in,
    block,
    mine,
    theirs,
    got,
    send_sem,
    recv_sem,
    kin_send_sem,
    kin_recv_sem,
    link_send,
    link_recv,
    own_sem,
):
    nz, ny, nx = cube
    g = lax.axis_index("grp")
    z, y, x = mesh_place(cube)
    slots = raw_ref.shape[2]
    width = raw_ref.shape[3]
    half = slots // nz
    body = half * (width // 128)

    def blk(z, y, x):
        return {"blk": (z * ny + y) * nx + x}

    partners = [{"grp": lax.rem(g + k, n_grp)} for k in range(1, n_grp)]
    turns = (1, nx - 1, 2)
    x_peers = [blk(z, y, lax.rem(x + k, nx)) for k in turns]
    y_peers = [blk(z, lax.rem(y + k, ny), x) for k in turns]
    near = blk(1 - z, y, x)
    partners += [near] + x_peers + y_peers
    barrier = pltpu.get_barrier_semaphore()
    for partner in partners:
        pl.semaphore_signal(barrier, inc=1, device_id=partner, device_id_type=MESH)
    loads = [
        pltpu.make_async_copy(src, dst, load_sem.at[i])
        for i, (src, dst) in enumerate(
            [
                (kin_hbm, kin_ref),
                (reader_hbm, reader_ref),
                (event_hbm, event_ref),
                (gain_hbm, gain_ref),
                (w1_hbm, w1_ref),
                (b1_hbm, b1_ref),
                (w2t_hbm, w2t_ref),
                (raw_ref.at[0, g], inbox.at[0]),
            ]
        )
    ]
    for load in loads:
        load.start()
    loads[0].wait()
    kin_send[...] = jnp.zeros_like(kin_send)
    for k in range(n_grp):
        kin_send[k, 0:4, :] = kin_ref[0, k].astype(F32)
    pl.semaphore_wait(barrier, len(partners))

    copies = []
    for k in range(1, n_grp):
        to = lax.rem(g + k, n_grp)
        for src, dst, ssem, rsem in (
            (raw_ref.at[0, to], inbox.at[n_grp - k], send_sem, recv_sem),
            (kin_send.at[to], kin_in.at[n_grp - k], kin_send_sem, kin_recv_sem),
        ):
            copy = pltpu.make_async_remote_copy(
                src_ref=src,
                dst_ref=dst,
                send_sem=ssem.at[k],
                recv_sem=rsem.at[n_grp - k],
                device_id={"grp": to},
                device_id_type=MESH,
            )
            copy.start()
            copies.append(copy)

    for load in loads[1:]:
        load.wait()
    pair_weights(w1_ref[...], b1_ref[...], w2t_ref[...], width // w2t_ref.shape[0], wfirst, wsecond)
    wanted = lax.rem(reader_ref[...] - g + n_grp, n_grp)
    stores = [
        pltpu.make_async_copy(wfirst, first_hbm, load_sem.at[0]),
        pltpu.make_async_copy(wsecond, second_hbm, load_sem.at[1]),
    ]
    for store in stores:
        store.start()
    column = jnp.broadcast_to(wanted, (slots, slots)).T
    kin = jnp.where(wanted == 0, kin_send[g, 0:4, :], 0.0)
    sides = [
        jnp.where(column == 0, inbox[0][:, h : h + slots].astype(F32), 0.0)
        for h in range(0, width, slots)
    ]
    for copy in copies:
        copy.wait()
    for k in range(1, n_grp):
        kin = kin + jnp.where(wanted == k, kin_in[k, 0:4, :], 0.0)
        sides = [
            side
            + jnp.where(column == k, inbox[k][:, i * slots : (i + 1) * slots].astype(F32), 0.0)
            for i, side in enumerate(sides)
        ]
    tokens = jnp.concatenate(sides, axis=1)
    normed = layer_norm(tokens, gain_ref[...]).astype(BF16)
    block[0:slots, :] = normed
    tail = jnp.concatenate(
        [kin, event_ref[...].astype(F32), jnp.zeros((KIN_ROWS - 5, slots), F32)], axis=0
    )
    block[slots : slots + KIN_ROWS, :] = jnp.concatenate([tail, tail], axis=1).astype(BF16)
    for ref, low in ((mine, z == 0), (theirs, z == 1)):
        for i in range(width // 128):
            cols = slice(i * 128, (i + 1) * 128)
            ref[i * half : (i + 1) * half, :] = jnp.where(
                low, normed[0:half, cols], normed[half : 2 * half, cols]
            )
    theirs[body : body + KIN_ROWS, :] = tail.astype(BF16)

    def push(slot, src, dst, to):
        copy = pltpu.make_async_remote_copy(
            src_ref=src,
            dst_ref=dst,
            send_sem=link_send.at[slot],
            recv_sem=link_recv.at[slot],
            device_id=to,
            device_id_type=MESH,
        )
        copy.start()
        return copy

    rows = pl.ds(0, body)
    swap = push(0, theirs, got, near)
    own_x = [push(1 + i, mine, keys_ref.at[y, x, z, rows], to) for i, to in enumerate(x_peers)]
    moves = [push(4 + i, mine, keys_ref.at[y, x, z, rows], to) for i, to in enumerate(y_peers)]
    here = [
        pltpu.make_async_copy(mine, keys_ref.at[y, x, z, rows], own_sem.at[0]),
        pltpu.make_async_copy(block, pair_ref.at[z], own_sem.at[1]),
    ]
    for copy in here:
        copy.start()
    swap.wait_recv()
    ends = got[body : body + KIN_ROWS, :].astype(F32)
    ends = jnp.concatenate([ends[:, half:], ends[:, :half]], axis=1)
    side = lax.broadcasted_iota(jnp.int32, (KIN_ROWS, slots), 1) // half
    got[body : body + KIN_ROWS, :] = jnp.where(side == z, tail, ends).astype(BF16)
    other_y = [push(7 + i, got, keys_ref.at[y, x, 1 - z], to) for i, to in enumerate(y_peers)]
    moves += [push(10 + i, got, keys_ref.at[y, x, 1 - z], to) for i, to in enumerate(x_peers)]
    here.append(pltpu.make_async_copy(got, keys_ref.at[y, x, 1 - z], own_sem.at[2]))
    here[-1].start()
    moves.append(push(13, block, pair_ref.at[z], near))
    slot = 14
    for i, k in enumerate(turns):
        own_x[i].wait_recv()
        piece = keys_ref.at[y, lax.rem(x - k + nx, nx), z, rows]
        for to in y_peers:
            moves.append(push(slot, piece, piece, to))
            slot += 1
    for i, k in enumerate(turns):
        other_y[i].wait_recv()
        piece = keys_ref.at[lax.rem(y - k + ny, ny), x, 1 - z]
        for to in x_peers:
            moves.append(push(slot, piece, piece, to))
            slot += 1
    for copy in here + stores:
        copy.wait()
    for copy in [swap] + own_x + other_y:
        copy.wait_send()
    for copy in moves:
        copy.wait()


def split_two(value):
    high = value.astype(BF16)
    low = (value - high.astype(F32)).astype(BF16)
    return high, low


def spread_over(weight):
    m, c = weight.shape
    up = (
        lax.broadcasted_iota(jnp.int32, (m * GROUP, m), 0) // GROUP
        == lax.broadcasted_iota(jnp.int32, (m * GROUP, m), 1)
    ).astype(F32)
    across = (
        lax.broadcasted_iota(jnp.int32, (c, c * GROUP), 1) // GROUP
        == lax.broadcasted_iota(jnp.int32, (c, c * GROUP), 0)
    ).astype(F32)
    tall = jnp.dot(up, weight, precision=HIGHEST, preferred_element_type=F32)
    wide = jnp.dot(tall, across, precision=HIGHEST, preferred_element_type=F32)
    same = (
        lax.broadcasted_iota(jnp.int32, (m * GROUP, c * GROUP), 0) % GROUP
        == lax.broadcasted_iota(jnp.int32, (m * GROUP, c * GROUP), 1) % GROUP
    )
    return jnp.where(same, wide, 0.0)


def pair_weights(w1, b1, w2t, head_size, wfirst, wsecond):
    feats, hid = w1.shape
    root = math.sqrt(head_size)
    first = jnp.concatenate([w1, b1, jnp.zeros((8 - feats - 1, hid), F32)], axis=0)
    line = lax.dot_general(
        w2t, first, (((1,), (1,)), ((), ())), precision=HIGHEST, preferred_element_type=F32
    ) * (0.5 * root)
    part = feats * GROUP

    stacked = jnp.concatenate([first.T * (1.0 / GELU_S), line], axis=0)
    high, low = split_two(spread_over(stacked))
    wfirst[:, 0:part] = high[:, 0:part]
    wfirst[:, part : 2 * part] = high[:, 0:part]
    wfirst[:, 2 * part : 3 * part] = low[:, 0:part]
    wfirst[:, 3 * part : 3 * part + GROUP] = high[:, part : part + GROUP]
    wfirst[:, 3 * part + GROUP : 3 * part + 2 * GROUP] = low[:, part : part + GROUP]
    wsecond[...] = spread_over(w2t * (0.5 * root * GELU_S)).astype(BF16)


def attend_kernel(
    heads,
    pair_hbm,
    keys_hbm,
    wq_hbm,
    wk_hbm,
    wv_hbm,
    first_hbm,
    second_hbm,
    out_ref,
    level_ref,
    pair_ref,
    keys_ref,
    wq_ref,
    wk_ref,
    wv_ref,
    wfirst,
    wsecond,
    load_sem,
    kt_ref,
    v_ref,
    terms,
    q_terms,
    qm_ref,
    s_ref,
    top_ref,
    total_ref,
    acc_ref,
    fresh,
    hidden,
    linear,
    turned,
    weight_ref,
    held_ref,
    ranges,
    limits,
):
    loads = [
        pltpu.make_async_copy(src, dst, load_sem.at[i])
        for i, (src, dst) in enumerate(
            [
                (keys_hbm, keys_ref),
                (pair_hbm, pair_ref),
                (wk_hbm, wk_ref),
                (wv_hbm, wv_ref),
                (wq_hbm, wq_ref),
                (first_hbm, wfirst),
                (second_hbm, wsecond),
            ]
        )
    ]
    for load in loads:
        load.start()
    nz, slots, width = out_ref.shape
    ny, nx = keys_ref.shape[0:2]
    half = slots // nz
    own_rows = nz * slots
    head_size = width // heads
    hid = wsecond.shape[1] // GROUP
    root = math.sqrt(head_size)
    groups = UNIT // GROUP
    rows_g = heads * GROUP
    rows_u = groups * rows_g
    n_units = own_rows // UNIT
    n_tiles = nz * ny
    z = lax.axis_index("blk") // (ny * nx)

    for load in loads:
        load.wait()

    def terms_of(mom, rap, azi, mass, ids):
        trans = jnp.sqrt(mom * mom + mass * mass)
        return (
            mom,
            rap,
            jnp.cos(azi),
            jnp.sin(azi),
            trans * jnp.exp(rap),
            trans * jnp.exp(-rap),
            mass * mass,
            ids,
        )

    body = half * (width // 128)
    lower = lax.broadcasted_iota(jnp.int32, (KIN_ROWS, 128), 1) < half
    ends = [[] for _ in range(nz)]
    for yy in range(ny):
        tails = [
            keys_ref[yy, xx, 1 - z, body : body + KIN_ROWS, :].astype(F32) for xx in range(nx)
        ]
        turned_tails = [jnp.concatenate([e[:, half:], e[:, :half]], axis=1) for e in tails]
        ends[0].append(
            [jnp.where(lower, tails[k], turned_tails[k + 1]) for k in range(0, nx, 2)]
        )
        ends[1].append(
            [jnp.where(lower, turned_tails[k], tails[k + 1]) for k in range(0, nx, 2)]
        )
    ends = [jnp.concatenate(end, axis=1) for zz in range(nz) for end in ends[zz]]
    raw_terms = [jnp.concatenate([end[i : i + 1] for end in ends], axis=0) for i in range(5)]
    ids = raw_terms[4]
    for i, term in enumerate(terms_of(*raw_terms)):
        for k in range(TILE // 128):
            terms[i, k] = term[:, k * 128 : (k + 1) * 128]
    ends = [pair_ref[zz, slots : slots + KIN_ROWS, 0:slots].astype(F32) for zz in range(nz)]
    raw_terms = [
        jnp.concatenate([ends[zz][i : i + 1] for zz in range(nz)], axis=0) for i in range(5)
    ]
    for i, term in enumerate(terms_of(*raw_terms)):
        for zz in range(nz):
            q_terms[i, zz * slots : (zz + 1) * slots, :] = jnp.broadcast_to(
                term[zz : zz + 1], (slots, slots)
            ).T

    counts = []
    for row in (0, UNIT - 1):
        bound = q_terms[7, pl.ds(row, n_units, stride=UNIT), :]
        count = jnp.zeros((n_units, 128), F32)
        for t in range(n_tiles):
            for k in range(TILE // 128):
                key = terms[7, k, t : t + 1, :]
                count = count + jnp.where(key < bound if row == 0 else key <= bound, 1.0, 0.0)
        counts.append(jnp.sum(count, axis=1, keepdims=True).astype(jnp.int32))
    start = jnp.minimum(counts[0] // TILE, n_tiles - 1)
    stop = jnp.maximum((counts[1] + (TILE - 1)) // TILE, start + 1)
    ranges[0] = jnp.broadcast_to(start, (n_units, 128))
    ranges[1] = jnp.broadcast_to(stop, (n_units, 128))
    to_scalars = pltpu.make_async_copy(ranges, limits, load_sem.at[7])
    to_scalars.start()

    wkt = wk_ref[...].astype(F32).T.astype(BF16)
    for yy in range(ny):
        for zz in range(nz):
            rows = jnp.concatenate(
                [
                    jnp.concatenate(
                        [keys_ref[yy, xx, zz, i : i + half, :] for i in range(0, body, half)],
                        axis=1,
                    )
                    for xx in range(nx)
                ],
                axis=0,
            )
            at = slice((zz * ny + yy) * TILE, (zz * ny + yy + 1) * TILE)
            kt_ref[:, at] = lax.dot_general(
                wkt, rows, (((1,), (1,)), ((), ())), preferred_element_type=F32
            ).astype(BF16)
            v_ref[at, :] = jnp.dot(rows, wv_ref[...], preferred_element_type=F32).astype(BF16)

    lane_head = lax.broadcasted_iota(jnp.int32, (GROUP, width), 1) // head_size
    for zz in range(nz):
        queries = jnp.dot(pair_ref[zz, 0:slots, :], wq_ref[...], preferred_element_type=F32)
        for base in range(0, slots, GROUP):
            rows = queries[base : base + GROUP]
            at = (zz * slots + base) * heads
            qm_ref[at : at + rows_g, :] = jnp.concatenate(
                [jnp.where(lane_head == h, rows, 0.0) for h in range(heads)], axis=0
            ).astype(BF16)

    top_ref[...] = jnp.full_like(top_ref, -1e30)
    total_ref[...] = jnp.zeros_like(total_ref)
    acc_ref[...] = jnp.zeros_like(acc_ref)

    to_scalars.wait()

    def following(u, t):
        more = t + 1 < limits[1, u, 0]
        then = jnp.where(more, u, jnp.minimum(u + 1, n_units - 1))
        return then, jnp.where(more, t + 1, limits[0, then, 0])

    steps = limits[1, 0, 0] - limits[0, 0, 0]
    for u in range(1, n_units):
        steps = steps + limits[1, u, 0] - limits[0, u, 0]

    def features(p, u, t):
        for g in range(groups):
            base = pl.multiple_of(u * UNIT + g * GROUP, GROUP)
            qt = [q_terms[i, pl.ds(base, GROUP), :] for i in range(7)]
            columns = []
            for i in range(TILE // 128):
                kt = [terms[j, i, pl.ds(t, 1), :] for j in range(7)]
                gap = qt[1] - kt[1]
                cos_gap = qt[2] * kt[2] + qt[3] * kt[3]
                dist = gap * gap + (2.0 - 2.0 * cos_gap)
                small = jnp.minimum(qt[0], kt[0])
                msq = (
                    qt[6]
                    + kt[6]
                    + (qt[4] * kt[5] + qt[5] * kt[4] - 2.0 * (qt[0] * kt[0] * cos_gap))
                )
                f = [
                    jnp.log(1.0 + dist),
                    jnp.log(1.0 + small * small * dist),
                    small / (qt[0] + kt[0]),
                    jnp.log(1.0 + msq),
                ]
                fh, fl = split_two(jnp.concatenate(f, axis=0))
                columns.append(
                    jnp.concatenate([fh, fl, fh, jnp.ones((2 * GROUP, 128), BF16)], axis=0)
                )
            fresh[p, g] = jnp.concatenate(columns, axis=1)

    def hiddens(p):
        for g in range(groups):
            z = jnp.dot(wfirst[...], fresh[p, g], preferred_element_type=F32)
            hidden[p, g] = z[0 : hid * GROUP].astype(BF16)
            linear[p, g] = z[hid * GROUP :]

    def gelus(p):
        for g in range(groups):
            inner = hidden[p, g]
            turned[p, g] = inner * jnp.tanh(inner * (ALPHA + inner * inner))

    def scores(p, u, t, away):
        start = pl.multiple_of(t * TILE, TILE)
        first_row = pl.multiple_of(u * rows_u, rows_u)
        products = jnp.dot(
            qm_ref[pl.ds(first_row, rows_u), :],
            kt_ref[:, pl.ds(start, TILE)],
            preferred_element_type=F32,
        )
        for g in range(groups):
            base = pl.multiple_of(u * UNIT + g * GROUP, GROUP)
            bias = jnp.dot(wsecond[...], turned[p, g], preferred_element_type=F32)
            s = products[g * rows_g : (g + 1) * rows_g] + (bias + linear[p, g])
            own = q_terms[7, pl.ds(base, GROUP), :] + away
            live = jnp.concatenate(
                [own == terms[7, i, pl.ds(t, 1), :] for i in range(TILE // 128)], axis=1
            )
            s = jnp.where(live[None], s.reshape(heads, GROUP, TILE), -1e30).reshape(rows_g, TILE)
            at = pl.ds(pl.multiple_of(first_row + g * rows_g, rows_g), rows_g)
            s_ref[at, pl.ds(start, TILE)] = s
            run_max = top_ref[at, :]
            for i in range(0, TILE, 128):
                run_max = jnp.maximum(run_max, s[:, i : i + 128])
            top_ref[at, :] = run_max

    def score_steps(i, carry):
        for k in range(SCORE_STEPS):
            p = k % 2
            u0, t0, u1, t1, u2, t2, u3, t3 = carry
            scores(1 - p, u3, t3, jnp.where(SCORE_STEPS * i + k >= 3, 0.0, 100.0))
            hiddens(1 - p)
            gelus(p)
            features(p, u0, t0)
            carry = (*following(u0, t0), u0, t0, u1, t1, u2, t2)
        return carry

    zero = jnp.int32(0)
    t_first = limits[0, 0, 0]
    lax.fori_loop(0, (steps + SCORE_STEPS + 2) // SCORE_STEPS, score_steps, (zero, t_first) * 4)

    for u in range(n_units):
        at = slice(u * rows_u, (u + 1) * rows_u)
        top_ref[at, :] = jnp.broadcast_to(
            jnp.max(top_ref[at, :], axis=1, keepdims=True), (rows_u, 128)
        )

    weight_ref[...] = jnp.zeros_like(weight_ref)

    def apply(p, u, t):
        at = pl.ds(pl.multiple_of(u * rows_u, rows_u), rows_u)
        acc_ref[at, :] += jnp.dot(
            weight_ref[p],
            v_ref[pl.ds(pl.multiple_of(t * TILE, TILE), TILE), :],
            preferred_element_type=F32,
        )

    def weigh(p, u, t, above):
        at = pl.ds(pl.multiple_of(u * rows_u, rows_u), rows_u)
        top = top_ref[at, :] + above
        total = total_ref[at, :]
        for i in range(0, TILE, 128):
            cols = pl.ds(pl.multiple_of(t * TILE + i, 128), 128)
            weight = jnp.exp2((s_ref[at, cols] - top) * (LOG2E / root))
            total = total + weight
            weight_ref[p, :, i : i + 128] = weight.astype(BF16)
        total_ref[at, :] = total

    def value_steps(i, carry):
        for k in range(VALUE_STEPS):
            u0, t0, u1, t1 = carry
            apply(1 - k % 2, u1, t1)
            weigh(k % 2, u0, t0, jnp.where(VALUE_STEPS * i + k < steps, 0.0, 1e32))
            carry = (*following(u0, t0), u0, t0)
        return carry

    lax.fori_loop(0, (steps + VALUE_STEPS) // VALUE_STEPS, value_steps, (zero, t_first) * 2)

    lane = lax.broadcasted_iota(jnp.int32, (rows_g, slots), 1)
    row = lax.rem(lax.broadcasted_iota(jnp.int32, (rows_g, slots), 0), GROUP)
    for zz in range(nz):
        level = jnp.zeros((rows_g, slots), F32)
        for base in range(0, slots, GROUP):
            at = (zz * slots + base) * heads
            total = jnp.sum(total_ref[at : at + rows_g, :], axis=1, keepdims=True)
            level = jnp.where(
                lane == base + row,
                top_ref[at : at + rows_g, :] * (LOG2E / root) + jnp.log(total) * LOG2E,
                level,
            )
            total = 1.0 / total
            out = jnp.zeros((GROUP, width), F32)
            for h in range(heads):
                rows = slice(at + h * GROUP, at + (h + 1) * GROUP)
                scaled = acc_ref[rows, :] * total[h * GROUP : (h + 1) * GROUP]
                out = jnp.where(lane_head == h, scaled, out)
            held_ref[base : base + GROUP, :] = out
        out_ref[zz] = held_ref[...].astype(BF16)
        level_ref[zz] = jnp.sum(level.reshape(heads, GROUP, slots), axis=1)


def finish_kernel(
    cube,
    part_ref,
    level_ref,
    wo_ref,
    gain_ref,
    out_ref,
    part_in,
    level_in,
    part_own,
    level_own,
    wo_own,
    gain_own,
    send_sem,
    recv_sem,
    load_sem,
):
    _, ny, nx = cube
    z, y, x = mesh_place(cube)
    near = {"blk": ((1 - z) * ny + y) * nx + x}
    heads = level_ref.shape[1]
    width = part_ref.shape[2]
    barrier = pltpu.get_barrier_semaphore()
    pl.semaphore_signal(barrier, inc=1, device_id=near, device_id_type=MESH)
    loads = [
        pltpu.make_async_copy(part_ref.at[z], part_own, load_sem.at[0]),
        pltpu.make_async_copy(level_ref.at[z], level_own, load_sem.at[1]),
        pltpu.make_async_copy(wo_ref, wo_own, load_sem.at[2]),
        pltpu.make_async_copy(gain_ref, gain_own, load_sem.at[3]),
    ]
    for load in loads:
        load.start()
    pl.semaphore_wait(barrier, 1)
    copies = [
        pltpu.make_async_remote_copy(
            src_ref=src,
            dst_ref=dst,
            send_sem=send_sem.at[i],
            recv_sem=recv_sem.at[i],
            device_id=near,
            device_id_type=MESH,
        )
        for i, (src, dst) in enumerate(
            [(part_ref.at[1 - z], part_in), (level_ref.at[1 - z], level_in)]
        )
    ]
    for copy in copies:
        copy.start()
    spread = (
        lax.broadcasted_iota(jnp.int32, (heads, width), 1) // (width // heads)
        == lax.broadcasted_iota(jnp.int32, (heads, width), 0)
    ).astype(F32)
    for copy in loads + copies:
        copy.wait()
    share = 1.0 / (1.0 + jnp.exp2(level_in[...] - level_own[...]))
    share = jnp.dot(share.T, spread, precision=HIGHEST, preferred_element_type=F32)
    theirs = part_in[...].astype(F32)
    attended = theirs + share * (part_own[...].astype(F32) - theirs)
    mixed = jnp.dot(attended.astype(BF16), wo_own[...], preferred_element_type=F32)
    out_ref[...] = layer_norm(mixed, gain_own[...]).astype(BF16)


def shards(
    n_grp,
    cube,
    raw,
    raw_kin,
    reader,
    event_id,
    pre_gain,
    w_query,
    w_key,
    w_value,
    w_out,
    post_gain,
    pair_w1,
    pair_b1,
    pair_w2,
):
    slots, width = raw.shape[2], raw.shape[3]
    heads = pair_w2.shape[1]
    nz, ny, nx = cube
    vmem = pl.BlockSpec(memory_space=pltpu.VMEM)
    free = pl.BlockSpec(memory_space=pl.ANY)
    dma = pltpu.SemaphoreType.DMA
    tall = slots + KIN_ROWS
    part_rows = slots // nz * (width // 128) + KIN_ROWS
    feats, hid = pair_w1.shape
    mixing = (3 * feats + 2) * GROUP
    pair, keys, first, second = pl.pallas_call(
        functools.partial(exchange_kernel, n_grp, cube),
        out_shape=(
            jax.ShapeDtypeStruct((nz, tall, width), BF16),
            jax.ShapeDtypeStruct((ny, nx, nz, part_rows, 128), BF16),
            jax.ShapeDtypeStruct(((hid + heads) * GROUP, mixing), BF16),
            jax.ShapeDtypeStruct((heads * GROUP, hid * GROUP), BF16),
        ),
        in_specs=[free] * 8,
        out_specs=(free,) * 4,
        scratch_shapes=[
            pltpu.VMEM(raw_kin.shape, BF16),
            pltpu.VMEM(reader.shape, jnp.int32),
            pltpu.VMEM(event_id.shape, jnp.int32),
            pltpu.VMEM((1, width), F32),
            pltpu.VMEM((feats, hid), F32),
            pltpu.VMEM((1, hid), F32),
            pltpu.VMEM((heads, hid), F32),
            pltpu.VMEM(((hid + heads) * GROUP, mixing), BF16),
            pltpu.VMEM((heads * GROUP, hid * GROUP), BF16),
            dma((8,)),
            pltpu.VMEM((n_grp, slots, width), BF16),
            pltpu.VMEM((n_grp, 8, slots), F32),
            pltpu.VMEM((n_grp, 8, slots), F32),
            pltpu.VMEM((tall, width), BF16),
            pltpu.VMEM((part_rows - KIN_ROWS, 128), BF16),
            pltpu.VMEM((part_rows, 128), BF16),
            pltpu.VMEM((part_rows, 128), BF16),
            dma((n_grp,)),
            dma((n_grp,)),
            dma((n_grp,)),
            dma((n_grp,)),
            dma((32,)),
            dma((32,)),
            dma((3,)),
        ],
        compiler_params=pltpu.CompilerParams(collective_id=0, has_side_effects=True),
        name="exchange",
    )(
        raw,
        raw_kin,
        reader,
        event_id,
        pre_gain[None],
        pair_w1,
        pair_b1[None],
        pair_w2.T,
    )

    own_rows = nz * slots
    n_tiles = nz * ny
    groups = UNIT // GROUP
    rows_all = heads * own_rows
    part, level = pl.pallas_call(
        functools.partial(attend_kernel, heads),
        out_shape=(
            jax.ShapeDtypeStruct((nz, slots, width), BF16),
            jax.ShapeDtypeStruct((nz, heads, slots), F32),
        ),
        in_specs=[free] * 7,
        out_specs=(vmem, vmem),
        scratch_shapes=[
            pltpu.VMEM((nz, tall, width), BF16),
            pltpu.VMEM((ny, nx, nz, part_rows, 128), BF16),
            pltpu.VMEM((width, width), BF16),
            pltpu.VMEM((width, width), BF16),
            pltpu.VMEM((width, width), BF16),
            pltpu.VMEM(((hid + heads) * GROUP, mixing), BF16),
            pltpu.VMEM((heads * GROUP, hid * GROUP), BF16),
            dma((8,)),
            pltpu.VMEM((width, n_tiles * TILE), BF16),
            pltpu.VMEM((n_tiles * TILE, width), BF16),
            pltpu.VMEM((8, TILE // 128, n_tiles, 128), F32),
            pltpu.VMEM((8, own_rows, slots), F32),
            pltpu.VMEM((rows_all, width), BF16),
            pltpu.VMEM((rows_all, n_tiles * TILE), F32),
            pltpu.VMEM((rows_all, 128), F32),
            pltpu.VMEM((rows_all, 128), F32),
            pltpu.VMEM((rows_all, width), F32),
            pltpu.VMEM((2, groups, mixing, TILE), BF16),
            pltpu.VMEM((2, groups, hid * GROUP, TILE), BF16),
            pltpu.VMEM((2, groups, heads * GROUP, TILE), F32),
            pltpu.VMEM((2, groups, hid * GROUP, TILE), BF16),
            pltpu.VMEM((2, heads * UNIT, TILE), BF16),
            pltpu.VMEM((slots, width), F32),
            pltpu.VMEM((2, own_rows // UNIT, 128), jnp.int32),
            pltpu.SMEM((2, own_rows // UNIT, 128), jnp.int32),
        ],
        compiler_params=pltpu.CompilerParams(vmem_limit_bytes=63 * 1024 * 1024),
        name="attend",
    )(pair, keys, w_query, w_key, w_value, first, second)

    encoded = pl.pallas_call(
        functools.partial(finish_kernel, cube),
        out_shape=jax.ShapeDtypeStruct((slots, width), BF16),
        in_specs=[free] * 4,
        out_specs=vmem,
        scratch_shapes=[
            pltpu.VMEM((slots, width), BF16),
            pltpu.VMEM((heads, slots), F32),
            pltpu.VMEM((slots, width), BF16),
            pltpu.VMEM((heads, slots), F32),
            pltpu.VMEM((width, width), BF16),
            pltpu.VMEM((1, width), F32),
            dma((2,)),
            dma((2,)),
            dma((4,)),
        ],
        compiler_params=pltpu.CompilerParams(collective_id=1, has_side_effects=True),
        name="finish",
    )(part, level, w_out, post_gain[None])
    return encoded[None]


def solution(mesh):
    in_specs = (
        P("grp", None, "blk", None),
        P("grp", None, None, "blk"),
        P("grp", "blk"),
        P("grp", "blk"),
        P(),
        P(),
        P(),
        P(),
        P(),
        P(),
        P(),
        P(),
        P(),
    )
    out_specs = P("grp", "blk", None)
    cube = (2, 4, mesh.shape["blk"] // 8)
    body = functools.partial(shards, mesh.shape["grp"], cube)
    return jax.shard_map(body, mesh=mesh, in_specs=in_specs, out_specs=out_specs, check_vma=False)
```

```python
import functools
import math

import jax
import jax.numpy as jnp
from jax import lax
from jax.experimental import pallas as pl
from jax.experimental.pallas import tpu as pltpu
from jax.sharding import PartitionSpec as P

MESH = pl.DeviceIdType.MESH
F32 = jnp.float32
BF16 = jnp.bfloat16
HIGHEST = lax.Precision.HIGHEST

KIN_ROWS = 16
GROUP = 8
UNIT = 16
TILE = 256
LANES = 128
SCORE_STEPS = 6
VALUE_STEPS = 8

GELU_A = math.sqrt(2.0 / math.pi)
GELU_B = GELU_A * 0.044715
GELU_S = GELU_B ** (-1.0 / 3.0)
ALPHA = GELU_A * GELU_S
LOG2E = 1.0 / math.log(2.0)


def layer_norm(rows, gain):
    center = rows - jnp.mean(rows, axis=-1, keepdims=True)
    spread = jnp.mean(center * center, axis=-1, keepdims=True)
    return center * lax.rsqrt(spread + 1e-05) * gain


def mesh_place(cube):
    _, ny, nx = cube
    b = lax.axis_index("blk")
    return b // (ny * nx), lax.rem(b // nx, ny), lax.rem(b, nx)


def exchange_kernel(
    n_grp,
    cube,
    raw_ref,
    kin_hbm,
    reader_hbm,
    event_hbm,
    gain_hbm,
    w1_hbm,
    b1_hbm,
    w2t_hbm,
    pair_ref,
    keys_ref,
    first_hbm,
    second_hbm,
    kin_ref,
    reader_ref,
    event_ref,
    gain_ref,
    w1_ref,
    b1_ref,
    w2t_ref,
    wfirst,
    wsecond,
    load_sem,
    inbox,
    kin_send,
    kin_in,
    block,
    mine,
    theirs,
    got,
    send_sem,
    recv_sem,
    kin_send_sem,
    kin_recv_sem,
    link_send,
    link_recv,
    own_sem,
):
    nz, ny, nx = cube
    g = lax.axis_index("grp")
    z, y, x = mesh_place(cube)
    slots = raw_ref.shape[2]
    width = raw_ref.shape[3]
    half = slots // nz
    body = half * (width // 128)

    def blk(z, y, x):
        return {"blk": (z * ny + y) * nx + x}

    partners = [{"grp": lax.rem(g + k, n_grp)} for k in range(1, n_grp)]
    turns = (1, nx - 1, 2)
    x_peers = [blk(z, y, lax.rem(x + k, nx)) for k in turns]
    y_peers = [blk(z, lax.rem(y + k, ny), x) for k in turns]
    near = blk(1 - z, y, x)
    partners += [near] + x_peers + y_peers
    barrier = pltpu.get_barrier_semaphore()
    for partner in partners:
        pl.semaphore_signal(barrier, inc=1, device_id=partner, device_id_type=MESH)
    loads = [
        pltpu.make_async_copy(src, dst, load_sem.at[i])
        for i, (src, dst) in enumerate(
            [
                (kin_hbm, kin_ref),
                (reader_hbm, reader_ref),
                (event_hbm, event_ref),
                (gain_hbm, gain_ref),
                (w1_hbm, w1_ref),
                (b1_hbm, b1_ref),
                (w2t_hbm, w2t_ref),
                (raw_ref.at[0, g], inbox.at[0]),
            ]
        )
    ]
    for load in loads:
        load.start()
    loads[0].wait()
    kin_send[...] = jnp.zeros_like(kin_send)
    for k in range(n_grp):
        kin_send[k, 0:4, :] = kin_ref[0, k].astype(F32)
    pl.semaphore_wait(barrier, len(partners))

    copies = []
    for k in range(1, n_grp):
        to = lax.rem(g + k, n_grp)
        for src, dst, ssem, rsem in (
            (raw_ref.at[0, to], inbox.at[n_grp - k], send_sem, recv_sem),
            (kin_send.at[to], kin_in.at[n_grp - k], kin_send_sem, kin_recv_sem),
        ):
            copy = pltpu.make_async_remote_copy(
                src_ref=src,
                dst_ref=dst,
                send_sem=ssem.at[k],
                recv_sem=rsem.at[n_grp - k],
                device_id={"grp": to},
                device_id_type=MESH,
            )
            copy.start()
            copies.append(copy)

    for load in loads[1:]:
        load.wait()
    pair_weights(w1_ref[...], b1_ref[...], w2t_ref[...], width // w2t_ref.shape[0], wfirst, wsecond)
    wanted = lax.rem(reader_ref[...] - g + n_grp, n_grp)
    stores = [
        pltpu.make_async_copy(wfirst, first_hbm, load_sem.at[0]),
        pltpu.make_async_copy(wsecond, second_hbm, load_sem.at[1]),
    ]
    for store in stores:
        store.start()
    column = jnp.broadcast_to(wanted, (slots, slots)).T
    kin = jnp.where(wanted == 0, kin_send[g, 0:4, :], 0.0)
    sides = [
        jnp.where(column == 0, inbox[0][:, h : h + slots].astype(F32), 0.0)
        for h in range(0, width, slots)
    ]
    for copy in copies:
        copy.wait()
    for k in range(1, n_grp):
        kin = kin + jnp.where(wanted == k, kin_in[k, 0:4, :], 0.0)
        sides = [
            side
            + jnp.where(column == k, inbox[k][:, i * slots : (i + 1) * slots].astype(F32), 0.0)
            for i, side in enumerate(sides)
        ]
    tokens = jnp.concatenate(sides, axis=1)
    normed = layer_norm(tokens, gain_ref[...]).astype(BF16)
    block[0:slots, :] = normed
    tail = jnp.concatenate(
        [kin, event_ref[...].astype(F32), jnp.zeros((KIN_ROWS - 5, slots), F32)], axis=0
    )
    block[slots : slots + KIN_ROWS, :] = jnp.concatenate([tail, tail], axis=1).astype(BF16)
    for ref, low in ((mine, z == 0), (theirs, z == 1)):
        for i in range(width // 128):
            cols = slice(i * 128, (i + 1) * 128)
            ref[i * half : (i + 1) * half, :] = jnp.where(
                low, normed[0:half, cols], normed[half : 2 * half, cols]
            )
    theirs[body : body + KIN_ROWS, :] = tail.astype(BF16)

    def push(slot, src, dst, to):
        copy = pltpu.make_async_remote_copy(
            src_ref=src,
            dst_ref=dst,
            send_sem=link_send.at[slot],
            recv_sem=link_recv.at[slot],
            device_id=to,
            device_id_type=MESH,
        )
        copy.start()
        return copy

    rows = pl.ds(0, body)
    swap = push(0, theirs, got, near)
    own_x = [push(1 + i, mine, keys_ref.at[y, x, z, rows], to) for i, to in enumerate(x_peers)]
    moves = [push(4 + i, mine, keys_ref.at[y, x, z, rows], to) for i, to in enumerate(y_peers)]
    here = [
        pltpu.make_async_copy(mine, keys_ref.at[y, x, z, rows], own_sem.at[0]),
        pltpu.make_async_copy(block, pair_ref.at[z], own_sem.at[1]),
    ]
    for copy in here:
        copy.start()
    swap.wait_recv()
    ends = got[body : body + KIN_ROWS, :].astype(F32)
    ends = jnp.concatenate([ends[:, half:], ends[:, :half]], axis=1)
    side = lax.broadcasted_iota(jnp.int32, (KIN_ROWS, slots), 1) // half
    got[body : body + KIN_ROWS, :] = jnp.where(side == z, tail, ends).astype(BF16)
    other_y = [push(7 + i, got, keys_ref.at[y, x, 1 - z], to) for i, to in enumerate(y_peers)]
    moves += [push(10 + i, got, keys_ref.at[y, x, 1 - z], to) for i, to in enumerate(x_peers)]
    here.append(pltpu.make_async_copy(got, keys_ref.at[y, x, 1 - z], own_sem.at[2]))
    here[-1].start()
    moves.append(push(13, block, pair_ref.at[z], near))
    slot = 14
    for i, k in enumerate(turns):
        own_x[i].wait_recv()
        piece = keys_ref.at[y, lax.rem(x - k + nx, nx), z, rows]
        for to in y_peers:
            moves.append(push(slot, piece, piece, to))
            slot += 1
    for i, k in enumerate(turns):
        other_y[i].wait_recv()
        piece = keys_ref.at[lax.rem(y - k + ny, ny), x, 1 - z]
        for to in x_peers:
            moves.append(push(slot, piece, piece, to))
            slot += 1
    for copy in here + stores:
        copy.wait()
    for copy in [swap] + own_x + other_y:
        copy.wait_send()
    for copy in moves:
        copy.wait()


def split_two(value):
    high = value.astype(BF16)
    low = (value - high.astype(F32)).astype(BF16)
    return high, low


def spread_over(weight):
    m, c = weight.shape
    up = (
        lax.broadcasted_iota(jnp.int32, (m * GROUP, m), 0) // GROUP
        == lax.broadcasted_iota(jnp.int32, (m * GROUP, m), 1)
    ).astype(F32)
    across = (
        lax.broadcasted_iota(jnp.int32, (c, c * GROUP), 1) // GROUP
        == lax.broadcasted_iota(jnp.int32, (c, c * GROUP), 0)
    ).astype(F32)
    tall = jnp.dot(up, weight, precision=HIGHEST, preferred_element_type=F32)
    wide = jnp.dot(tall, across, precision=HIGHEST, preferred_element_type=F32)
    same = (
        lax.broadcasted_iota(jnp.int32, (m * GROUP, c * GROUP), 0) % GROUP
        == lax.broadcasted_iota(jnp.int32, (m * GROUP, c * GROUP), 1) % GROUP
    )
    return jnp.where(same, wide, 0.0)


def pair_weights(w1, b1, w2t, head_size, wfirst, wsecond):
    feats, hid = w1.shape
    root = math.sqrt(head_size)
    first = jnp.concatenate([w1, b1, jnp.zeros((8 - feats - 1, hid), F32)], axis=0)
    line = lax.dot_general(
        w2t, first, (((1,), (1,)), ((), ())), precision=HIGHEST, preferred_element_type=F32
    ) * (0.5 * root)
    part = feats * GROUP

    stacked = jnp.concatenate([first.T * (1.0 / GELU_S), line], axis=0)
    high, low = split_two(spread_over(stacked))
    wfirst[:, 0:part] = high[:, 0:part]
    wfirst[:, part : 2 * part] = high[:, 0:part]
    wfirst[:, 2 * part : 3 * part] = low[:, 0:part]
    wfirst[:, 3 * part : 3 * part + GROUP] = high[:, part : part + GROUP]
    wfirst[:, 3 * part + GROUP : 3 * part + 2 * GROUP] = low[:, part : part + GROUP]
    wsecond[...] = spread_over(w2t * (0.5 * root * GELU_S)).astype(BF16)


def attend_kernel(
    heads,
    pair_hbm,
    keys_hbm,
    wq_hbm,
    wk_hbm,
    wv_hbm,
    first_hbm,
    second_hbm,
    out_ref,
    level_ref,
    pair_ref,
    keys_ref,
    wq_ref,
    wk_ref,
    wv_ref,
    wfirst,
    wsecond,
    load_sem,
    kt_ref,
    v_ref,
    terms,
    q_terms,
    qm_ref,
    s_ref,
    top_ref,
    total_ref,
    acc_ref,
    fresh,
    hidden,
    linear,
    turned,
    weight_ref,
    held_ref,
    ranges,
    limits,
):
    loads = [
        pltpu.make_async_copy(src, dst, load_sem.at[i])
        for i, (src, dst) in enumerate(
            [
                (keys_hbm, keys_ref),
                (pair_hbm, pair_ref),
                (wk_hbm, wk_ref),
                (wv_hbm, wv_ref),
                (wq_hbm, wq_ref),
                (first_hbm, wfirst),
                (second_hbm, wsecond),
            ]
        )
    ]
    for load in loads:
        load.start()
    nz, slots, width = out_ref.shape
    ny, nx = keys_ref.shape[0:2]
    half = slots // nz
    own_rows = nz * slots
    head_size = width // heads
    hid = wsecond.shape[1] // GROUP
    root = math.sqrt(head_size)
    groups = UNIT // GROUP
    rows_g = heads * GROUP
    rows_u = groups * rows_g
    n_units = own_rows // UNIT
    n_tiles = nz * ny
    per_step = TILE // LANES
    z = lax.axis_index("blk") // (ny * nx)

    for load in loads:
        load.wait()

    def terms_of(mom, rap, azi, mass, ids):
        trans = jnp.sqrt(mom * mom + mass * mass)
        return (
            mom,
            rap,
            jnp.cos(azi),
            jnp.sin(azi),
            trans * jnp.exp(rap),
            trans * jnp.exp(-rap),
            mass * mass,
            ids,
        )

    body = half * (width // 128)
    lower = lax.broadcasted_iota(jnp.int32, (KIN_ROWS, 128), 1) < half
    ends = [[] for _ in range(nz)]
    for yy in range(ny):
        tails = [
            keys_ref[yy, xx, 1 - z, body : body + KIN_ROWS, :].astype(F32) for xx in range(nx)
        ]
        turned_tails = [jnp.concatenate([e[:, half:], e[:, :half]], axis=1) for e in tails]
        ends[0].append(
            [jnp.where(lower, tails[k], turned_tails[k + 1]) for k in range(0, nx, 2)]
        )
        ends[1].append(
            [jnp.where(lower, turned_tails[k], tails[k + 1]) for k in range(0, nx, 2)]
        )
    ends = [jnp.concatenate(end, axis=1) for zz in range(nz) for end in ends[zz]]
    raw_terms = [jnp.concatenate([end[i : i + 1] for end in ends], axis=0) for i in range(5)]
    n_rows = n_tiles * TILE // LANES
    raw_terms = [
        jnp.concatenate(
            [
                term[t : t + 1, k : k + LANES]
                for t in range(n_tiles)
                for k in range(0, TILE, LANES)
            ],
            axis=0,
        )
        for term in raw_terms
    ]
    for i, term in enumerate(terms_of(*raw_terms)):
        terms[i, 0:n_rows, :] = term
        terms[i, n_rows : n_rows + 8, :] = jnp.full((8, LANES), -1.0 if i == 7 else 1.0, F32)
    ends = [pair_ref[zz, slots : slots + KIN_ROWS, 0:slots].astype(F32) for zz in range(nz)]
    raw_terms = [
        jnp.concatenate([ends[zz][i : i + 1] for zz in range(nz)], axis=0) for i in range(5)
    ]
    for i, term in enumerate(terms_of(*raw_terms)):
        for zz in range(nz):
            q_terms[i, zz * slots : (zz + 1) * slots, :] = jnp.broadcast_to(
                term[zz : zz + 1], (slots, slots)
            ).T

    counts = []
    for row in (0, UNIT - 1):
        bound = q_terms[7, pl.ds(row, n_units, stride=UNIT), :]
        count = jnp.zeros((n_units, 128), F32)
        for t in range(n_rows):
            key = terms[7, t : t + 1, :]
            count = count + jnp.where(key < bound if row == 0 else key <= bound, 1.0, 0.0)
        counts.append(jnp.sum(count, axis=1, keepdims=True).astype(jnp.int32))
    start = jnp.minimum(counts[0] // LANES, n_rows - 1)
    stop = jnp.maximum((counts[1] + (LANES - 1)) // LANES, start + 1)
    ranges[0] = start + jnp.zeros((n_units, 128), jnp.int32)
    ranges[1] = (stop - start + (per_step - 1)) // per_step + jnp.zeros((n_units, 128), jnp.int32)
    to_scalars = pltpu.make_async_copy(ranges, limits, load_sem.at[7])
    to_scalars.start()

    wkt = wk_ref[...].astype(F32).T.astype(BF16)
    for yy in range(ny):
        for zz in range(nz):
            rows = jnp.concatenate(
                [
                    jnp.concatenate(
                        [keys_ref[yy, xx, zz, i : i + half, :] for i in range(0, body, half)],
                        axis=1,
                    )
                    for xx in range(nx)
                ],
                axis=0,
            )
            at = slice((zz * ny + yy) * TILE, (zz * ny + yy + 1) * TILE)
            kt_ref[:, at] = lax.dot_general(
                wkt, rows, (((1,), (1,)), ((), ())), preferred_element_type=F32
            ).astype(BF16)
            v_ref[at, :] = jnp.dot(rows, wv_ref[...], preferred_element_type=F32).astype(BF16)

    kt_ref[:, n_tiles * TILE :] = jnp.zeros((width, LANES), BF16)
    v_ref[n_tiles * TILE :, :] = jnp.zeros((LANES, width), BF16)

    lane_head = lax.broadcasted_iota(jnp.int32, (GROUP, width), 1) // head_size
    for zz in range(nz):
        queries = jnp.dot(pair_ref[zz, 0:slots, :], wq_ref[...], preferred_element_type=F32)
        for base in range(0, slots, GROUP):
            rows = queries[base : base + GROUP]
            at = (zz * slots + base) * heads
            qm_ref[at : at + rows_g, :] = jnp.concatenate(
                [jnp.where(lane_head == h, rows, 0.0) for h in range(heads)], axis=0
            ).astype(BF16)

    top_ref[...] = jnp.full_like(top_ref, -1e30)
    total_ref[...] = jnp.zeros_like(total_ref)
    acc_ref[...] = jnp.zeros_like(acc_ref)

    to_scalars.wait()

    def following(u, k):
        more = k + 1 < limits[1, u, 0]
        return jnp.where(more, u, jnp.minimum(u + 1, n_units - 1)), jnp.where(more, k + 1, 0)

    steps = limits[1, 0, 0]
    for u in range(1, n_units):
        steps = steps + limits[1, u, 0]

    def place(u, k):
        return limits[0, u, 0] + k * per_step

    def features(p, u, k):
        t = place(u, k)
        for g in range(groups):
            base = pl.multiple_of(u * UNIT + g * GROUP, GROUP)
            qt = [q_terms[i, pl.ds(base, GROUP), :] for i in range(7)]
            columns = []
            for i in range(per_step):
                kt = [terms[j, pl.ds(t + i, 1), :] for j in range(7)]
                gap = qt[1] - kt[1]
                cos_gap = qt[2] * kt[2] + qt[3] * kt[3]
                dist = gap * gap + (2.0 - 2.0 * cos_gap)
                small = jnp.minimum(qt[0], kt[0])
                msq = (
                    qt[6]
                    + kt[6]
                    + (qt[4] * kt[5] + qt[5] * kt[4] - 2.0 * (qt[0] * kt[0] * cos_gap))
                )
                f = [
                    jnp.log(1.0 + dist),
                    jnp.log(1.0 + small * small * dist),
                    small / (qt[0] + kt[0]),
                    jnp.log(1.0 + msq),
                ]
                fh, fl = split_two(jnp.concatenate(f, axis=0))
                columns.append(
                    jnp.concatenate([fh, fl, fh, jnp.ones((2 * GROUP, 128), BF16)], axis=0)
                )
            fresh[p, g] = jnp.concatenate(columns, axis=1)

    def hiddens(p):
        for g in range(groups):
            z = jnp.dot(wfirst[...], fresh[p, g], preferred_element_type=F32)
            hidden[p, g] = z[0 : hid * GROUP].astype(BF16)
            linear[p, g] = z[hid * GROUP :]

    def gelus(p):
        for g in range(groups):
            inner = hidden[p, g]
            turned[p, g] = inner * jnp.tanh(inner * (ALPHA + inner * inner))

    def scores(p, u, k, away):
        t = place(u, k)
        start = pl.multiple_of(t * LANES, LANES)
        first_row = pl.multiple_of(u * rows_u, rows_u)
        products = jnp.dot(
            qm_ref[pl.ds(first_row, rows_u), :],
            kt_ref[:, pl.ds(start, TILE)],
            preferred_element_type=F32,
        )
        for g in range(groups):
            base = pl.multiple_of(u * UNIT + g * GROUP, GROUP)
            bias = jnp.dot(wsecond[...], turned[p, g], preferred_element_type=F32)
            s = products[g * rows_g : (g + 1) * rows_g] + (bias + linear[p, g])
            own = q_terms[7, pl.ds(base, GROUP), :] + away
            live = jnp.concatenate(
                [own == terms[7, pl.ds(t + i, 1), :] for i in range(per_step)], axis=1
            )
            s = jnp.where(live[None], s.reshape(heads, GROUP, TILE), -1e30).reshape(rows_g, TILE)
            at = pl.ds(pl.multiple_of(first_row + g * rows_g, rows_g), rows_g)
            s_ref[at, pl.ds(start, TILE)] = s
            run_max = top_ref[at, :]
            for i in range(0, TILE, 128):
                run_max = jnp.maximum(run_max, s[:, i : i + 128])
            top_ref[at, :] = run_max

    def score_steps(i, carry):
        for k in range(SCORE_STEPS):
            p = k % 2
            u0, t0, u1, t1, u2, t2, u3, t3 = carry
            scores(1 - p, u3, t3, jnp.where(SCORE_STEPS * i + k >= 3, 0.0, 100.0))
            hiddens(1 - p)
            gelus(p)
            features(p, u0, t0)
            carry = (*following(u0, t0), u0, t0, u1, t1, u2, t2)
        return carry

    zero = jnp.int32(0)
    lax.fori_loop(0, (steps + SCORE_STEPS + 2) // SCORE_STEPS, score_steps, (zero,) * 8)

    for u in range(n_units):
        at = slice(u * rows_u, (u + 1) * rows_u)
        top_ref[at, :] = jnp.broadcast_to(
            jnp.max(top_ref[at, :], axis=1, keepdims=True), (rows_u, 128)
        )

    weight_ref[...] = jnp.zeros_like(weight_ref)

    def apply(p, u, k):
        at = pl.ds(pl.multiple_of(u * rows_u, rows_u), rows_u)
        acc_ref[at, :] += jnp.dot(
            weight_ref[p],
            v_ref[pl.ds(pl.multiple_of(place(u, k) * LANES, LANES), TILE), :],
            preferred_element_type=F32,
        )

    def weigh(p, u, k, above):
        t = place(u, k)
        at = pl.ds(pl.multiple_of(u * rows_u, rows_u), rows_u)
        top = top_ref[at, :] + above
        total = total_ref[at, :]
        for i in range(0, TILE, 128):
            cols = pl.ds(pl.multiple_of(t * LANES + i, 128), 128)
            weight = jnp.exp2((s_ref[at, cols] - top) * (LOG2E / root))
            total = total + weight
            weight_ref[p, :, i : i + 128] = weight.astype(BF16)
        total_ref[at, :] = total

    def value_steps(i, carry):
        for k in range(VALUE_STEPS):
            u0, t0, u1, t1 = carry
            apply(1 - k % 2, u1, t1)
            weigh(k % 2, u0, t0, jnp.where(VALUE_STEPS * i + k < steps, 0.0, 1e32))
            carry = (*following(u0, t0), u0, t0)
        return carry

    lax.fori_loop(0, (steps + VALUE_STEPS) // VALUE_STEPS, value_steps, (zero,) * 4)

    lane = lax.broadcasted_iota(jnp.int32, (rows_g, slots), 1)
    row = lax.rem(lax.broadcasted_iota(jnp.int32, (rows_g, slots), 0), GROUP)
    for zz in range(nz):
        level = jnp.zeros((rows_g, slots), F32)
        for base in range(0, slots, GROUP):
            at = (zz * slots + base) * heads
            total = jnp.sum(total_ref[at : at + rows_g, :], axis=1, keepdims=True)
            level = jnp.where(
                lane == base + row,
                top_ref[at : at + rows_g, :] * (LOG2E / root) + jnp.log(total) * LOG2E,
                level,
            )
            total = 1.0 / total
            out = jnp.zeros((GROUP, width), F32)
            for h in range(heads):
                rows = slice(at + h * GROUP, at + (h + 1) * GROUP)
                scaled = acc_ref[rows, :] * total[h * GROUP : (h + 1) * GROUP]
                out = jnp.where(lane_head == h, scaled, out)
            held_ref[base : base + GROUP, :] = out
        out_ref[zz] = held_ref[...].astype(BF16)
        level_ref[zz] = jnp.sum(level.reshape(heads, GROUP, slots), axis=1)


def finish_kernel(
    cube,
    part_ref,
    level_ref,
    wo_ref,
    gain_ref,
    out_ref,
    part_in,
    level_in,
    part_own,
    level_own,
    wo_own,
    gain_own,
    send_sem,
    recv_sem,
    load_sem,
):
    _, ny, nx = cube
    z, y, x = mesh_place(cube)
    near = {"blk": ((1 - z) * ny + y) * nx + x}
    heads = level_ref.shape[1]
    width = part_ref.shape[2]
    barrier = pltpu.get_barrier_semaphore()
    pl.semaphore_signal(barrier, inc=1, device_id=near, device_id_type=MESH)
    loads = [
        pltpu.make_async_copy(part_ref.at[z], part_own, load_sem.at[0]),
        pltpu.make_async_copy(level_ref.at[z], level_own, load_sem.at[1]),
        pltpu.make_async_copy(wo_ref, wo_own, load_sem.at[2]),
        pltpu.make_async_copy(gain_ref, gain_own, load_sem.at[3]),
    ]
    for load in loads:
        load.start()
    pl.semaphore_wait(barrier, 1)
    copies = [
        pltpu.make_async_remote_copy(
            src_ref=src,
            dst_ref=dst,
            send_sem=send_sem.at[i],
            recv_sem=recv_sem.at[i],
            device_id=near,
            device_id_type=MESH,
        )
        for i, (src, dst) in enumerate(
            [(part_ref.at[1 - z], part_in), (level_ref.at[1 - z], level_in)]
        )
    ]
    for copy in copies:
        copy.start()
    spread = (
        lax.broadcasted_iota(jnp.int32, (heads, width), 1) // (width // heads)
        == lax.broadcasted_iota(jnp.int32, (heads, width), 0)
    ).astype(F32)
    for copy in loads + copies:
        copy.wait()
    share = 1.0 / (1.0 + jnp.exp2(level_in[...] - level_own[...]))
    share = jnp.dot(share.T, spread, precision=HIGHEST, preferred_element_type=F32)
    theirs = part_in[...].astype(F32)
    attended = theirs + share * (part_own[...].astype(F32) - theirs)
    mixed = jnp.dot(attended.astype(BF16), wo_own[...], preferred_element_type=F32)
    out_ref[...] = layer_norm(mixed, gain_own[...]).astype(BF16)


def shards(
    n_grp,
    cube,
    raw,
    raw_kin,
    reader,
    event_id,
    pre_gain,
    w_query,
    w_key,
    w_value,
    w_out,
    post_gain,
    pair_w1,
    pair_b1,
    pair_w2,
):
    slots, width = raw.shape[2], raw.shape[3]
    heads = pair_w2.shape[1]
    nz, ny, nx = cube
    vmem = pl.BlockSpec(memory_space=pltpu.VMEM)
    free = pl.BlockSpec(memory_space=pl.ANY)
    dma = pltpu.SemaphoreType.DMA
    tall = slots + KIN_ROWS
    part_rows = slots // nz * (width // 128) + KIN_ROWS
    feats, hid = pair_w1.shape
    mixing = (3 * feats + 2) * GROUP
    pair, keys, first, second = pl.pallas_call(
        functools.partial(exchange_kernel, n_grp, cube),
        out_shape=(
            jax.ShapeDtypeStruct((nz, tall, width), BF16),
            jax.ShapeDtypeStruct((ny, nx, nz, part_rows, 128), BF16),
            jax.ShapeDtypeStruct(((hid + heads) * GROUP, mixing), BF16),
            jax.ShapeDtypeStruct((heads * GROUP, hid * GROUP), BF16),
        ),
        in_specs=[free] * 8,
        out_specs=(free,) * 4,
        scratch_shapes=[
            pltpu.VMEM(raw_kin.shape, BF16),
            pltpu.VMEM(reader.shape, jnp.int32),
            pltpu.VMEM(event_id.shape, jnp.int32),
            pltpu.VMEM((1, width), F32),
            pltpu.VMEM((feats, hid), F32),
            pltpu.VMEM((1, hid), F32),
            pltpu.VMEM((heads, hid), F32),
            pltpu.VMEM(((hid + heads) * GROUP, mixing), BF16),
            pltpu.VMEM((heads * GROUP, hid * GROUP), BF16),
            dma((8,)),
            pltpu.VMEM((n_grp, slots, width), BF16),
            pltpu.VMEM((n_grp, 8, slots), F32),
            pltpu.VMEM((n_grp, 8, slots), F32),
            pltpu.VMEM((tall, width), BF16),
            pltpu.VMEM((part_rows - KIN_ROWS, 128), BF16),
            pltpu.VMEM((part_rows, 128), BF16),
            pltpu.VMEM((part_rows, 128), BF16),
            dma((n_grp,)),
            dma((n_grp,)),
            dma((n_grp,)),
            dma((n_grp,)),
            dma((32,)),
            dma((32,)),
            dma((3,)),
        ],
        compiler_params=pltpu.CompilerParams(collective_id=0, has_side_effects=True),
        name="exchange",
    )(
        raw,
        raw_kin,
        reader,
        event_id,
        pre_gain[None],
        pair_w1,
        pair_b1[None],
        pair_w2.T,
    )

    own_rows = nz * slots
    n_tiles = nz * ny
    groups = UNIT // GROUP
    rows_all = heads * own_rows
    part, level = pl.pallas_call(
        functools.partial(attend_kernel, heads),
        out_shape=(
            jax.ShapeDtypeStruct((nz, slots, width), BF16),
            jax.ShapeDtypeStruct((nz, heads, slots), F32),
        ),
        in_specs=[free] * 7,
        out_specs=(vmem, vmem),
        scratch_shapes=[
            pltpu.VMEM((nz, tall, width), BF16),
            pltpu.VMEM((ny, nx, nz, part_rows, 128), BF16),
            pltpu.VMEM((width, width), BF16),
            pltpu.VMEM((width, width), BF16),
            pltpu.VMEM((width, width), BF16),
            pltpu.VMEM(((hid + heads) * GROUP, mixing), BF16),
            pltpu.VMEM((heads * GROUP, hid * GROUP), BF16),
            dma((8,)),
            pltpu.VMEM((width, n_tiles * TILE + LANES), BF16),
            pltpu.VMEM((n_tiles * TILE + LANES, width), BF16),
            pltpu.VMEM((8, n_tiles * TILE // LANES + 8, LANES), F32),
            pltpu.VMEM((8, own_rows, slots), F32),
            pltpu.VMEM((rows_all, width), BF16),
            pltpu.VMEM((rows_all, n_tiles * TILE + LANES), F32),
            pltpu.VMEM((rows_all, 128), F32),
            pltpu.VMEM((rows_all, 128), F32),
            pltpu.VMEM((rows_all, width), F32),
            pltpu.VMEM((2, groups, mixing, TILE), BF16),
            pltpu.VMEM((2, groups, hid * GROUP, TILE), BF16),
            pltpu.VMEM((2, groups, heads * GROUP, TILE), F32),
            pltpu.VMEM((2, groups, hid * GROUP, TILE), BF16),
            pltpu.VMEM((2, heads * UNIT, TILE), BF16),
            pltpu.VMEM((slots, width), F32),
            pltpu.VMEM((2, own_rows // UNIT, 128), jnp.int32),
            pltpu.SMEM((2, own_rows // UNIT, 128), jnp.int32),
        ],
        compiler_params=pltpu.CompilerParams(vmem_limit_bytes=63 * 1024 * 1024),
        name="attend",
    )(pair, keys, w_query, w_key, w_value, first, second)

    encoded = pl.pallas_call(
        functools.partial(finish_kernel, cube),
        out_shape=jax.ShapeDtypeStruct((slots, width), BF16),
        in_specs=[free] * 4,
        out_specs=vmem,
        scratch_shapes=[
            pltpu.VMEM((slots, width), BF16),
            pltpu.VMEM((heads, slots), F32),
            pltpu.VMEM((slots, width), BF16),
            pltpu.VMEM((heads, slots), F32),
            pltpu.VMEM((width, width), BF16),
            pltpu.VMEM((1, width), F32),
            dma((2,)),
            dma((2,)),
            dma((4,)),
        ],
        compiler_params=pltpu.CompilerParams(collective_id=1, has_side_effects=True),
        name="finish",
    )(part, level, w_out, post_gain[None])
    return encoded[None]


def solution(mesh):
    in_specs = (
        P("grp", None, "blk", None),
        P("grp", None, None, "blk"),
        P("grp", "blk"),
        P("grp", "blk"),
        P(),
        P(),
        P(),
        P(),
        P(),
        P(),
        P(),
        P(),
        P(),
    )
    out_specs = P("grp", "blk", None)
    cube = (2, 4, mesh.shape["blk"] // 8)
    body = functools.partial(shards, mesh.shape["grp"], cube)
    return jax.shard_map(body, mesh=mesh, in_specs=in_specs, out_specs=out_specs, check_vma=False)
```

```python
import functools
import math

import jax
import jax.numpy as jnp
from jax import lax
from jax.experimental import pallas as pl
from jax.experimental.pallas import tpu as pltpu
from jax.sharding import PartitionSpec as P

MESH = pl.DeviceIdType.MESH
F32 = jnp.float32
BF16 = jnp.bfloat16
HIGHEST = lax.Precision.HIGHEST

KIN_ROWS = 16
GROUP = 8
UNIT = 16
TILE = 256
LANES = 128
SCORE_STEPS = 6
VALUE_STEPS = 8

GELU_A = math.sqrt(2.0 / math.pi)
GELU_B = GELU_A * 0.044715
GELU_S = GELU_B ** (-1.0 / 3.0)
ALPHA = GELU_A * GELU_S
LOG2E = 1.0 / math.log(2.0)


def layer_norm(rows, gain):
    center = rows - jnp.mean(rows, axis=-1, keepdims=True)
    spread = jnp.mean(center * center, axis=-1, keepdims=True)
    return center * lax.rsqrt(spread + 1e-05) * gain


def mesh_place(cube):
    _, ny, nx = cube
    b = lax.axis_index("blk")
    return b // (ny * nx), lax.rem(b // nx, ny), lax.rem(b, nx)


def exchange_kernel(
    n_grp,
    cube,
    raw_ref,
    kin_hbm,
    reader_hbm,
    event_hbm,
    gain_hbm,
    w1_hbm,
    b1_hbm,
    w2t_hbm,
    pair_ref,
    keys_ref,
    first_hbm,
    second_hbm,
    kin_ref,
    reader_ref,
    event_ref,
    gain_ref,
    w1_ref,
    b1_ref,
    w2t_ref,
    wfirst,
    wsecond,
    load_sem,
    inbox,
    kin_send,
    kin_in,
    block,
    mine,
    theirs,
    got,
    send_sem,
    recv_sem,
    kin_send_sem,
    kin_recv_sem,
    link_send,
    link_recv,
    own_sem,
):
    nz, ny, nx = cube
    g = lax.axis_index("grp")
    z, y, x = mesh_place(cube)
    slots = raw_ref.shape[2]
    width = raw_ref.shape[3]
    half = slots // nz
    body = half * (width // 128)

    def blk(z, y, x):
        return {"blk": (z * ny + y) * nx + x}

    partners = [{"grp": lax.rem(g + k, n_grp)} for k in range(1, n_grp)]
    turns = (1, nx - 1, 2)
    x_peers = [blk(z, y, lax.rem(x + k, nx)) for k in turns]
    y_peers = [blk(z, lax.rem(y + k, ny), x) for k in turns]
    near = blk(1 - z, y, x)
    partners += [near] + x_peers + y_peers
    barrier = pltpu.get_barrier_semaphore()
    for partner in partners:
        pl.semaphore_signal(barrier, inc=1, device_id=partner, device_id_type=MESH)
    loads = [
        pltpu.make_async_copy(src, dst, load_sem.at[i])
        for i, (src, dst) in enumerate(
            [
                (kin_hbm, kin_ref),
                (reader_hbm, reader_ref),
                (event_hbm, event_ref),
                (gain_hbm, gain_ref),
                (w1_hbm, w1_ref),
                (b1_hbm, b1_ref),
                (w2t_hbm, w2t_ref),
                (raw_ref.at[0, g], inbox.at[0]),
            ]
        )
    ]
    for load in loads:
        load.start()
    loads[0].wait()
    kin_send[...] = jnp.zeros_like(kin_send)
    for k in range(n_grp):
        kin_send[k, 0:4, :] = kin_ref[0, k].astype(F32)
    pl.semaphore_wait(barrier, len(partners))

    copies = []
    for k in range(1, n_grp):
        to = lax.rem(g + k, n_grp)
        for src, dst, ssem, rsem in (
            (raw_ref.at[0, to], inbox.at[n_grp - k], send_sem, recv_sem),
            (kin_send.at[to], kin_in.at[n_grp - k], kin_send_sem, kin_recv_sem),
        ):
            copy = pltpu.make_async_remote_copy(
                src_ref=src,
                dst_ref=dst,
                send_sem=ssem.at[k],
                recv_sem=rsem.at[n_grp - k],
                device_id={"grp": to},
                device_id_type=MESH,
            )
            copy.start()
            copies.append(copy)

    for load in loads[1:]:
        load.wait()
    pair_weights(w1_ref[...], b1_ref[...], w2t_ref[...], width // w2t_ref.shape[0], wfirst, wsecond)
    wanted = lax.rem(reader_ref[...] - g + n_grp, n_grp)
    stores = [
        pltpu.make_async_copy(wfirst, first_hbm, load_sem.at[0]),
        pltpu.make_async_copy(wsecond, second_hbm, load_sem.at[1]),
    ]
    for store in stores:
        store.start()
    column = jnp.broadcast_to(wanted, (slots, slots)).T
    kin = jnp.where(wanted == 0, kin_send[g, 0:4, :], 0.0)
    sides = [
        jnp.where(column == 0, inbox[0][:, h : h + slots].astype(F32), 0.0)
        for h in range(0, width, slots)
    ]
    for copy in copies:
        copy.wait_recv()
    for k in range(1, n_grp):
        kin = kin + jnp.where(wanted == k, kin_in[k, 0:4, :], 0.0)
        sides = [
            side
            + jnp.where(column == k, inbox[k][:, i * slots : (i + 1) * slots].astype(F32), 0.0)
            for i, side in enumerate(sides)
        ]
    tokens = jnp.concatenate(sides, axis=1)
    normed = layer_norm(tokens, gain_ref[...]).astype(BF16)
    block[0:slots, :] = normed
    tail = jnp.concatenate(
        [kin, event_ref[...].astype(F32), jnp.zeros((KIN_ROWS - 5, slots), F32)], axis=0
    )
    block[slots : slots + KIN_ROWS, :] = jnp.concatenate([tail, tail], axis=1).astype(BF16)
    for ref, low in ((mine, z == 0), (theirs, z == 1)):
        for i in range(width // 128):
            cols = slice(i * 128, (i + 1) * 128)
            ref[i * half : (i + 1) * half, :] = jnp.where(
                low, normed[0:half, cols], normed[half : 2 * half, cols]
            )
    theirs[body : body + KIN_ROWS, :] = tail.astype(BF16)

    def push(slot, src, dst, to):
        copy = pltpu.make_async_remote_copy(
            src_ref=src,
            dst_ref=dst,
            send_sem=link_send.at[slot],
            recv_sem=link_recv.at[slot],
            device_id=to,
            device_id_type=MESH,
        )
        copy.start()
        return copy

    rows = pl.ds(0, body)
    swap = push(0, theirs, got, near)
    own_x = [push(1 + i, mine, keys_ref.at[y, x, z, rows], to) for i, to in enumerate(x_peers)]
    moves = [push(4 + i, mine, keys_ref.at[y, x, z, rows], to) for i, to in enumerate(y_peers)]
    here = [
        pltpu.make_async_copy(mine, keys_ref.at[y, x, z, rows], own_sem.at[0]),
        pltpu.make_async_copy(block, pair_ref.at[z], own_sem.at[1]),
    ]
    for copy in here:
        copy.start()
    swap.wait_recv()
    ends = got[body : body + KIN_ROWS, :].astype(F32)
    ends = jnp.concatenate([ends[:, half:], ends[:, :half]], axis=1)
    side = lax.broadcasted_iota(jnp.int32, (KIN_ROWS, slots), 1) // half
    got[body : body + KIN_ROWS, :] = jnp.where(side == z, tail, ends).astype(BF16)
    other_y = [push(7 + i, got, keys_ref.at[y, x, 1 - z], to) for i, to in enumerate(y_peers)]
    moves += [push(10 + i, got, keys_ref.at[y, x, 1 - z], to) for i, to in enumerate(x_peers)]
    here.append(pltpu.make_async_copy(got, keys_ref.at[y, x, 1 - z], own_sem.at[2]))
    here[-1].start()
    moves.append(push(13, block, pair_ref.at[z], near))
    slot = 14
    for i, k in enumerate(turns):
        own_x[i].wait_recv()
        piece = keys_ref.at[y, lax.rem(x - k + nx, nx), z, rows]
        for to in y_peers:
            moves.append(push(slot, piece, piece, to))
            slot += 1
    for i, k in enumerate(turns):
        other_y[i].wait_recv()
        piece = keys_ref.at[lax.rem(y - k + ny, ny), x, 1 - z]
        for to in x_peers:
            moves.append(push(slot, piece, piece, to))
            slot += 1
    for copy in here + stores:
        copy.wait()
    for copy in copies + [swap] + own_x + other_y:
        copy.wait_send()
    for copy in moves:
        copy.wait()


def split_two(value):
    high = value.astype(BF16)
    low = (value - high.astype(F32)).astype(BF16)
    return high, low


def spread_over(weight):
    m, c = weight.shape
    up = (
        lax.broadcasted_iota(jnp.int32, (m * GROUP, m), 0) // GROUP
        == lax.broadcasted_iota(jnp.int32, (m * GROUP, m), 1)
    ).astype(F32)
    across = (
        lax.broadcasted_iota(jnp.int32, (c, c * GROUP), 1) // GROUP
        == lax.broadcasted_iota(jnp.int32, (c, c * GROUP), 0)
    ).astype(F32)
    tall = jnp.dot(up, weight, precision=HIGHEST, preferred_element_type=F32)
    wide = jnp.dot(tall, across, precision=HIGHEST, preferred_element_type=F32)
    same = (
        lax.broadcasted_iota(jnp.int32, (m * GROUP, c * GROUP), 0) % GROUP
        == lax.broadcasted_iota(jnp.int32, (m * GROUP, c * GROUP), 1) % GROUP
    )
    return jnp.where(same, wide, 0.0)


def pair_weights(w1, b1, w2t, head_size, wfirst, wsecond):
    feats, hid = w1.shape
    root = math.sqrt(head_size)
    first = jnp.concatenate([w1, b1, jnp.zeros((8 - feats - 1, hid), F32)], axis=0)
    line = lax.dot_general(
        w2t, first, (((1,), (1,)), ((), ())), precision=HIGHEST, preferred_element_type=F32
    ) * (0.5 * root)
    part = feats * GROUP

    stacked = jnp.concatenate([first.T * (1.0 / GELU_S), line], axis=0)
    high, low = split_two(spread_over(stacked))
    wfirst[:, 0:part] = high[:, 0:part]
    wfirst[:, part : 2 * part] = high[:, 0:part]
    wfirst[:, 2 * part : 3 * part] = low[:, 0:part]
    wfirst[:, 3 * part : 3 * part + GROUP] = high[:, part : part + GROUP]
    wfirst[:, 3 * part + GROUP : 3 * part + 2 * GROUP] = low[:, part : part + GROUP]
    wsecond[...] = spread_over(w2t * (0.5 * root * GELU_S)).astype(BF16)


def attend_kernel(
    heads,
    pair_hbm,
    keys_hbm,
    wq_hbm,
    wk_hbm,
    wv_hbm,
    first_hbm,
    second_hbm,
    out_ref,
    level_ref,
    pair_ref,
    keys_ref,
    wq_ref,
    wk_ref,
    wv_ref,
    wfirst,
    wsecond,
    load_sem,
    kt_ref,
    v_ref,
    terms,
    q_terms,
    qm_ref,
    s_ref,
    top_ref,
    total_ref,
    acc_ref,
    fresh,
    hidden,
    linear,
    turned,
    weight_ref,
    held_ref,
    ranges,
    limits,
):
    loads = [
        pltpu.make_async_copy(src, dst, load_sem.at[i])
        for i, (src, dst) in enumerate(
            [
                (keys_hbm, keys_ref),
                (pair_hbm, pair_ref),
                (wk_hbm, wk_ref),
                (wv_hbm, wv_ref),
                (wq_hbm, wq_ref),
                (first_hbm, wfirst),
                (second_hbm, wsecond),
            ]
        )
    ]
    for load in loads:
        load.start()
    nz, slots, width = out_ref.shape
    ny, nx = keys_ref.shape[0:2]
    half = slots // nz
    own_rows = nz * slots
    head_size = width // heads
    hid = wsecond.shape[1] // GROUP
    root = math.sqrt(head_size)
    groups = UNIT // GROUP
    rows_g = heads * GROUP
    rows_u = groups * rows_g
    n_units = own_rows // UNIT
    n_tiles = nz * ny
    per_step = TILE // LANES
    z = lax.axis_index("blk") // (ny * nx)

    for load in loads[0:2]:
        load.wait()

    def terms_of(mom, rap, azi, mass, ids):
        trans = jnp.sqrt(mom * mom + mass * mass)
        return (
            mom,
            rap,
            jnp.cos(azi),
            jnp.sin(azi),
            trans * jnp.exp(rap),
            trans * jnp.exp(-rap),
            mass * mass,
            ids,
        )

    body = half * (width // 128)
    lower = lax.broadcasted_iota(jnp.int32, (KIN_ROWS, 128), 1) < half
    ends = [[] for _ in range(nz)]
    for yy in range(ny):
        tails = [
            keys_ref[yy, xx, 1 - z, body : body + KIN_ROWS, :].astype(F32) for xx in range(nx)
        ]
        turned_tails = [jnp.concatenate([e[:, half:], e[:, :half]], axis=1) for e in tails]
        ends[0].append(
            [jnp.where(lower, tails[k], turned_tails[k + 1]) for k in range(0, nx, 2)]
        )
        ends[1].append(
            [jnp.where(lower, turned_tails[k], tails[k + 1]) for k in range(0, nx, 2)]
        )
    ends = [jnp.concatenate(end, axis=1) for zz in range(nz) for end in ends[zz]]
    raw_terms = [jnp.concatenate([end[i : i + 1] for end in ends], axis=0) for i in range(5)]
    n_rows = n_tiles * TILE // LANES
    raw_terms = [
        jnp.concatenate(
            [
                term[t : t + 1, k : k + LANES]
                for t in range(n_tiles)
                for k in range(0, TILE, LANES)
            ],
            axis=0,
        )
        for term in raw_terms
    ]
    for i, term in enumerate(terms_of(*raw_terms)):
        terms[i, 0:n_rows, :] = term
        terms[i, n_rows : n_rows + 8, :] = jnp.full((8, LANES), -1.0 if i == 7 else 1.0, F32)
    ends = [pair_ref[zz, slots : slots + KIN_ROWS, 0:slots].astype(F32) for zz in range(nz)]
    raw_terms = [
        jnp.concatenate([ends[zz][i : i + 1] for zz in range(nz)], axis=0) for i in range(5)
    ]
    for i, term in enumerate(terms_of(*raw_terms)):
        for zz in range(nz):
            q_terms[i, zz * slots : (zz + 1) * slots, :] = jnp.broadcast_to(
                term[zz : zz + 1], (slots, slots)
            ).T

    counts = []
    for row in (0, UNIT - 1):
        bound = q_terms[7, pl.ds(row, n_units, stride=UNIT), :]
        count = jnp.zeros((n_units, 128), F32)
        for t in range(n_rows):
            key = terms[7, t : t + 1, :]
            count = count + jnp.where(key < bound if row == 0 else key <= bound, 1.0, 0.0)
        counts.append(jnp.sum(count, axis=1, keepdims=True).astype(jnp.int32))
    start = jnp.minimum(counts[0] // LANES, n_rows - 1)
    stop = jnp.maximum((counts[1] + (LANES - 1)) // LANES, start + 1)
    ranges[0] = start + jnp.zeros((n_units, 128), jnp.int32)
    ranges[1] = (stop - start + (per_step - 1)) // per_step + jnp.zeros((n_units, 128), jnp.int32)
    to_scalars = pltpu.make_async_copy(ranges, limits, load_sem.at[7])
    to_scalars.start()

    for load in loads[2:]:
        load.wait()
    wkt = wk_ref[...].astype(F32).T.astype(BF16)
    for yy in range(ny):
        for zz in range(nz):
            rows = jnp.concatenate(
                [
                    jnp.concatenate(
                        [keys_ref[yy, xx, zz, i : i + half, :] for i in range(0, body, half)],
                        axis=1,
                    )
                    for xx in range(nx)
                ],
                axis=0,
            )
            at = slice((zz * ny + yy) * TILE, (zz * ny + yy + 1) * TILE)
            kt_ref[:, at] = lax.dot_general(
                wkt, rows, (((1,), (1,)), ((), ())), preferred_element_type=F32
            ).astype(BF16)
            v_ref[at, :] = jnp.dot(rows, wv_ref[...], preferred_element_type=F32).astype(BF16)

    kt_ref[:, n_tiles * TILE :] = jnp.zeros((width, LANES), BF16)
    v_ref[n_tiles * TILE :, :] = jnp.zeros((LANES, width), BF16)

    lane_head = lax.broadcasted_iota(jnp.int32, (GROUP, width), 1) // head_size
    for zz in range(nz):
        queries = jnp.dot(pair_ref[zz, 0:slots, :], wq_ref[...], preferred_element_type=F32)
        for base in range(0, slots, GROUP):
            rows = queries[base : base + GROUP]
            at = (zz * slots + base) * heads
            qm_ref[at : at + rows_g, :] = jnp.concatenate(
                [jnp.where(lane_head == h, rows, 0.0) for h in range(heads)], axis=0
            ).astype(BF16)

    top_ref[...] = jnp.full_like(top_ref, -1e30)
    total_ref[...] = jnp.zeros_like(total_ref)
    acc_ref[...] = jnp.zeros_like(acc_ref)

    to_scalars.wait()

    def following(u, k):
        more = k + 1 < limits[1, u, 0]
        return jnp.where(more, u, jnp.minimum(u + 1, n_units - 1)), jnp.where(more, k + 1, 0)

    steps = limits[1, 0, 0]
    for u in range(1, n_units):
        steps = steps + limits[1, u, 0]

    def place(u, k):
        return limits[0, u, 0] + k * per_step

    def features(p, u, k):
        t = place(u, k)
        for g in range(groups):
            base = pl.multiple_of(u * UNIT + g * GROUP, GROUP)
            qt = [q_terms[i, pl.ds(base, GROUP), :] for i in range(7)]
            columns = []
            for i in range(per_step):
                kt = [terms[j, pl.ds(t + i, 1), :] for j in range(7)]
                gap = qt[1] - kt[1]
                cos_gap = qt[2] * kt[2] + qt[3] * kt[3]
                dist = gap * gap + (2.0 - 2.0 * cos_gap)
                small = jnp.minimum(qt[0], kt[0])
                msq = (
                    qt[6]
                    + kt[6]
                    + (qt[4] * kt[5] + qt[5] * kt[4] - 2.0 * (qt[0] * kt[0] * cos_gap))
                )
                f = [
                    jnp.log(1.0 + dist),
                    jnp.log(1.0 + small * small * dist),
                    small / (qt[0] + kt[0]),
                    jnp.log(1.0 + msq),
                ]
                fh, fl = split_two(jnp.concatenate(f, axis=0))
                columns.append(
                    jnp.concatenate([fh, fl, fh, jnp.ones((2 * GROUP, 128), BF16)], axis=0)
                )
            fresh[p, g] = jnp.concatenate(columns, axis=1)

    def hiddens(p):
        for g in range(groups):
            z = jnp.dot(wfirst[...], fresh[p, g], preferred_element_type=F32)
            hidden[p, g] = z[0 : hid * GROUP].astype(BF16)
            linear[p, g] = z[hid * GROUP :]

    def gelus(p):
        for g in range(groups):
            inner = hidden[p, g]
            turned[p, g] = inner * jnp.tanh(inner * (ALPHA + inner * inner))

    def scores(p, u, k, away):
        t = place(u, k)
        start = pl.multiple_of(t * LANES, LANES)
        first_row = pl.multiple_of(u * rows_u, rows_u)
        products = jnp.dot(
            qm_ref[pl.ds(first_row, rows_u), :],
            kt_ref[:, pl.ds(start, TILE)],
            preferred_element_type=F32,
        )
        for g in range(groups):
            base = pl.multiple_of(u * UNIT + g * GROUP, GROUP)
            bias = jnp.dot(wsecond[...], turned[p, g], preferred_element_type=F32)
            s = products[g * rows_g : (g + 1) * rows_g] + (bias + linear[p, g])
            own = q_terms[7, pl.ds(base, GROUP), :] + away
            live = jnp.concatenate(
                [own == terms[7, pl.ds(t + i, 1), :] for i in range(per_step)], axis=1
            )
            s = jnp.where(live[None], s.reshape(heads, GROUP, TILE), -1e30).reshape(rows_g, TILE)
            at = pl.ds(pl.multiple_of(first_row + g * rows_g, rows_g), rows_g)
            s_ref[at, pl.ds(start, TILE)] = s
            run_max = top_ref[at, :]
            for i in range(0, TILE, 128):
                run_max = jnp.maximum(run_max, s[:, i : i + 128])
            top_ref[at, :] = run_max

    def score_steps(i, carry):
        for k in range(SCORE_STEPS):
            p = k % 2
            u0, t0, u1, t1, u2, t2, u3, t3 = carry
            scores(1 - p, u3, t3, jnp.where(SCORE_STEPS * i + k >= 3, 0.0, 100.0))
            hiddens(1 - p)
            gelus(p)
            features(p, u0, t0)
            carry = (*following(u0, t0), u0, t0, u1, t1, u2, t2)
        return carry

    zero = jnp.int32(0)
    lax.fori_loop(0, (steps + SCORE_STEPS + 2) // SCORE_STEPS, score_steps, (zero,) * 8)

    for u in range(n_units):
        at = slice(u * rows_u, (u + 1) * rows_u)
        top_ref[at, :] = jnp.broadcast_to(
            jnp.max(top_ref[at, :], axis=1, keepdims=True), (rows_u, 128)
        )

    weight_ref[...] = jnp.zeros_like(weight_ref)

    def apply(p, u, k):
        at = pl.ds(pl.multiple_of(u * rows_u, rows_u), rows_u)
        acc_ref[at, :] += jnp.dot(
            weight_ref[p],
            v_ref[pl.ds(pl.multiple_of(place(u, k) * LANES, LANES), TILE), :],
            preferred_element_type=F32,
        )

    def weigh(p, u, k, above):
        t = place(u, k)
        at = pl.ds(pl.multiple_of(u * rows_u, rows_u), rows_u)
        top = top_ref[at, :] + above
        total = total_ref[at, :]
        for i in range(0, TILE, 128):
            cols = pl.ds(pl.multiple_of(t * LANES + i, 128), 128)
            weight = jnp.exp2((s_ref[at, cols] - top) * (LOG2E / root))
            total = total + weight
            weight_ref[p, :, i : i + 128] = weight.astype(BF16)
        total_ref[at, :] = total

    def value_steps(i, carry):
        for k in range(VALUE_STEPS):
            u0, t0, u1, t1 = carry
            apply(1 - k % 2, u1, t1)
            weigh(k % 2, u0, t0, jnp.where(VALUE_STEPS * i + k < steps, 0.0, 1e32))
            carry = (*following(u0, t0), u0, t0)
        return carry

    lax.fori_loop(0, (steps + VALUE_STEPS) // VALUE_STEPS, value_steps, (zero,) * 4)

    lane = lax.broadcasted_iota(jnp.int32, (rows_g, slots), 1)
    row = lax.rem(lax.broadcasted_iota(jnp.int32, (rows_g, slots), 0), GROUP)
    for zz in range(nz):
        level = jnp.zeros((rows_g, slots), F32)
        for base in range(0, slots, GROUP):
            at = (zz * slots + base) * heads
            total = jnp.sum(total_ref[at : at + rows_g, :], axis=1, keepdims=True)
            level = jnp.where(
                lane == base + row,
                top_ref[at : at + rows_g, :] * (LOG2E / root) + jnp.log(total) * LOG2E,
                level,
            )
            total = 1.0 / total
            out = jnp.zeros((GROUP, width), F32)
            for h in range(heads):
                rows = slice(at + h * GROUP, at + (h + 1) * GROUP)
                scaled = acc_ref[rows, :] * total[h * GROUP : (h + 1) * GROUP]
                out = jnp.where(lane_head == h, scaled, out)
            held_ref[base : base + GROUP, :] = out
        out_ref[zz] = held_ref[...].astype(BF16)
        level_ref[zz] = jnp.sum(level.reshape(heads, GROUP, slots), axis=1)


def finish_kernel(
    cube,
    part_ref,
    level_ref,
    wo_ref,
    gain_ref,
    out_ref,
    part_in,
    level_in,
    part_own,
    level_own,
    wo_own,
    gain_own,
    send_sem,
    recv_sem,
    load_sem,
):
    _, ny, nx = cube
    z, y, x = mesh_place(cube)
    near = {"blk": ((1 - z) * ny + y) * nx + x}
    heads = level_ref.shape[1]
    width = part_ref.shape[2]
    barrier = pltpu.get_barrier_semaphore()
    pl.semaphore_signal(barrier, inc=1, device_id=near, device_id_type=MESH)
    loads = [
        pltpu.make_async_copy(part_ref.at[z], part_own, load_sem.at[0]),
        pltpu.make_async_copy(level_ref.at[z], level_own, load_sem.at[1]),
        pltpu.make_async_copy(wo_ref, wo_own, load_sem.at[2]),
        pltpu.make_async_copy(gain_ref, gain_own, load_sem.at[3]),
    ]
    for load in loads:
        load.start()
    pl.semaphore_wait(barrier, 1)
    copies = [
        pltpu.make_async_remote_copy(
            src_ref=src,
            dst_ref=dst,
            send_sem=send_sem.at[i],
            recv_sem=recv_sem.at[i],
            device_id=near,
            device_id_type=MESH,
        )
        for i, (src, dst) in enumerate(
            [(part_ref.at[1 - z], part_in), (level_ref.at[1 - z], level_in)]
        )
    ]
    for copy in copies:
        copy.start()
    spread = (
        lax.broadcasted_iota(jnp.int32, (heads, width), 1) // (width // heads)
        == lax.broadcasted_iota(jnp.int32, (heads, width), 0)
    ).astype(F32)
    for copy in loads + copies:
        copy.wait()
    share = 1.0 / (1.0 + jnp.exp2(level_in[...] - level_own[...]))
    share = jnp.dot(share.T, spread, precision=HIGHEST, preferred_element_type=F32)
    theirs = part_in[...].astype(F32)
    attended = theirs + share * (part_own[...].astype(F32) - theirs)
    mixed = jnp.dot(attended.astype(BF16), wo_own[...], preferred_element_type=F32)
    out_ref[...] = layer_norm(mixed, gain_own[...]).astype(BF16)


def shards(
    n_grp,
    cube,
    raw,
    raw_kin,
    reader,
    event_id,
    pre_gain,
    w_query,
    w_key,
    w_value,
    w_out,
    post_gain,
    pair_w1,
    pair_b1,
    pair_w2,
):
    slots, width = raw.shape[2], raw.shape[3]
    heads = pair_w2.shape[1]
    nz, ny, nx = cube
    vmem = pl.BlockSpec(memory_space=pltpu.VMEM)
    free = pl.BlockSpec(memory_space=pl.ANY)
    dma = pltpu.SemaphoreType.DMA
    tall = slots + KIN_ROWS
    part_rows = slots // nz * (width // 128) + KIN_ROWS
    feats, hid = pair_w1.shape
    mixing = (3 * feats + 2) * GROUP
    pair, keys, first, second = pl.pallas_call(
        functools.partial(exchange_kernel, n_grp, cube),
        out_shape=(
            jax.ShapeDtypeStruct((nz, tall, width), BF16),
            jax.ShapeDtypeStruct((ny, nx, nz, part_rows, 128), BF16),
            jax.ShapeDtypeStruct(((hid + heads) * GROUP, mixing), BF16),
            jax.ShapeDtypeStruct((heads * GROUP, hid * GROUP), BF16),
        ),
        in_specs=[free] * 8,
        out_specs=(free,) * 4,
        scratch_shapes=[
            pltpu.VMEM(raw_kin.shape, BF16),
            pltpu.VMEM(reader.shape, jnp.int32),
            pltpu.VMEM(event_id.shape, jnp.int32),
            pltpu.VMEM((1, width), F32),
            pltpu.VMEM((feats, hid), F32),
            pltpu.VMEM((1, hid), F32),
            pltpu.VMEM((heads, hid), F32),
            pltpu.VMEM(((hid + heads) * GROUP, mixing), BF16),
            pltpu.VMEM((heads * GROUP, hid * GROUP), BF16),
            dma((8,)),
            pltpu.VMEM((n_grp, slots, width), BF16),
            pltpu.VMEM((n_grp, 8, slots), F32),
            pltpu.VMEM((n_grp, 8, slots), F32),
            pltpu.VMEM((tall, width), BF16),
            pltpu.VMEM((part_rows - KIN_ROWS, 128), BF16),
            pltpu.VMEM((part_rows, 128), BF16),
            pltpu.VMEM((part_rows, 128), BF16),
            dma((n_grp,)),
            dma((n_grp,)),
            dma((n_grp,)),
            dma((n_grp,)),
            dma((32,)),
            dma((32,)),
            dma((3,)),
        ],
        compiler_params=pltpu.CompilerParams(collective_id=0, has_side_effects=True),
        name="exchange",
    )(
        raw,
        raw_kin,
        reader,
        event_id,
        pre_gain[None],
        pair_w1,
        pair_b1[None],
        pair_w2.T,
    )

    own_rows = nz * slots
    n_tiles = nz * ny
    groups = UNIT // GROUP
    rows_all = heads * own_rows
    part, level = pl.pallas_call(
        functools.partial(attend_kernel, heads),
        out_shape=(
            jax.ShapeDtypeStruct((nz, slots, width), BF16),
            jax.ShapeDtypeStruct((nz, heads, slots), F32),
        ),
        in_specs=[free] * 7,
        out_specs=(vmem, vmem),
        scratch_shapes=[
            pltpu.VMEM((nz, tall, width), BF16),
            pltpu.VMEM((ny, nx, nz, part_rows, 128), BF16),
            pltpu.VMEM((width, width), BF16),
            pltpu.VMEM((width, width), BF16),
            pltpu.VMEM((width, width), BF16),
            pltpu.VMEM(((hid + heads) * GROUP, mixing), BF16),
            pltpu.VMEM((heads * GROUP, hid * GROUP), BF16),
            dma((8,)),
            pltpu.VMEM((width, n_tiles * TILE + LANES), BF16),
            pltpu.VMEM((n_tiles * TILE + LANES, width), BF16),
            pltpu.VMEM((8, n_tiles * TILE // LANES + 8, LANES), F32),
            pltpu.VMEM((8, own_rows, slots), F32),
            pltpu.VMEM((rows_all, width), BF16),
            pltpu.VMEM((rows_all, n_tiles * TILE + LANES), F32),
            pltpu.VMEM((rows_all, 128), F32),
            pltpu.VMEM((rows_all, 128), F32),
            pltpu.VMEM((rows_all, width), F32),
            pltpu.VMEM((2, groups, mixing, TILE), BF16),
            pltpu.VMEM((2, groups, hid * GROUP, TILE), BF16),
            pltpu.VMEM((2, groups, heads * GROUP, TILE), F32),
            pltpu.VMEM((2, groups, hid * GROUP, TILE), BF16),
            pltpu.VMEM((2, heads * UNIT, TILE), BF16),
            pltpu.VMEM((slots, width), F32),
            pltpu.VMEM((2, own_rows // UNIT, 128), jnp.int32),
            pltpu.SMEM((2, own_rows // UNIT, 128), jnp.int32),
        ],
        compiler_params=pltpu.CompilerParams(vmem_limit_bytes=63 * 1024 * 1024),
        name="attend",
    )(pair, keys, w_query, w_key, w_value, first, second)

    encoded = pl.pallas_call(
        functools.partial(finish_kernel, cube),
        out_shape=jax.ShapeDtypeStruct((slots, width), BF16),
        in_specs=[free] * 4,
        out_specs=vmem,
        scratch_shapes=[
            pltpu.VMEM((slots, width), BF16),
            pltpu.VMEM((heads, slots), F32),
            pltpu.VMEM((slots, width), BF16),
            pltpu.VMEM((heads, slots), F32),
            pltpu.VMEM((width, width), BF16),
            pltpu.VMEM((1, width), F32),
            dma((2,)),
            dma((2,)),
            dma((4,)),
        ],
        compiler_params=pltpu.CompilerParams(collective_id=1, has_side_effects=True),
        name="finish",
    )(part, level, w_out, post_gain[None])
    return encoded[None]


def solution(mesh):
    in_specs = (
        P("grp", None, "blk", None),
        P("grp", None, None, "blk"),
        P("grp", "blk"),
        P("grp", "blk"),
        P(),
        P(),
        P(),
        P(),
        P(),
        P(),
        P(),
        P(),
        P(),
    )
    out_specs = P("grp", "blk", None)
    cube = (2, 4, mesh.shape["blk"] // 8)
    body = functools.partial(shards, mesh.shape["grp"], cube)
    return jax.shard_map(body, mesh=mesh, in_specs=in_specs, out_specs=out_specs, check_vma=False)
```

```python
import functools
import math

import jax
import jax.numpy as jnp
from jax import lax
from jax.experimental import pallas as pl
from jax.experimental.pallas import tpu as pltpu
from jax.sharding import PartitionSpec as P

MESH = pl.DeviceIdType.MESH
F32 = jnp.float32
BF16 = jnp.bfloat16
HIGHEST = lax.Precision.HIGHEST

KIN_ROWS = 16
GROUP = 8
UNIT = 16
TILE = 256
LANES = 128
SCORE_STEPS = 6
VALUE_STEPS = 8

GELU_A = math.sqrt(2.0 / math.pi)
GELU_B = GELU_A * 0.044715
GELU_S = GELU_B ** (-1.0 / 3.0)
ALPHA = GELU_A * GELU_S
LOG2E = 1.0 / math.log(2.0)


def layer_norm(rows, gain):
    center = rows - jnp.mean(rows, axis=-1, keepdims=True)
    spread = jnp.mean(center * center, axis=-1, keepdims=True)
    return center * lax.rsqrt(spread + 1e-05) * gain


def mesh_place(cube):
    _, ny, nx = cube
    b = lax.axis_index("blk")
    return b // (ny * nx), lax.rem(b // nx, ny), lax.rem(b, nx)


def exchange_kernel(
    n_grp,
    cube,
    raw_ref,
    kin_hbm,
    reader_hbm,
    event_hbm,
    gain_hbm,
    w1_hbm,
    b1_hbm,
    w2t_hbm,
    pair_ref,
    keys_ref,
    first_hbm,
    second_hbm,
    kin_ref,
    reader_ref,
    event_ref,
    gain_ref,
    w1_ref,
    b1_ref,
    w2t_ref,
    wfirst,
    wsecond,
    load_sem,
    inbox,
    kin_send,
    kin_in,
    block,
    mine,
    theirs,
    got,
    send_sem,
    recv_sem,
    kin_send_sem,
    kin_recv_sem,
    link_send,
    link_recv,
    own_sem,
):
    nz, ny, nx = cube
    g = lax.axis_index("grp")
    z, y, x = mesh_place(cube)
    slots = raw_ref.shape[2]
    width = raw_ref.shape[3]
    half = slots // nz
    body = half * (width // 128)

    def blk(z, y, x):
        return {"blk": (z * ny + y) * nx + x}

    partners = [{"grp": lax.rem(g + k, n_grp)} for k in range(1, n_grp)]
    turns = (1, nx - 1, 2)
    x_peers = [blk(z, y, lax.rem(x + k, nx)) for k in turns]
    y_peers = [blk(z, lax.rem(y + k, ny), x) for k in turns]
    near = blk(1 - z, y, x)
    partners += [near] + x_peers + y_peers
    barrier = pltpu.get_barrier_semaphore()
    for partner in partners:
        pl.semaphore_signal(barrier, inc=1, device_id=partner, device_id_type=MESH)
    loads = [
        pltpu.make_async_copy(src, dst, load_sem.at[i])
        for i, (src, dst) in enumerate(
            [
                (kin_hbm, kin_ref),
                (reader_hbm, reader_ref),
                (event_hbm, event_ref),
                (gain_hbm, gain_ref),
                (w1_hbm, w1_ref),
                (b1_hbm, b1_ref),
                (w2t_hbm, w2t_ref),
                (raw_ref.at[0, g], inbox.at[0]),
            ]
        )
    ]
    for load in loads:
        load.start()
    loads[0].wait()
    kin_send[...] = jnp.zeros_like(kin_send)
    for k in range(n_grp):
        kin_send[k, 0:4, :] = kin_ref[0, k].astype(F32)
    pl.semaphore_wait(barrier, len(partners))

    copies = []
    for k in range(1, n_grp):
        to = lax.rem(g + k, n_grp)
        for src, dst, ssem, rsem in (
            (raw_ref.at[0, to], inbox.at[n_grp - k], send_sem, recv_sem),
            (kin_send.at[to], kin_in.at[n_grp - k], kin_send_sem, kin_recv_sem),
        ):
            copy = pltpu.make_async_remote_copy(
                src_ref=src,
                dst_ref=dst,
                send_sem=ssem.at[k],
                recv_sem=rsem.at[n_grp - k],
                device_id={"grp": to},
                device_id_type=MESH,
            )
            copy.start()
            copies.append(copy)

    for load in loads[1:]:
        load.wait()
    pair_weights(w1_ref[...], b1_ref[...], w2t_ref[...], width // w2t_ref.shape[0], wfirst, wsecond)
    wanted = lax.rem(reader_ref[...] - g + n_grp, n_grp)
    stores = [
        pltpu.make_async_copy(wfirst, first_hbm, load_sem.at[0]),
        pltpu.make_async_copy(wsecond, second_hbm, load_sem.at[1]),
    ]
    for store in stores:
        store.start()
    column = jnp.broadcast_to(wanted, (slots, slots)).T
    kin = jnp.where(wanted == 0, kin_send[g, 0:4, :], 0.0)
    sides = [
        jnp.where(column == 0, inbox[0][:, h : h + slots].astype(F32), 0.0)
        for h in range(0, width, slots)
    ]
    for copy in copies:
        copy.wait_recv()
    for k in range(1, n_grp):
        kin = kin + jnp.where(wanted == k, kin_in[k, 0:4, :], 0.0)
        sides = [
            side
            + jnp.where(column == k, inbox[k][:, i * slots : (i + 1) * slots].astype(F32), 0.0)
            for i, side in enumerate(sides)
        ]
    tokens = jnp.concatenate(sides, axis=1)
    normed = layer_norm(tokens, gain_ref[...]).astype(BF16)
    block[0:slots, :] = normed
    tail = jnp.concatenate(
        [kin, event_ref[...].astype(F32), jnp.zeros((KIN_ROWS - 5, slots), F32)], axis=0
    )
    block[slots : slots + KIN_ROWS, :] = jnp.concatenate([tail, tail], axis=1).astype(BF16)
    for ref, low in ((mine, z == 0), (theirs, z == 1)):
        for i in range(width // 128):
            cols = slice(i * 128, (i + 1) * 128)
            ref[i * half : (i + 1) * half, :] = jnp.where(
                low, normed[0:half, cols], normed[half : 2 * half, cols]
            )
    theirs[body : body + KIN_ROWS, :] = tail.astype(BF16)

    def push(slot, src, dst, to):
        copy = pltpu.make_async_remote_copy(
            src_ref=src,
            dst_ref=dst,
            send_sem=link_send.at[slot],
            recv_sem=link_recv.at[slot],
            device_id=to,
            device_id_type=MESH,
        )
        copy.start()
        return copy

    rows = pl.ds(0, body)
    swap = push(0, theirs, got, near)
    own_x = [push(1 + i, mine, keys_ref.at[y, x, z, rows], to) for i, to in enumerate(x_peers)]
    moves = [push(4 + i, mine, keys_ref.at[y, x, z, rows], to) for i, to in enumerate(y_peers)]
    here = [
        pltpu.make_async_copy(mine, keys_ref.at[y, x, z, rows], own_sem.at[0]),
        pltpu.make_async_copy(block, pair_ref.at[z], own_sem.at[1]),
    ]
    for copy in here:
        copy.start()
    swap.wait_recv()
    ends = got[body : body + KIN_ROWS, :].astype(F32)
    ends = jnp.concatenate([ends[:, half:], ends[:, :half]], axis=1)
    side = lax.broadcasted_iota(jnp.int32, (KIN_ROWS, slots), 1) // half
    got[body : body + KIN_ROWS, :] = jnp.where(side == z, tail, ends).astype(BF16)
    other_y = [push(7 + i, got, keys_ref.at[y, x, 1 - z], to) for i, to in enumerate(y_peers)]
    moves += [push(10 + i, got, keys_ref.at[y, x, 1 - z], to) for i, to in enumerate(x_peers)]
    here.append(pltpu.make_async_copy(got, keys_ref.at[y, x, 1 - z], own_sem.at[2]))
    here[-1].start()
    moves.append(push(13, block, pair_ref.at[z], near))
    slot = 14
    for i, k in enumerate(turns):
        own_x[i].wait_recv()
        piece = keys_ref.at[y, lax.rem(x - k + nx, nx), z, rows]
        for to in y_peers:
            moves.append(push(slot, piece, piece, to))
            slot += 1
    for i, k in enumerate(turns):
        other_y[i].wait_recv()
        piece = keys_ref.at[lax.rem(y - k + ny, ny), x, 1 - z]
        for to in x_peers:
            moves.append(push(slot, piece, piece, to))
            slot += 1
    for copy in here + stores:
        copy.wait()
    for copy in copies + [swap] + own_x + other_y:
        copy.wait_send()
    for copy in moves:
        copy.wait()


def split_two(value):
    high = value.astype(BF16)
    low = (value - high.astype(F32)).astype(BF16)
    return high, low


def spread_over(weight):
    m, c = weight.shape
    up = (
        lax.broadcasted_iota(jnp.int32, (m * GROUP, m), 0) // GROUP
        == lax.broadcasted_iota(jnp.int32, (m * GROUP, m), 1)
    ).astype(F32)
    across = (
        lax.broadcasted_iota(jnp.int32, (c, c * GROUP), 1) // GROUP
        == lax.broadcasted_iota(jnp.int32, (c, c * GROUP), 0)
    ).astype(F32)
    tall = jnp.dot(up, weight, precision=HIGHEST, preferred_element_type=F32)
    wide = jnp.dot(tall, across, precision=HIGHEST, preferred_element_type=F32)
    same = (
        lax.broadcasted_iota(jnp.int32, (m * GROUP, c * GROUP), 0) % GROUP
        == lax.broadcasted_iota(jnp.int32, (m * GROUP, c * GROUP), 1) % GROUP
    )
    return jnp.where(same, wide, 0.0)


def pair_weights(w1, b1, w2t, head_size, wfirst, wsecond):
    feats, hid = w1.shape
    root = math.sqrt(head_size)
    first = jnp.concatenate([w1, b1, jnp.zeros((8 - feats - 1, hid), F32)], axis=0)
    line = lax.dot_general(
        w2t, first, (((1,), (1,)), ((), ())), precision=HIGHEST, preferred_element_type=F32
    ) * (0.5 * root)
    part = feats * GROUP

    stacked = jnp.concatenate([first.T * (1.0 / GELU_S), line], axis=0)
    high, low = split_two(spread_over(stacked))
    wfirst[:, 0:part] = high[:, 0:part]
    wfirst[:, part : 2 * part] = high[:, 0:part]
    wfirst[:, 2 * part : 3 * part] = low[:, 0:part]
    wfirst[:, 3 * part : 3 * part + GROUP] = high[:, part : part + GROUP]
    wfirst[:, 3 * part + GROUP : 3 * part + 2 * GROUP] = low[:, part : part + GROUP]
    wsecond[...] = spread_over(w2t * (0.5 * root * GELU_S)).astype(BF16)


def attend_kernel(
    heads,
    pair_hbm,
    keys_hbm,
    wq_hbm,
    wk_hbm,
    wv_hbm,
    first_hbm,
    second_hbm,
    keep_hbm,
    send_hbm,
    pair_ref,
    keys_ref,
    wq_ref,
    wk_ref,
    wv_ref,
    wfirst,
    wsecond,
    load_sem,
    kt_ref,
    v_ref,
    terms,
    q_terms,
    qm_ref,
    s_ref,
    top_ref,
    total_ref,
    acc_ref,
    fresh,
    hidden,
    linear,
    turned,
    weight_ref,
    held_ref,
    ranges,
    limits,
):
    loads = [
        pltpu.make_async_copy(src, dst, load_sem.at[i])
        for i, (src, dst) in enumerate(
            [
                (keys_hbm, keys_ref),
                (pair_hbm, pair_ref),
                (wk_hbm, wk_ref),
                (wv_hbm, wv_ref),
                (wq_hbm, wq_ref),
                (first_hbm, wfirst),
                (second_hbm, wsecond),
            ]
        )
    ]
    for load in loads:
        load.start()
    nz, slots, width = held_ref.shape[0], held_ref.shape[1] - 2 * heads, held_ref.shape[2]
    ny, nx = keys_ref.shape[0:2]
    half = slots // nz
    own_rows = nz * slots
    head_size = width // heads
    hid = wsecond.shape[1] // GROUP
    root = math.sqrt(head_size)
    groups = UNIT // GROUP
    rows_g = heads * GROUP
    rows_u = groups * rows_g
    n_units = own_rows // UNIT
    n_tiles = nz * ny
    per_step = TILE // LANES
    z = lax.axis_index("blk") // (ny * nx)

    for load in loads[0:2]:
        load.wait()

    def terms_of(mom, rap, azi, mass, ids):
        trans = jnp.sqrt(mom * mom + mass * mass)
        return (
            mom,
            rap,
            jnp.cos(azi),
            jnp.sin(azi),
            trans * jnp.exp(rap),
            trans * jnp.exp(-rap),
            mass * mass,
            ids,
        )

    body = half * (width // 128)
    lower = lax.broadcasted_iota(jnp.int32, (KIN_ROWS, 128), 1) < half
    ends = [[] for _ in range(nz)]
    for yy in range(ny):
        tails = [
            keys_ref[yy, xx, 1 - z, body : body + KIN_ROWS, :].astype(F32) for xx in range(nx)
        ]
        turned_tails = [jnp.concatenate([e[:, half:], e[:, :half]], axis=1) for e in tails]
        ends[0].append(
            [jnp.where(lower, tails[k], turned_tails[k + 1]) for k in range(0, nx, 2)]
        )
        ends[1].append(
            [jnp.where(lower, turned_tails[k], tails[k + 1]) for k in range(0, nx, 2)]
        )
    ends = [jnp.concatenate(end, axis=1) for zz in range(nz) for end in ends[zz]]
    raw_terms = [jnp.concatenate([end[i : i + 1] for end in ends], axis=0) for i in range(5)]
    n_rows = n_tiles * TILE // LANES
    raw_terms = [
        jnp.concatenate(
            [
                term[t : t + 1, k : k + LANES]
                for t in range(n_tiles)
                for k in range(0, TILE, LANES)
            ],
            axis=0,
        )
        for term in raw_terms
    ]
    for i, term in enumerate(terms_of(*raw_terms)):
        terms[i, 0:n_rows, :] = term
        terms[i, n_rows : n_rows + 8, :] = jnp.full((8, LANES), -1.0 if i == 7 else 1.0, F32)
    ends = [pair_ref[zz, slots : slots + KIN_ROWS, 0:slots].astype(F32) for zz in range(nz)]
    raw_terms = [
        jnp.concatenate([ends[zz][i : i + 1] for zz in range(nz)], axis=0) for i in range(5)
    ]
    for i, term in enumerate(terms_of(*raw_terms)):
        for zz in range(nz):
            q_terms[i, zz * slots : (zz + 1) * slots, :] = jnp.broadcast_to(
                term[zz : zz + 1], (slots, slots)
            ).T

    counts = []
    for row in (0, UNIT - 1):
        bound = q_terms[7, pl.ds(row, n_units, stride=UNIT), :]
        count = jnp.zeros((n_units, 128), F32)
        for t in range(n_rows):
            key = terms[7, t : t + 1, :]
            count = count + jnp.where(key < bound if row == 0 else key <= bound, 1.0, 0.0)
        counts.append(jnp.sum(count, axis=1, keepdims=True).astype(jnp.int32))
    start = jnp.minimum(counts[0] // LANES, n_rows - 1)
    stop = jnp.maximum((counts[1] + (LANES - 1)) // LANES, start + 1)
    ranges[0] = start + jnp.zeros((n_units, 128), jnp.int32)
    ranges[1] = (stop - start + (per_step - 1)) // per_step + jnp.zeros((n_units, 128), jnp.int32)
    to_scalars = pltpu.make_async_copy(ranges, limits, load_sem.at[7])
    to_scalars.start()

    for load in loads[2:]:
        load.wait()
    wkt = wk_ref[...].astype(F32).T.astype(BF16)
    for yy in range(ny):
        for zz in range(nz):
            rows = jnp.concatenate(
                [
                    jnp.concatenate(
                        [keys_ref[yy, xx, zz, i : i + half, :] for i in range(0, body, half)],
                        axis=1,
                    )
                    for xx in range(nx)
                ],
                axis=0,
            )
            at = slice((zz * ny + yy) * TILE, (zz * ny + yy + 1) * TILE)
            kt_ref[:, at] = lax.dot_general(
                wkt, rows, (((1,), (1,)), ((), ())), preferred_element_type=F32
            ).astype(BF16)
            v_ref[at, :] = jnp.dot(rows, wv_ref[...], preferred_element_type=F32).astype(BF16)

    kt_ref[:, n_tiles * TILE :] = jnp.zeros((width, LANES), BF16)
    v_ref[n_tiles * TILE :, :] = jnp.zeros((LANES, width), BF16)

    lane_head = lax.broadcasted_iota(jnp.int32, (GROUP, width), 1) // head_size
    for zz in range(nz):
        queries = jnp.dot(pair_ref[zz, 0:slots, :], wq_ref[...], preferred_element_type=F32)
        for base in range(0, slots, GROUP):
            rows = queries[base : base + GROUP]
            at = (zz * slots + base) * heads
            qm_ref[at : at + rows_g, :] = jnp.concatenate(
                [jnp.where(lane_head == h, rows, 0.0) for h in range(heads)], axis=0
            ).astype(BF16)

    top_ref[...] = jnp.full_like(top_ref, -1e30)
    total_ref[...] = jnp.zeros_like(total_ref)
    acc_ref[...] = jnp.zeros_like(acc_ref)

    to_scalars.wait()

    def following(u, k):
        more = k + 1 < limits[1, u, 0]
        return jnp.where(more, u, jnp.minimum(u + 1, n_units - 1)), jnp.where(more, k + 1, 0)

    steps = limits[1, 0, 0]
    for u in range(1, n_units):
        steps = steps + limits[1, u, 0]

    def place(u, k):
        return limits[0, u, 0] + k * per_step

    def features(p, u, k):
        t = place(u, k)
        for g in range(groups):
            base = pl.multiple_of(u * UNIT + g * GROUP, GROUP)
            qt = [q_terms[i, pl.ds(base, GROUP), :] for i in range(7)]
            columns = []
            for i in range(per_step):
                kt = [terms[j, pl.ds(t + i, 1), :] for j in range(7)]
                gap = qt[1] - kt[1]
                cos_gap = qt[2] * kt[2] + qt[3] * kt[3]
                dist = gap * gap + (2.0 - 2.0 * cos_gap)
                small = jnp.minimum(qt[0], kt[0])
                msq = (
                    qt[6]
                    + kt[6]
                    + (qt[4] * kt[5] + qt[5] * kt[4] - 2.0 * (qt[0] * kt[0] * cos_gap))
                )
                f = [
                    jnp.log(1.0 + dist),
                    jnp.log(1.0 + small * small * dist),
                    small / (qt[0] + kt[0]),
                    jnp.log(1.0 + msq),
                ]
                fh, fl = split_two(jnp.concatenate(f, axis=0))
                columns.append(
                    jnp.concatenate([fh, fl, fh, jnp.ones((2 * GROUP, 128), BF16)], axis=0)
                )
            fresh[p, g] = jnp.concatenate(columns, axis=1)

    def hiddens(p):
        for g in range(groups):
            z = jnp.dot(wfirst[...], fresh[p, g], preferred_element_type=F32)
            hidden[p, g] = z[0 : hid * GROUP].astype(BF16)
            linear[p, g] = z[hid * GROUP :]

    def gelus(p):
        for g in range(groups):
            inner = hidden[p, g]
            turned[p, g] = inner * jnp.tanh(inner * (ALPHA + inner * inner))

    def scores(p, u, k, away):
        t = place(u, k)
        start = pl.multiple_of(t * LANES, LANES)
        first_row = pl.multiple_of(u * rows_u, rows_u)
        products = jnp.dot(
            qm_ref[pl.ds(first_row, rows_u), :],
            kt_ref[:, pl.ds(start, TILE)],
            preferred_element_type=F32,
        )
        for g in range(groups):
            base = pl.multiple_of(u * UNIT + g * GROUP, GROUP)
            bias = jnp.dot(wsecond[...], turned[p, g], preferred_element_type=F32)
            s = products[g * rows_g : (g + 1) * rows_g] + (bias + linear[p, g])
            own = q_terms[7, pl.ds(base, GROUP), :] + away
            live = jnp.concatenate(
                [own == terms[7, pl.ds(t + i, 1), :] for i in range(per_step)], axis=1
            )
            s = jnp.where(live[None], s.reshape(heads, GROUP, TILE), -1e30).reshape(rows_g, TILE)
            at = pl.ds(pl.multiple_of(first_row + g * rows_g, rows_g), rows_g)
            s_ref[at, pl.ds(start, TILE)] = s
            run_max = top_ref[at, :]
            for i in range(0, TILE, 128):
                run_max = jnp.maximum(run_max, s[:, i : i + 128])
            top_ref[at, :] = run_max

    def score_steps(i, carry):
        for k in range(SCORE_STEPS):
            p = k % 2
            u0, t0, u1, t1, u2, t2, u3, t3 = carry
            scores(1 - p, u3, t3, jnp.where(SCORE_STEPS * i + k >= 3, 0.0, 100.0))
            hiddens(1 - p)
            gelus(p)
            features(p, u0, t0)
            carry = (*following(u0, t0), u0, t0, u1, t1, u2, t2)
        return carry

    zero = jnp.int32(0)
    lax.fori_loop(0, (steps + SCORE_STEPS + 2) // SCORE_STEPS, score_steps, (zero,) * 8)

    for u in range(n_units):
        at = slice(u * rows_u, (u + 1) * rows_u)
        top_ref[at, :] = jnp.broadcast_to(
            jnp.max(top_ref[at, :], axis=1, keepdims=True), (rows_u, 128)
        )

    weight_ref[...] = jnp.zeros_like(weight_ref)

    def apply(p, u, k):
        at = pl.ds(pl.multiple_of(u * rows_u, rows_u), rows_u)
        acc_ref[at, :] += jnp.dot(
            weight_ref[p],
            v_ref[pl.ds(pl.multiple_of(place(u, k) * LANES, LANES), TILE), :],
            preferred_element_type=F32,
        )

    def weigh(p, u, k, above):
        t = place(u, k)
        at = pl.ds(pl.multiple_of(u * rows_u, rows_u), rows_u)
        top = top_ref[at, :] + above
        total = total_ref[at, :]
        for i in range(0, TILE, 128):
            cols = pl.ds(pl.multiple_of(t * LANES + i, 128), 128)
            weight = jnp.exp2((s_ref[at, cols] - top) * (LOG2E / root))
            total = total + weight
            weight_ref[p, :, i : i + 128] = weight.astype(BF16)
        total_ref[at, :] = total

    def value_steps(i, carry):
        for k in range(VALUE_STEPS):
            u0, t0, u1, t1 = carry
            apply(1 - k % 2, u1, t1)
            weigh(k % 2, u0, t0, jnp.where(VALUE_STEPS * i + k < steps, 0.0, 1e32))
            carry = (*following(u0, t0), u0, t0)
        return carry

    lax.fori_loop(0, (steps + VALUE_STEPS) // VALUE_STEPS, value_steps, (zero,) * 4)

    lane = lax.broadcasted_iota(jnp.int32, (rows_g, slots), 1)
    row = lax.rem(lax.broadcasted_iota(jnp.int32, (rows_g, slots), 0), GROUP)
    for zz in range(nz):
        level = jnp.zeros((rows_g, slots), F32)
        for base in range(0, slots, GROUP):
            at = (zz * slots + base) * heads
            total = jnp.sum(total_ref[at : at + rows_g, :], axis=1, keepdims=True)
            level = jnp.where(
                lane == base + row,
                top_ref[at : at + rows_g, :] * (LOG2E / root) + jnp.log(total) * LOG2E,
                level,
            )
            total = 1.0 / total
            out = jnp.zeros((GROUP, width), F32)
            for h in range(heads):
                rows = slice(at + h * GROUP, at + (h + 1) * GROUP)
                scaled = acc_ref[rows, :] * total[h * GROUP : (h + 1) * GROUP]
                out = jnp.where(lane_head == h, scaled, out)
            acc_ref[base : base + GROUP, :] = out
        held_ref[zz, 0:slots, :] = acc_ref[0:slots, :].astype(BF16)
        level = jnp.sum(level.reshape(heads, GROUP, slots), axis=1)
        high, middle = split_two(level)
        low = (level - high.astype(F32) - middle.astype(F32)).astype(BF16)
        held_ref[zz, slots : slots + 2 * heads, :] = jnp.concatenate(
            [
                jnp.concatenate([high, middle], axis=1),
                jnp.concatenate([low, jnp.zeros_like(low)], axis=1),
            ],
            axis=0,
        )
    stores = [
        pltpu.make_async_copy(held_ref.at[z], keep_hbm, load_sem.at[0]),
        pltpu.make_async_copy(held_ref.at[1 - z], send_hbm, load_sem.at[1]),
    ]
    for store in stores:
        store.start()
    for store in stores:
        store.wait()


def finish_kernel(
    heads,
    keep_ref,
    came_ref,
    wo_ref,
    gain_ref,
    out_ref,
):
    slots, width = out_ref.shape
    spread = (
        lax.broadcasted_iota(jnp.int32, (heads, width), 1) // (width // heads)
        == lax.broadcasted_iota(jnp.int32, (heads, width), 0)
    ).astype(F32)

    def level_of(ref):
        pieces = ref[slots : slots + 2 * heads, :].astype(F32)
        return pieces[0:heads, 0:slots] + pieces[0:heads, slots:] + pieces[heads:, 0:slots]

    share = 1.0 / (1.0 + jnp.exp2(level_of(came_ref) - level_of(keep_ref)))
    share = jnp.dot(share.T, spread, precision=HIGHEST, preferred_element_type=F32)
    theirs = came_ref[0:slots, :].astype(F32)
    attended = theirs + share * (keep_ref[0:slots, :].astype(F32) - theirs)
    mixed = jnp.dot(attended.astype(BF16), wo_ref[...], preferred_element_type=F32)
    out_ref[...] = layer_norm(mixed, gain_ref[...]).astype(BF16)


def shards(
    n_grp,
    cube,
    raw,
    raw_kin,
    reader,
    event_id,
    pre_gain,
    w_query,
    w_key,
    w_value,
    w_out,
    post_gain,
    pair_w1,
    pair_b1,
    pair_w2,
):
    slots, width = raw.shape[2], raw.shape[3]
    heads = pair_w2.shape[1]
    nz, ny, nx = cube
    vmem = pl.BlockSpec(memory_space=pltpu.VMEM)
    free = pl.BlockSpec(memory_space=pl.ANY)
    dma = pltpu.SemaphoreType.DMA
    tall = slots + KIN_ROWS
    part_rows = slots // nz * (width // 128) + KIN_ROWS
    feats, hid = pair_w1.shape
    mixing = (3 * feats + 2) * GROUP
    pair, keys, first, second = pl.pallas_call(
        functools.partial(exchange_kernel, n_grp, cube),
        out_shape=(
            jax.ShapeDtypeStruct((nz, tall, width), BF16),
            jax.ShapeDtypeStruct((ny, nx, nz, part_rows, 128), BF16),
            jax.ShapeDtypeStruct(((hid + heads) * GROUP, mixing), BF16),
            jax.ShapeDtypeStruct((heads * GROUP, hid * GROUP), BF16),
        ),
        in_specs=[free] * 8,
        out_specs=(free,) * 4,
        scratch_shapes=[
            pltpu.VMEM(raw_kin.shape, BF16),
            pltpu.VMEM(reader.shape, jnp.int32),
            pltpu.VMEM(event_id.shape, jnp.int32),
            pltpu.VMEM((1, width), F32),
            pltpu.VMEM((feats, hid), F32),
            pltpu.VMEM((1, hid), F32),
            pltpu.VMEM((heads, hid), F32),
            pltpu.VMEM(((hid + heads) * GROUP, mixing), BF16),
            pltpu.VMEM((heads * GROUP, hid * GROUP), BF16),
            dma((8,)),
            pltpu.VMEM((n_grp, slots, width), BF16),
            pltpu.VMEM((n_grp, 8, slots), F32),
            pltpu.VMEM((n_grp, 8, slots), F32),
            pltpu.VMEM((tall, width), BF16),
            pltpu.VMEM((part_rows - KIN_ROWS, 128), BF16),
            pltpu.VMEM((part_rows, 128), BF16),
            pltpu.VMEM((part_rows, 128), BF16),
            dma((n_grp,)),
            dma((n_grp,)),
            dma((n_grp,)),
            dma((n_grp,)),
            dma((32,)),
            dma((32,)),
            dma((3,)),
        ],
        compiler_params=pltpu.CompilerParams(collective_id=0, has_side_effects=True),
        name="exchange",
    )(
        raw,
        raw_kin,
        reader,
        event_id,
        pre_gain[None],
        pair_w1,
        pair_b1[None],
        pair_w2.T,
    )

    own_rows = nz * slots
    n_tiles = nz * ny
    groups = UNIT // GROUP
    rows_all = heads * own_rows
    keep, send = pl.pallas_call(
        functools.partial(attend_kernel, heads),
        out_shape=(jax.ShapeDtypeStruct((slots + 2 * heads, width), BF16),) * 2,
        in_specs=[free] * 7,
        out_specs=(free, free),
        scratch_shapes=[
            pltpu.VMEM((nz, tall, width), BF16),
            pltpu.VMEM((ny, nx, nz, part_rows, 128), BF16),
            pltpu.VMEM((width, width), BF16),
            pltpu.VMEM((width, width), BF16),
            pltpu.VMEM((width, width), BF16),
            pltpu.VMEM(((hid + heads) * GROUP, mixing), BF16),
            pltpu.VMEM((heads * GROUP, hid * GROUP), BF16),
            dma((8,)),
            pltpu.VMEM((width, n_tiles * TILE + LANES), BF16),
            pltpu.VMEM((n_tiles * TILE + LANES, width), BF16),
            pltpu.VMEM((8, n_tiles * TILE // LANES + 8, LANES), F32),
            pltpu.VMEM((8, own_rows, slots), F32),
            pltpu.VMEM((rows_all, width), BF16),
            pltpu.VMEM((rows_all, n_tiles * TILE + LANES), F32),
            pltpu.VMEM((rows_all, 128), F32),
            pltpu.VMEM((rows_all, 128), F32),
            pltpu.VMEM((rows_all, width), F32),
            pltpu.VMEM((2, groups, mixing, TILE), BF16),
            pltpu.VMEM((2, groups, hid * GROUP, TILE), BF16),
            pltpu.VMEM((2, groups, heads * GROUP, TILE), F32),
            pltpu.VMEM((2, groups, hid * GROUP, TILE), BF16),
            pltpu.VMEM((2, heads * UNIT, TILE), BF16),
            pltpu.VMEM((nz, slots + 2 * heads, width), BF16),
            pltpu.VMEM((2, own_rows // UNIT, 128), jnp.int32),
            pltpu.SMEM((2, own_rows // UNIT, 128), jnp.int32),
        ],
        compiler_params=pltpu.CompilerParams(vmem_limit_bytes=63 * 1024 * 1024),
        name="attend",
    )(pair, keys, w_query, w_key, w_value, first, second)

    n_blk = nz * ny * nx
    swap = [(i, (i + ny * nx) % n_blk) for i in range(n_blk)]
    came = lax.ppermute(send, "blk", swap)
    encoded = pl.pallas_call(
        functools.partial(finish_kernel, heads),
        out_shape=jax.ShapeDtypeStruct((slots, width), BF16),
        in_specs=[vmem] * 4,
        out_specs=vmem,
        compiler_params=pltpu.CompilerParams(vmem_limit_bytes=8 * 1024 * 1024),
        name="finish",
    )(keep, came, w_out, post_gain[None])
    return encoded[None]


def solution(mesh):
    in_specs = (
        P("grp", None, "blk", None),
        P("grp", None, None, "blk"),
        P("grp", "blk"),
        P("grp", "blk"),
        P(),
        P(),
        P(),
        P(),
        P(),
        P(),
        P(),
        P(),
        P(),
    )
    out_specs = P("grp", "blk", None)
    cube = (2, 4, mesh.shape["blk"] // 8)
    body = functools.partial(shards, mesh.shape["grp"], cube)
    return jax.shard_map(body, mesh=mesh, in_specs=in_specs, out_specs=out_specs, check_vma=False)
```

```python
import functools
import math

import jax
import jax.numpy as jnp
from jax import lax
from jax.experimental import pallas as pl
from jax.experimental.pallas import tpu as pltpu
from jax.sharding import PartitionSpec as P

MESH = pl.DeviceIdType.MESH
F32 = jnp.float32
BF16 = jnp.bfloat16
HIGHEST = lax.Precision.HIGHEST

KIN_ROWS = 16
GROUP = 8
UNIT = 16
TILE = 256
LANES = 128
SCORE_STEPS = 6
VALUE_STEPS = 8

GELU_A = math.sqrt(2.0 / math.pi)
GELU_B = GELU_A * 0.044715
GELU_S = GELU_B ** (-1.0 / 3.0)
ALPHA = GELU_A * GELU_S
LOG2E = 1.0 / math.log(2.0)


def layer_norm(rows, gain):
    center = rows - jnp.mean(rows, axis=-1, keepdims=True)
    spread = jnp.mean(center * center, axis=-1, keepdims=True)
    return center * lax.rsqrt(spread + 1e-05) * gain


def mesh_place(cube):
    _, ny, nx = cube
    b = lax.axis_index("blk")
    return b // (ny * nx), lax.rem(b // nx, ny), lax.rem(b, nx)


def exchange_kernel(
    n_grp,
    cube,
    raw_ref,
    kin_hbm,
    reader_hbm,
    event_hbm,
    gain_hbm,
    w1_hbm,
    b1_hbm,
    w2t_hbm,
    pair_ref,
    keys_ref,
    first_hbm,
    second_hbm,
    kin_ref,
    reader_ref,
    event_ref,
    gain_ref,
    w1_ref,
    b1_ref,
    w2t_ref,
    wfirst,
    wsecond,
    load_sem,
    inbox,
    kin_send,
    kin_in,
    block,
    mine,
    theirs,
    got,
    send_sem,
    recv_sem,
    kin_send_sem,
    kin_recv_sem,
    link_send,
    link_recv,
    own_sem,
):
    nz, ny, nx = cube
    g = lax.axis_index("grp")
    z, y, x = mesh_place(cube)
    slots = raw_ref.shape[2]
    width = raw_ref.shape[3]
    half = slots // nz
    body = half * (width // 128)

    def blk(z, y, x):
        return {"blk": (z * ny + y) * nx + x}

    partners = [{"grp": lax.rem(g + k, n_grp)} for k in range(1, n_grp)]
    turns = (1, nx - 1, 2)
    x_peers = [blk(z, y, lax.rem(x + k, nx)) for k in turns]
    y_peers = [blk(z, lax.rem(y + k, ny), x) for k in turns]
    near = blk(1 - z, y, x)
    partners += [near] + x_peers + y_peers
    barrier = pltpu.get_barrier_semaphore()
    for partner in partners:
        pl.semaphore_signal(barrier, inc=1, device_id=partner, device_id_type=MESH)
    loads = [
        pltpu.make_async_copy(src, dst, load_sem.at[i])
        for i, (src, dst) in enumerate(
            [
                (kin_hbm, kin_ref),
                (reader_hbm, reader_ref),
                (event_hbm, event_ref),
                (gain_hbm, gain_ref),
                (w1_hbm, w1_ref),
                (b1_hbm, b1_ref),
                (w2t_hbm, w2t_ref),
                (raw_ref.at[0, g], inbox.at[0]),
            ]
        )
    ]
    for load in loads:
        load.start()
    loads[0].wait()
    kin_send[...] = jnp.zeros_like(kin_send)
    for k in range(n_grp):
        kin_send[k, 0:4, :] = kin_ref[0, k].astype(F32)
    pl.semaphore_wait(barrier, len(partners))

    copies = []
    for k in range(1, n_grp):
        to = lax.rem(g + k, n_grp)
        for src, dst, ssem, rsem in (
            (raw_ref.at[0, to], inbox.at[n_grp - k], send_sem, recv_sem),
            (kin_send.at[to], kin_in.at[n_grp - k], kin_send_sem, kin_recv_sem),
        ):
            copy = pltpu.make_async_remote_copy(
                src_ref=src,
                dst_ref=dst,
                send_sem=ssem.at[k],
                recv_sem=rsem.at[n_grp - k],
                device_id={"grp": to},
                device_id_type=MESH,
            )
            copy.start()
            copies.append(copy)

    for load in loads[1:]:
        load.wait()
    pair_weights(w1_ref[...], b1_ref[...], w2t_ref[...], width // w2t_ref.shape[0], wfirst, wsecond)
    wanted = lax.rem(reader_ref[...] - g + n_grp, n_grp)
    stores = [
        pltpu.make_async_copy(wfirst, first_hbm, load_sem.at[0]),
        pltpu.make_async_copy(wsecond, second_hbm, load_sem.at[1]),
    ]
    for store in stores:
        store.start()
    column = jnp.broadcast_to(wanted, (slots, slots)).T
    kin = jnp.where(wanted == 0, kin_send[g, 0:4, :], 0.0)
    sides = [
        jnp.where(column == 0, inbox[0][:, h : h + slots].astype(F32), 0.0)
        for h in range(0, width, slots)
    ]
    for copy in copies:
        copy.wait_recv()
    for k in range(1, n_grp):
        kin = kin + jnp.where(wanted == k, kin_in[k, 0:4, :], 0.0)
        sides = [
            side
            + jnp.where(column == k, inbox[k][:, i * slots : (i + 1) * slots].astype(F32), 0.0)
            for i, side in enumerate(sides)
        ]
    tokens = jnp.concatenate(sides, axis=1)
    normed = layer_norm(tokens, gain_ref[...]).astype(BF16)
    block[0:slots, :] = normed
    tail = jnp.concatenate(
        [kin, event_ref[...].astype(F32), jnp.zeros((KIN_ROWS - 5, slots), F32)], axis=0
    )
    block[slots : slots + KIN_ROWS, :] = jnp.concatenate([tail, tail], axis=1).astype(BF16)
    for ref, low in ((mine, z == 0), (theirs, z == 1)):
        for i in range(width // 128):
            cols = slice(i * 128, (i + 1) * 128)
            ref[i * half : (i + 1) * half, :] = jnp.where(
                low, normed[0:half, cols], normed[half : 2 * half, cols]
            )
    theirs[body : body + KIN_ROWS, :] = tail.astype(BF16)

    def push(slot, src, dst, to):
        copy = pltpu.make_async_remote_copy(
            src_ref=src,
            dst_ref=dst,
            send_sem=link_send.at[slot],
            recv_sem=link_recv.at[slot],
            device_id=to,
            device_id_type=MESH,
        )
        copy.start()
        return copy

    rows = pl.ds(0, body)
    swap = push(0, theirs, got, near)
    own_x = [push(1 + i, mine, keys_ref.at[y, x, z, rows], to) for i, to in enumerate(x_peers)]
    moves = [push(4 + i, mine, keys_ref.at[y, x, z, rows], to) for i, to in enumerate(y_peers)]
    here = [
        pltpu.make_async_copy(mine, keys_ref.at[y, x, z, rows], own_sem.at[0]),
        pltpu.make_async_copy(block, pair_ref.at[z], own_sem.at[1]),
    ]
    for copy in here:
        copy.start()
    swap.wait_recv()
    ends = got[body : body + KIN_ROWS, :].astype(F32)
    ends = jnp.concatenate([ends[:, half:], ends[:, :half]], axis=1)
    side = lax.broadcasted_iota(jnp.int32, (KIN_ROWS, slots), 1) // half
    got[body : body + KIN_ROWS, :] = jnp.where(side == z, tail, ends).astype(BF16)
    other_y = [push(7 + i, got, keys_ref.at[y, x, 1 - z], to) for i, to in enumerate(y_peers)]
    moves += [push(10 + i, got, keys_ref.at[y, x, 1 - z], to) for i, to in enumerate(x_peers)]
    here.append(pltpu.make_async_copy(got, keys_ref.at[y, x, 1 - z], own_sem.at[2]))
    here[-1].start()
    moves.append(push(13, block, pair_ref.at[z], near))
    slot = 14
    for i, k in enumerate(turns):
        own_x[i].wait_recv()
        piece = keys_ref.at[y, lax.rem(x - k + nx, nx), z, rows]
        for to in y_peers:
            moves.append(push(slot, piece, piece, to))
            slot += 1
    for i, k in enumerate(turns):
        other_y[i].wait_recv()
        piece = keys_ref.at[lax.rem(y - k + ny, ny), x, 1 - z]
        for to in x_peers:
            moves.append(push(slot, piece, piece, to))
            slot += 1
    for copy in here + stores:
        copy.wait()
    for copy in copies + [swap] + own_x + other_y:
        copy.wait_send()
    for copy in moves:
        copy.wait()


def split_two(value):
    high = value.astype(BF16)
    low = (value - high.astype(F32)).astype(BF16)
    return high, low


def spread_over(weight):
    m, c = weight.shape
    up = (
        lax.broadcasted_iota(jnp.int32, (m * GROUP, m), 0) // GROUP
        == lax.broadcasted_iota(jnp.int32, (m * GROUP, m), 1)
    ).astype(F32)
    across = (
        lax.broadcasted_iota(jnp.int32, (c, c * GROUP), 1) // GROUP
        == lax.broadcasted_iota(jnp.int32, (c, c * GROUP), 0)
    ).astype(F32)
    tall = jnp.dot(up, weight, precision=HIGHEST, preferred_element_type=F32)
    wide = jnp.dot(tall, across, precision=HIGHEST, preferred_element_type=F32)
    same = (
        lax.broadcasted_iota(jnp.int32, (m * GROUP, c * GROUP), 0) % GROUP
        == lax.broadcasted_iota(jnp.int32, (m * GROUP, c * GROUP), 1) % GROUP
    )
    return jnp.where(same, wide, 0.0)


def pair_weights(w1, b1, w2t, head_size, wfirst, wsecond):
    feats, hid = w1.shape
    root = math.sqrt(head_size)
    first = jnp.concatenate([w1, b1, jnp.zeros((8 - feats - 1, hid), F32)], axis=0)
    line = lax.dot_general(
        w2t, first, (((1,), (1,)), ((), ())), precision=HIGHEST, preferred_element_type=F32
    ) * (0.5 * root)
    part = feats * GROUP

    stacked = jnp.concatenate([first.T * (1.0 / GELU_S), line], axis=0)
    high, low = split_two(spread_over(stacked))
    wfirst[:, 0:part] = high[:, 0:part]
    wfirst[:, part : 2 * part] = high[:, 0:part]
    wfirst[:, 2 * part : 3 * part] = low[:, 0:part]
    wfirst[:, 3 * part : 3 * part + GROUP] = high[:, part : part + GROUP]
    wfirst[:, 3 * part + GROUP : 3 * part + 2 * GROUP] = low[:, part : part + GROUP]
    wsecond[...] = spread_over(w2t * (0.5 * root * GELU_S)).astype(BF16)


def attend_kernel(
    heads,
    pair_hbm,
    keys_hbm,
    wq_hbm,
    wk_hbm,
    wv_hbm,
    first_hbm,
    second_hbm,
    keep_hbm,
    send_hbm,
    pair_ref,
    keys_ref,
    wq_ref,
    wk_ref,
    wv_ref,
    wfirst,
    wsecond,
    load_sem,
    kt_ref,
    v_ref,
    terms,
    q_terms,
    qm_ref,
    s_ref,
    top_ref,
    total_ref,
    acc_ref,
    fresh,
    hidden,
    linear,
    turned,
    weight_ref,
    held_ref,
    ranges,
    limits,
):
    loads = [
        pltpu.make_async_copy(src, dst, load_sem.at[i])
        for i, (src, dst) in enumerate(
            [
                (keys_hbm, keys_ref),
                (pair_hbm, pair_ref),
                (wk_hbm, wk_ref),
                (wv_hbm, wv_ref),
                (wq_hbm, wq_ref),
                (first_hbm, wfirst),
                (second_hbm, wsecond),
            ]
        )
    ]
    for load in loads:
        load.start()
    nz, slots, width = held_ref.shape[0], held_ref.shape[1] - 2 * heads, held_ref.shape[2]
    ny, nx = keys_ref.shape[0:2]
    half = slots // nz
    own_rows = nz * slots
    head_size = width // heads
    hid = wsecond.shape[1] // GROUP
    root = math.sqrt(head_size)
    groups = UNIT // GROUP
    rows_g = heads * GROUP
    rows_u = groups * rows_g
    n_units = own_rows // UNIT
    n_tiles = nz * ny
    per_step = TILE // LANES
    z = lax.axis_index("blk") // (ny * nx)

    for load in loads[0:2]:
        load.wait()

    def terms_of(mom, rap, azi, mass, ids):
        trans = jnp.sqrt(mom * mom + mass * mass)
        return (
            mom,
            rap,
            jnp.cos(azi),
            jnp.sin(azi),
            trans * jnp.exp(rap),
            trans * jnp.exp(-rap),
            mass * mass,
            ids,
        )

    body = half * (width // 128)
    lower = lax.broadcasted_iota(jnp.int32, (KIN_ROWS, 128), 1) < half
    ends = [[] for _ in range(nz)]
    for yy in range(ny):
        tails = [
            keys_ref[yy, xx, 1 - z, body : body + KIN_ROWS, :].astype(F32) for xx in range(nx)
        ]
        turned_tails = [jnp.concatenate([e[:, half:], e[:, :half]], axis=1) for e in tails]
        ends[0].append(
            [jnp.where(lower, tails[k], turned_tails[k + 1]) for k in range(0, nx, 2)]
        )
        ends[1].append(
            [jnp.where(lower, turned_tails[k], tails[k + 1]) for k in range(0, nx, 2)]
        )
    ends = [jnp.concatenate(end, axis=1) for zz in range(nz) for end in ends[zz]]
    raw_terms = [jnp.concatenate([end[i : i + 1] for end in ends], axis=0) for i in range(5)]
    n_rows = n_tiles * TILE // LANES
    raw_terms = [
        jnp.concatenate(
            [
                term[t : t + 1, k : k + LANES]
                for t in range(n_tiles)
                for k in range(0, TILE, LANES)
            ],
            axis=0,
        )
        for term in raw_terms
    ]
    for i, term in enumerate(terms_of(*raw_terms)):
        terms[i, 0:n_rows, :] = term
        terms[i, n_rows : n_rows + 8, :] = jnp.full((8, LANES), -1.0 if i == 7 else 1.0, F32)
    ends = [pair_ref[zz, slots : slots + KIN_ROWS, 0:slots].astype(F32) for zz in range(nz)]
    raw_terms = [
        jnp.concatenate([ends[zz][i : i + 1] for zz in range(nz)], axis=0) for i in range(5)
    ]
    for i, term in enumerate(terms_of(*raw_terms)):
        for zz in range(nz):
            q_terms[i, zz * slots : (zz + 1) * slots, :] = jnp.broadcast_to(
                term[zz : zz + 1], (slots, slots)
            ).T

    counts = []
    for row in (0, UNIT - 1):
        bound = q_terms[7, pl.ds(row, n_units, stride=UNIT), :]
        count = jnp.zeros((n_units, 128), F32)
        for t in range(n_rows):
            key = terms[7, t : t + 1, :]
            count = count + jnp.where(key < bound if row == 0 else key <= bound, 1.0, 0.0)
        counts.append(jnp.sum(count, axis=1, keepdims=True).astype(jnp.int32))
    start = jnp.minimum(counts[0] // LANES, n_rows - 1)
    stop = jnp.maximum((counts[1] + (LANES - 1)) // LANES, start + 1)
    ranges[0] = start + jnp.zeros((n_units, 128), jnp.int32)
    ranges[1] = (stop - start + (per_step - 1)) // per_step + jnp.zeros((n_units, 128), jnp.int32)
    to_scalars = pltpu.make_async_copy(ranges, limits, load_sem.at[7])
    to_scalars.start()

    for load in loads[2:]:
        load.wait()
    wkt = wk_ref[...].astype(F32).T.astype(BF16)
    for yy in range(ny):
        for zz in range(nz):
            rows = jnp.concatenate(
                [
                    jnp.concatenate(
                        [keys_ref[yy, xx, zz, i : i + half, :] for i in range(0, body, half)],
                        axis=1,
                    )
                    for xx in range(nx)
                ],
                axis=0,
            )
            at = slice((zz * ny + yy) * TILE, (zz * ny + yy + 1) * TILE)
            kt_ref[:, at] = lax.dot_general(
                wkt, rows, (((1,), (1,)), ((), ())), preferred_element_type=F32
            ).astype(BF16)
            v_ref[at, :] = jnp.dot(rows, wv_ref[...], preferred_element_type=F32).astype(BF16)

    kt_ref[:, n_tiles * TILE :] = jnp.zeros((width, LANES), BF16)
    v_ref[n_tiles * TILE :, :] = jnp.zeros((LANES, width), BF16)

    lane_head = lax.broadcasted_iota(jnp.int32, (GROUP, width), 1) // head_size
    for zz in range(nz):
        queries = jnp.dot(pair_ref[zz, 0:slots, :], wq_ref[...], preferred_element_type=F32)
        for base in range(0, slots, GROUP):
            rows = queries[base : base + GROUP]
            at = (zz * slots + base) * heads
            qm_ref[at : at + rows_g, :] = jnp.concatenate(
                [jnp.where(lane_head == h, rows, 0.0) for h in range(heads)], axis=0
            ).astype(BF16)

    top_ref[...] = jnp.full_like(top_ref, -1e30)
    total_ref[...] = jnp.zeros_like(total_ref)
    acc_ref[...] = jnp.zeros_like(acc_ref)

    to_scalars.wait()

    def following(u, k):
        more = k + 1 < limits[1, u, 0]
        return jnp.where(more, u, jnp.minimum(u + 1, n_units - 1)), jnp.where(more, k + 1, 0)

    steps = limits[1, 0, 0]
    for u in range(1, n_units):
        steps = steps + limits[1, u, 0]

    def place(u, k):
        return limits[0, u, 0] + k * per_step

    def features(p, u, k):
        t = place(u, k)
        for g in range(groups):
            base = pl.multiple_of(u * UNIT + g * GROUP, GROUP)
            qt = [q_terms[i, pl.ds(base, GROUP), :] for i in range(7)]
            columns = []
            for i in range(per_step):
                kt = [terms[j, pl.ds(t + i, 1), :] for j in range(7)]
                gap = qt[1] - kt[1]
                cos_gap = qt[2] * kt[2] + qt[3] * kt[3]
                dist = gap * gap + (2.0 - 2.0 * cos_gap)
                small = jnp.minimum(qt[0], kt[0])
                msq = (
                    qt[6]
                    + kt[6]
                    + (qt[4] * kt[5] + qt[5] * kt[4] - 2.0 * (qt[0] * kt[0] * cos_gap))
                )
                f = [
                    jnp.log(1.0 + dist),
                    jnp.log(1.0 + small * small * dist),
                    small / (qt[0] + kt[0]),
                    jnp.log(1.0 + msq),
                ]
                fh, fl = split_two(jnp.concatenate(f, axis=0))
                columns.append(
                    jnp.concatenate([fh, fl, fh, jnp.ones((2 * GROUP, 128), BF16)], axis=0)
                )
            fresh[p, g] = jnp.concatenate(columns, axis=1)

    def hiddens(p):
        for g in range(groups):
            z = jnp.dot(wfirst[...], fresh[p, g], preferred_element_type=F32)
            hidden[p, g] = z[0 : hid * GROUP].astype(BF16)
            linear[p, g] = z[hid * GROUP :]

    def gelus(p):
        for g in range(groups):
            inner = hidden[p, g]
            turned[p, g] = inner * jnp.tanh(inner * (ALPHA + inner * inner))

    def scores(p, u, k, away):
        t = place(u, k)
        start = pl.multiple_of(t * LANES, LANES)
        first_row = pl.multiple_of(u * rows_u, rows_u)
        products = jnp.dot(
            qm_ref[pl.ds(first_row, rows_u), :],
            kt_ref[:, pl.ds(start, TILE)],
            preferred_element_type=F32,
        )
        for g in range(groups):
            base = pl.multiple_of(u * UNIT + g * GROUP, GROUP)
            bias = jnp.dot(wsecond[...], turned[p, g], preferred_element_type=F32)
            s = products[g * rows_g : (g + 1) * rows_g] + (bias + linear[p, g])
            own = q_terms[7, pl.ds(base, GROUP), :] + away
            live = jnp.concatenate(
                [own == terms[7, pl.ds(t + i, 1), :] for i in range(per_step)], axis=1
            )
            s = jnp.where(live[None], s.reshape(heads, GROUP, TILE), -1e30).reshape(rows_g, TILE)
            at = pl.ds(pl.multiple_of(first_row + g * rows_g, rows_g), rows_g)
            s_ref[at, pl.ds(start, TILE)] = s
            run_max = top_ref[at, :]
            for i in range(0, TILE, 128):
                run_max = jnp.maximum(run_max, s[:, i : i + 128])
            top_ref[at, :] = run_max

    def score_steps(i, carry):
        for k in range(SCORE_STEPS):
            p = k % 2
            u0, t0, u1, t1, u2, t2, u3, t3 = carry
            scores(1 - p, u3, t3, jnp.where(SCORE_STEPS * i + k >= 3, 0.0, 100.0))
            hiddens(1 - p)
            gelus(p)
            features(p, u0, t0)
            carry = (*following(u0, t0), u0, t0, u1, t1, u2, t2)
        return carry

    zero = jnp.int32(0)
    lax.fori_loop(0, (steps + SCORE_STEPS + 2) // SCORE_STEPS, score_steps, (zero,) * 8)

    for u in range(n_units):
        at = slice(u * rows_u, (u + 1) * rows_u)
        top_ref[at, :] = jnp.broadcast_to(
            jnp.max(top_ref[at, :], axis=1, keepdims=True), (rows_u, 128)
        )

    weight_ref[...] = jnp.zeros_like(weight_ref)

    def apply(p, u, k):
        at = pl.ds(pl.multiple_of(u * rows_u, rows_u), rows_u)
        acc_ref[at, :] += jnp.dot(
            weight_ref[p],
            v_ref[pl.ds(pl.multiple_of(place(u, k) * LANES, LANES), TILE), :],
            preferred_element_type=F32,
        )

    def weigh(p, u, k, above):
        t = place(u, k)
        at = pl.ds(pl.multiple_of(u * rows_u, rows_u), rows_u)
        top = top_ref[at, :] + above
        total = total_ref[at, :]
        for i in range(0, TILE, 128):
            cols = pl.ds(pl.multiple_of(t * LANES + i, 128), 128)
            weight = jnp.exp2((s_ref[at, cols] - top) * (LOG2E / root))
            total = total + weight
            weight_ref[p, :, i : i + 128] = weight.astype(BF16)
        total_ref[at, :] = total

    def value_steps(i, carry):
        for k in range(VALUE_STEPS):
            u0, t0, u1, t1 = carry
            apply(1 - k % 2, u1, t1)
            weigh(k % 2, u0, t0, jnp.where(VALUE_STEPS * i + k < steps, 0.0, 1e32))
            carry = (*following(u0, t0), u0, t0)
        return carry

    lax.fori_loop(0, (steps + VALUE_STEPS) // VALUE_STEPS, value_steps, (zero,) * 4)

    lane = lax.broadcasted_iota(jnp.int32, (rows_g, slots), 1)
    row = lax.rem(lax.broadcasted_iota(jnp.int32, (rows_g, slots), 0), GROUP)
    for zz in range(nz):
        level = jnp.zeros((rows_g, slots), F32)
        for base in range(0, slots, GROUP):
            at = (zz * slots + base) * heads
            total = jnp.sum(total_ref[at : at + rows_g, :], axis=1, keepdims=True)
            level = jnp.where(
                lane == base + row,
                top_ref[at : at + rows_g, :] * (LOG2E / root) + jnp.log(total) * LOG2E,
                level,
            )
            total = 1.0 / total
            out = jnp.zeros((GROUP, width), F32)
            for h in range(heads):
                rows = slice(at + h * GROUP, at + (h + 1) * GROUP)
                scaled = acc_ref[rows, :] * total[h * GROUP : (h + 1) * GROUP]
                out = jnp.where(lane_head == h, scaled, out)
            acc_ref[base : base + GROUP, :] = out
        held_ref[zz, 0:slots, :] = acc_ref[0:slots, :].astype(BF16)
        level = jnp.sum(level.reshape(heads, GROUP, slots), axis=1)
        high, middle = split_two(level)
        low = (level - high.astype(F32) - middle.astype(F32)).astype(BF16)
        held_ref[zz, slots : slots + 2 * heads, :] = jnp.concatenate(
            [
                jnp.concatenate([high, middle], axis=1),
                jnp.concatenate([low, jnp.zeros_like(low)], axis=1),
            ],
            axis=0,
        )
    stores = [
        pltpu.make_async_copy(held_ref.at[z], keep_hbm, load_sem.at[0]),
        pltpu.make_async_copy(held_ref.at[1 - z], send_hbm, load_sem.at[1]),
    ]
    for store in stores:
        store.start()
    for store in stores:
        store.wait()


def finish_kernel(
    heads,
    keep_ref,
    came_ref,
    wo_ref,
    gain_ref,
    out_ref,
):
    slots, width = out_ref.shape
    spread = (
        lax.broadcasted_iota(jnp.int32, (heads, width), 1) // (width // heads)
        == lax.broadcasted_iota(jnp.int32, (heads, width), 0)
    ).astype(F32)

    def level_of(ref):
        pieces = ref[slots : slots + 2 * heads, :].astype(F32)
        return pieces[0:heads, 0:slots] + pieces[0:heads, slots:] + pieces[heads:, 0:slots]

    share = 1.0 / (1.0 + jnp.exp2(level_of(came_ref) - level_of(keep_ref)))
    share = jnp.dot(share.T, spread, precision=HIGHEST, preferred_element_type=F32)
    theirs = came_ref[0:slots, :].astype(F32)
    attended = theirs + share * (keep_ref[0:slots, :].astype(F32) - theirs)
    mixed = jnp.dot(attended.astype(BF16), wo_ref[...], preferred_element_type=F32)
    out_ref[...] = layer_norm(mixed, gain_ref[...]).astype(BF16)


def shards(
    n_grp,
    cube,
    raw,
    raw_kin,
    reader,
    event_id,
    pre_gain,
    w_query,
    w_key,
    w_value,
    w_out,
    post_gain,
    pair_w1,
    pair_b1,
    pair_w2,
):
    slots, width = raw.shape[2], raw.shape[3]
    heads = pair_w2.shape[1]
    nz, ny, nx = cube
    vmem = pl.BlockSpec(memory_space=pltpu.VMEM)
    free = pl.BlockSpec(memory_space=pl.ANY)
    dma = pltpu.SemaphoreType.DMA
    tall = slots + KIN_ROWS
    part_rows = slots // nz * (width // 128) + KIN_ROWS
    feats, hid = pair_w1.shape
    mixing = (3 * feats + 2) * GROUP
    pair, keys, first, second = pl.pallas_call(
        functools.partial(exchange_kernel, n_grp, cube),
        out_shape=(
            jax.ShapeDtypeStruct((nz, tall, width), BF16),
            jax.ShapeDtypeStruct((ny, nx, nz, part_rows, 128), BF16),
            jax.ShapeDtypeStruct(((hid + heads) * GROUP, mixing), BF16),
            jax.ShapeDtypeStruct((heads * GROUP, hid * GROUP), BF16),
        ),
        in_specs=[free] * 8,
        out_specs=(free,) * 4,
        scratch_shapes=[
            pltpu.VMEM(raw_kin.shape, BF16),
            pltpu.VMEM(reader.shape, jnp.int32),
            pltpu.VMEM(event_id.shape, jnp.int32),
            pltpu.VMEM((1, width), F32),
            pltpu.VMEM((feats, hid), F32),
            pltpu.VMEM((1, hid), F32),
            pltpu.VMEM((heads, hid), F32),
            pltpu.VMEM(((hid + heads) * GROUP, mixing), BF16),
            pltpu.VMEM((heads * GROUP, hid * GROUP), BF16),
            dma((8,)),
            pltpu.VMEM((n_grp, slots, width), BF16),
            pltpu.VMEM((n_grp, 8, slots), F32),
            pltpu.VMEM((n_grp, 8, slots), F32),
            pltpu.VMEM((tall, width), BF16),
            pltpu.VMEM((part_rows - KIN_ROWS, 128), BF16),
            pltpu.VMEM((part_rows, 128), BF16),
            pltpu.VMEM((part_rows, 128), BF16),
            dma((n_grp,)),
            dma((n_grp,)),
            dma((n_grp,)),
            dma((n_grp,)),
            dma((32,)),
            dma((32,)),
            dma((3,)),
        ],
        compiler_params=pltpu.CompilerParams(collective_id=0, has_side_effects=True),
        name="exchange",
    )(
        raw,
        raw_kin,
        reader,
        event_id,
        pre_gain[None],
        pair_w1,
        pair_b1[None],
        pair_w2.T,
    )

    own_rows = nz * slots
    n_tiles = nz * ny
    groups = UNIT // GROUP
    rows_all = heads * own_rows
    keep, send = pl.pallas_call(
        functools.partial(attend_kernel, heads),
        out_shape=(jax.ShapeDtypeStruct((slots + 2 * heads, width), BF16),) * 2,
        in_specs=[free] * 7,
        out_specs=(free, free),
        scratch_shapes=[
            pltpu.VMEM((nz, tall, width), BF16),
            pltpu.VMEM((ny, nx, nz, part_rows, 128), BF16),
            pltpu.VMEM((width, width), BF16),
            pltpu.VMEM((width, width), BF16),
            pltpu.VMEM((width, width), BF16),
            pltpu.VMEM(((hid + heads) * GROUP, mixing), BF16),
            pltpu.VMEM((heads * GROUP, hid * GROUP), BF16),
            dma((8,)),
            pltpu.VMEM((width, n_tiles * TILE + LANES), BF16),
            pltpu.VMEM((n_tiles * TILE + LANES, width), BF16),
            pltpu.VMEM((8, n_tiles * TILE // LANES + 8, LANES), F32),
            pltpu.VMEM((8, own_rows, slots), F32),
            pltpu.VMEM((rows_all, width), BF16),
            pltpu.VMEM((rows_all, n_tiles * TILE + LANES), F32),
            pltpu.VMEM((rows_all, 128), F32),
            pltpu.VMEM((rows_all, 128), F32),
            pltpu.VMEM((rows_all, width), F32),
            pltpu.VMEM((2, groups, mixing, TILE), BF16),
            pltpu.VMEM((2, groups, hid * GROUP, TILE), BF16),
            pltpu.VMEM((2, groups, heads * GROUP, TILE), F32),
            pltpu.VMEM((2, groups, hid * GROUP, TILE), BF16),
            pltpu.VMEM((2, heads * UNIT, TILE), BF16),
            pltpu.VMEM((nz, slots + 2 * heads, width), BF16),
            pltpu.VMEM((2, own_rows // UNIT, 128), jnp.int32),
            pltpu.SMEM((2, own_rows // UNIT, 128), jnp.int32),
        ],
        compiler_params=pltpu.CompilerParams(vmem_limit_bytes=63 * 1024 * 1024),
        name="attend",
    )(pair, keys, w_query, w_key, w_value, first, second)

    n_blk = nz * ny * nx
    swap = [(i, (i + ny * nx) % n_blk) for i in range(n_blk)]
    came = lax.ppermute(send, "blk", swap)
    encoded = pl.pallas_call(
        functools.partial(finish_kernel, heads),
        out_shape=jax.ShapeDtypeStruct((slots, width), BF16),
        in_specs=[vmem] * 4,
        out_specs=vmem,
        compiler_params=pltpu.CompilerParams(vmem_limit_bytes=8 * 1024 * 1024),
        name="finish",
    )(keep.astype(F32), came, w_out, post_gain[None])
    return encoded[None]


def solution(mesh):
    in_specs = (
        P("grp", None, "blk", None),
        P("grp", None, None, "blk"),
        P("grp", "blk"),
        P("grp", "blk"),
        P(),
        P(),
        P(),
        P(),
        P(),
        P(),
        P(),
        P(),
        P(),
    )
    out_specs = P("grp", "blk", None)
    cube = (2, 4, mesh.shape["blk"] // 8)
    body = functools.partial(shards, mesh.shape["grp"], cube)
    return jax.shard_map(body, mesh=mesh, in_specs=in_specs, out_specs=out_specs, check_vma=False)
```

```python
import functools
import math

import jax
import jax.numpy as jnp
from jax import lax
from jax.experimental import pallas as pl
from jax.experimental.pallas import tpu as pltpu
from jax.sharding import PartitionSpec as P

MESH = pl.DeviceIdType.MESH
F32 = jnp.float32
BF16 = jnp.bfloat16
HIGHEST = lax.Precision.HIGHEST

KIN_ROWS = 16
GROUP = 8
UNIT = 16
TILE = 256
LANES = 128
SCORE_STEPS = 6
VALUE_STEPS = 8

GELU_A = math.sqrt(2.0 / math.pi)
GELU_B = GELU_A * 0.044715
GELU_S = GELU_B ** (-1.0 / 3.0)
ALPHA = GELU_A * GELU_S
LOG2E = 1.0 / math.log(2.0)


def layer_norm(rows, gain):
    center = rows - jnp.mean(rows, axis=-1, keepdims=True)
    spread = jnp.mean(center * center, axis=-1, keepdims=True)
    return center * lax.rsqrt(spread + 1e-05) * gain


def mesh_place(cube):
    _, ny, nx = cube
    b = lax.axis_index("blk")
    return b // (ny * nx), lax.rem(b // nx, ny), lax.rem(b, nx)


def exchange_kernel(
    n_grp,
    cube,
    raw_ref,
    kin_hbm,
    reader_hbm,
    event_hbm,
    gain_hbm,
    w1_hbm,
    b1_hbm,
    w2t_hbm,
    pair_ref,
    keys_ref,
    first_hbm,
    second_hbm,
    kin_ref,
    reader_ref,
    event_ref,
    gain_ref,
    w1_ref,
    b1_ref,
    w2t_ref,
    wfirst,
    wsecond,
    load_sem,
    inbox,
    kin_send,
    kin_in,
    block,
    mine,
    theirs,
    got,
    send_sem,
    recv_sem,
    kin_send_sem,
    kin_recv_sem,
    link_send,
    link_recv,
    own_sem,
):
    nz, ny, nx = cube
    g = lax.axis_index("grp")
    z, y, x = mesh_place(cube)
    slots = raw_ref.shape[2]
    width = raw_ref.shape[3]
    half = slots // nz
    body = half * (width // 128)

    def blk(z, y, x):
        return {"blk": (z * ny + y) * nx + x}

    partners = [{"grp": lax.rem(g + k, n_grp)} for k in range(1, n_grp)]
    turns = (1, nx - 1, 2)
    x_peers = [blk(z, y, lax.rem(x + k, nx)) for k in turns]
    y_peers = [blk(z, lax.rem(y + k, ny), x) for k in turns]
    near = blk(1 - z, y, x)
    partners += [near] + x_peers + y_peers
    barrier = pltpu.get_barrier_semaphore()
    for partner in partners:
        pl.semaphore_signal(barrier, inc=1, device_id=partner, device_id_type=MESH)
    loads = [
        pltpu.make_async_copy(src, dst, load_sem.at[i])
        for i, (src, dst) in enumerate(
            [
                (kin_hbm, kin_ref),
                (reader_hbm, reader_ref),
                (event_hbm, event_ref),
                (gain_hbm, gain_ref),
                (w1_hbm, w1_ref),
                (b1_hbm, b1_ref),
                (w2t_hbm, w2t_ref),
                (raw_ref.at[0, g], inbox.at[0]),
            ]
        )
    ]
    for load in loads:
        load.start()
    loads[0].wait()
    kin_send[...] = jnp.zeros_like(kin_send)
    for k in range(n_grp):
        kin_send[k, 0:4, :] = kin_ref[0, k].astype(F32)
    pl.semaphore_wait(barrier, len(partners))

    copies = []
    for k in range(1, n_grp):
        to = lax.rem(g + k, n_grp)
        for src, dst, ssem, rsem in (
            (raw_ref.at[0, to], inbox.at[n_grp - k], send_sem, recv_sem),
            (kin_send.at[to], kin_in.at[n_grp - k], kin_send_sem, kin_recv_sem),
        ):
            copy = pltpu.make_async_remote_copy(
                src_ref=src,
                dst_ref=dst,
                send_sem=ssem.at[k],
                recv_sem=rsem.at[n_grp - k],
                device_id={"grp": to},
                device_id_type=MESH,
            )
            copy.start()
            copies.append(copy)

    for load in loads[1:]:
        load.wait()
    pair_weights(w1_ref[...], b1_ref[...], w2t_ref[...], width // w2t_ref.shape[0], wfirst, wsecond)
    wanted = lax.rem(reader_ref[...] - g + n_grp, n_grp)
    stores = [
        pltpu.make_async_copy(wfirst, first_hbm, load_sem.at[0]),
        pltpu.make_async_copy(wsecond, second_hbm, load_sem.at[1]),
    ]
    for store in stores:
        store.start()
    column = jnp.broadcast_to(wanted, (slots, slots)).T
    kin = jnp.where(wanted == 0, kin_send[g, 0:4, :], 0.0)
    sides = [
        jnp.where(column == 0, inbox[0][:, h : h + slots].astype(F32), 0.0)
        for h in range(0, width, slots)
    ]
    for copy in copies:
        copy.wait_recv()
    for k in range(1, n_grp):
        kin = kin + jnp.where(wanted == k, kin_in[k, 0:4, :], 0.0)
        sides = [
            side
            + jnp.where(column == k, inbox[k][:, i * slots : (i + 1) * slots].astype(F32), 0.0)
            for i, side in enumerate(sides)
        ]
    tokens = jnp.concatenate(sides, axis=1)
    normed = layer_norm(tokens, gain_ref[...]).astype(BF16)
    block[0:slots, :] = normed
    tail = jnp.concatenate(
        [kin, event_ref[...].astype(F32), jnp.zeros((KIN_ROWS - 5, slots), F32)], axis=0
    )
    block[slots : slots + KIN_ROWS, :] = jnp.concatenate([tail, tail], axis=1).astype(BF16)
    for ref, low in ((mine, z == 0), (theirs, z == 1)):
        for i in range(width // 128):
            cols = slice(i * 128, (i + 1) * 128)
            ref[i * half : (i + 1) * half, :] = jnp.where(
                low, normed[0:half, cols], normed[half : 2 * half, cols]
            )
    theirs[body : body + KIN_ROWS, :] = tail.astype(BF16)

    def push(slot, src, dst, to):
        copy = pltpu.make_async_remote_copy(
            src_ref=src,
            dst_ref=dst,
            send_sem=link_send.at[slot],
            recv_sem=link_recv.at[slot],
            device_id=to,
            device_id_type=MESH,
        )
        copy.start()
        return copy

    rows = pl.ds(0, body)
    swap = push(0, theirs, got, near)
    own_x = [push(1 + i, mine, keys_ref.at[y, x, z, rows], to) for i, to in enumerate(x_peers)]
    moves = [push(4 + i, mine, keys_ref.at[y, x, z, rows], to) for i, to in enumerate(y_peers)]
    here = [
        pltpu.make_async_copy(mine, keys_ref.at[y, x, z, rows], own_sem.at[0]),
        pltpu.make_async_copy(block, pair_ref.at[z], own_sem.at[1]),
    ]
    for copy in here:
        copy.start()
    swap.wait_recv()
    ends = got[body : body + KIN_ROWS, :].astype(F32)
    ends = jnp.concatenate([ends[:, half:], ends[:, :half]], axis=1)
    side = lax.broadcasted_iota(jnp.int32, (KIN_ROWS, slots), 1) // half
    got[body : body + KIN_ROWS, :] = jnp.where(side == z, tail, ends).astype(BF16)
    other_y = [push(7 + i, got, keys_ref.at[y, x, 1 - z], to) for i, to in enumerate(y_peers)]
    moves += [push(10 + i, got, keys_ref.at[y, x, 1 - z], to) for i, to in enumerate(x_peers)]
    here.append(pltpu.make_async_copy(got, keys_ref.at[y, x, 1 - z], own_sem.at[2]))
    here[-1].start()
    moves.append(push(13, block, pair_ref.at[z], near))
    slot = 14
    for i, k in enumerate(turns):
        own_x[i].wait_recv()
        piece = keys_ref.at[y, lax.rem(x - k + nx, nx), z, rows]
        for to in y_peers:
            moves.append(push(slot, piece, piece, to))
            slot += 1
    for i, k in enumerate(turns):
        other_y[i].wait_recv()
        piece = keys_ref.at[lax.rem(y - k + ny, ny), x, 1 - z]
        for to in x_peers:
            moves.append(push(slot, piece, piece, to))
            slot += 1
    for copy in here + stores:
        copy.wait()
    for copy in copies + [swap] + own_x + other_y:
        copy.wait_send()
    for copy in moves:
        copy.wait()


def split_two(value):
    high = value.astype(BF16)
    low = (value - high.astype(F32)).astype(BF16)
    return high, low


def spread_over(weight):
    m, c = weight.shape
    up = (
        lax.broadcasted_iota(jnp.int32, (m * GROUP, m), 0) // GROUP
        == lax.broadcasted_iota(jnp.int32, (m * GROUP, m), 1)
    ).astype(F32)
    across = (
        lax.broadcasted_iota(jnp.int32, (c, c * GROUP), 1) // GROUP
        == lax.broadcasted_iota(jnp.int32, (c, c * GROUP), 0)
    ).astype(F32)
    tall = jnp.dot(up, weight, precision=HIGHEST, preferred_element_type=F32)
    wide = jnp.dot(tall, across, precision=HIGHEST, preferred_element_type=F32)
    same = (
        lax.broadcasted_iota(jnp.int32, (m * GROUP, c * GROUP), 0) % GROUP
        == lax.broadcasted_iota(jnp.int32, (m * GROUP, c * GROUP), 1) % GROUP
    )
    return jnp.where(same, wide, 0.0)


def pair_weights(w1, b1, w2t, head_size, wfirst, wsecond):
    feats, hid = w1.shape
    root = math.sqrt(head_size)
    first = jnp.concatenate([w1, b1, jnp.zeros((8 - feats - 1, hid), F32)], axis=0)
    line = lax.dot_general(
        w2t, first, (((1,), (1,)), ((), ())), precision=HIGHEST, preferred_element_type=F32
    ) * (0.5 * root)
    part = feats * GROUP

    stacked = jnp.concatenate([first.T * (1.0 / GELU_S), line], axis=0)
    high, low = split_two(spread_over(stacked))
    wfirst[:, 0:part] = high[:, 0:part]
    wfirst[:, part : 2 * part] = high[:, 0:part]
    wfirst[:, 2 * part : 3 * part] = low[:, 0:part]
    wfirst[:, 3 * part : 3 * part + GROUP] = high[:, part : part + GROUP]
    wfirst[:, 3 * part + GROUP : 3 * part + 2 * GROUP] = low[:, part : part + GROUP]
    wsecond[...] = spread_over(w2t * (0.5 * root * GELU_S)).astype(BF16)


def attend_kernel(
    heads,
    pair_hbm,
    keys_hbm,
    wq_hbm,
    wk_hbm,
    wv_hbm,
    first_hbm,
    second_hbm,
    keep_hbm,
    send_hbm,
    pair_ref,
    keys_ref,
    wq_ref,
    wk_ref,
    wv_ref,
    wfirst,
    wsecond,
    load_sem,
    kt_ref,
    v_ref,
    terms,
    q_terms,
    qm_ref,
    s_ref,
    top_ref,
    total_ref,
    acc_ref,
    fresh,
    hidden,
    linear,
    turned,
    weight_ref,
    held_ref,
    ranges,
    limits,
):
    loads = [
        pltpu.make_async_copy(src, dst, load_sem.at[i])
        for i, (src, dst) in enumerate(
            [
                (keys_hbm, keys_ref),
                (pair_hbm, pair_ref),
                (wk_hbm, wk_ref),
                (wv_hbm, wv_ref),
                (wq_hbm, wq_ref),
                (first_hbm, wfirst),
                (second_hbm, wsecond),
            ]
        )
    ]
    for load in loads:
        load.start()
    nz, slots, width = held_ref.shape[0], held_ref.shape[1] - 2 * heads, held_ref.shape[2]
    ny, nx = keys_ref.shape[0:2]
    half = slots // nz
    own_rows = nz * slots
    head_size = width // heads
    hid = wsecond.shape[1] // GROUP
    root = math.sqrt(head_size)
    groups = UNIT // GROUP
    rows_g = heads * GROUP
    rows_u = groups * rows_g
    n_units = own_rows // UNIT
    n_tiles = nz * ny
    per_step = TILE // LANES
    z = lax.axis_index("blk") // (ny * nx)

    for load in loads:
        load.wait()

    def terms_of(mom, rap, azi, mass, ids):
        trans = jnp.sqrt(mom * mom + mass * mass)
        return (
            mom,
            rap,
            jnp.cos(azi),
            jnp.sin(azi),
            trans * jnp.exp(rap),
            trans * jnp.exp(-rap),
            mass * mass,
            ids,
        )

    body = half * (width // 128)
    lower = lax.broadcasted_iota(jnp.int32, (KIN_ROWS, 128), 1) < half
    ends = [[] for _ in range(nz)]
    for yy in range(ny):
        tails = [
            keys_ref[yy, xx, 1 - z, body : body + KIN_ROWS, :].astype(F32) for xx in range(nx)
        ]
        turned_tails = [jnp.concatenate([e[:, half:], e[:, :half]], axis=1) for e in tails]
        ends[0].append(
            [jnp.where(lower, tails[k], turned_tails[k + 1]) for k in range(0, nx, 2)]
        )
        ends[1].append(
            [jnp.where(lower, turned_tails[k], tails[k + 1]) for k in range(0, nx, 2)]
        )
    ends = [jnp.concatenate(end, axis=1) for zz in range(nz) for end in ends[zz]]
    raw_terms = [jnp.concatenate([end[i : i + 1] for end in ends], axis=0) for i in range(5)]
    n_rows = n_tiles * TILE // LANES
    raw_terms = [
        jnp.concatenate(
            [
                term[t : t + 1, k : k + LANES]
                for t in range(n_tiles)
                for k in range(0, TILE, LANES)
            ],
            axis=0,
        )
        for term in raw_terms
    ]
    for i, term in enumerate(terms_of(*raw_terms)):
        terms[i, 0:n_rows, :] = term
        terms[i, n_rows : n_rows + 8, :] = jnp.full((8, LANES), -1.0 if i == 7 else 1.0, F32)
    ends = [pair_ref[zz, slots : slots + KIN_ROWS, 0:slots].astype(F32) for zz in range(nz)]
    raw_terms = [
        jnp.concatenate([ends[zz][i : i + 1] for zz in range(nz)], axis=0) for i in range(5)
    ]
    for i, term in enumerate(terms_of(*raw_terms)):
        for zz in range(nz):
            q_terms[i, zz * slots : (zz + 1) * slots, :] = jnp.broadcast_to(
                term[zz : zz + 1], (slots, slots)
            ).T

    counts = []
    for row in (0, UNIT - 1):
        bound = q_terms[7, pl.ds(row, n_units, stride=UNIT), :]
        count = jnp.zeros((n_units, 128), F32)
        for t in range(n_rows):
            key = terms[7, t : t + 1, :]
            count = count + jnp.where(key < bound if row == 0 else key <= bound, 1.0, 0.0)
        counts.append(jnp.sum(count, axis=1, keepdims=True).astype(jnp.int32))
    start = jnp.minimum(counts[0] // LANES, n_rows - 1)
    stop = jnp.maximum((counts[1] + (LANES - 1)) // LANES, start + 1)
    ranges[0] = start + jnp.zeros((n_units, 128), jnp.int32)
    ranges[1] = (stop - start + (per_step - 1)) // per_step + jnp.zeros((n_units, 128), jnp.int32)
    to_scalars = pltpu.make_async_copy(ranges, limits, load_sem.at[7])
    to_scalars.start()

    wkt = wk_ref[...].astype(F32).T.astype(BF16)
    for yy in range(ny):
        for zz in range(nz):
            rows = jnp.concatenate(
                [
                    jnp.concatenate(
                        [keys_ref[yy, xx, zz, i : i + half, :] for i in range(0, body, half)],
                        axis=1,
                    )
                    for xx in range(nx)
                ],
                axis=0,
            )
            at = slice((zz * ny + yy) * TILE, (zz * ny + yy + 1) * TILE)
            kt_ref[:, at] = lax.dot_general(
                wkt, rows, (((1,), (1,)), ((), ())), preferred_element_type=F32
            ).astype(BF16)
            v_ref[at, :] = jnp.dot(rows, wv_ref[...], preferred_element_type=F32).astype(BF16)

    kt_ref[:, n_tiles * TILE :] = jnp.zeros((width, LANES), BF16)
    v_ref[n_tiles * TILE :, :] = jnp.zeros((LANES, width), BF16)

    lane_head = lax.broadcasted_iota(jnp.int32, (GROUP, width), 1) // head_size
    for zz in range(nz):
        queries = jnp.dot(pair_ref[zz, 0:slots, :], wq_ref[...], preferred_element_type=F32)
        for base in range(0, slots, GROUP):
            rows = queries[base : base + GROUP]
            at = (zz * slots + base) * heads
            qm_ref[at : at + rows_g, :] = jnp.concatenate(
                [jnp.where(lane_head == h, rows, 0.0) for h in range(heads)], axis=0
            ).astype(BF16)

    top_ref[...] = jnp.full_like(top_ref, -1e30)
    total_ref[...] = jnp.zeros_like(total_ref)
    acc_ref[...] = jnp.zeros_like(acc_ref)

    to_scalars.wait()

    def following(u, k):
        more = k + 1 < limits[1, u, 0]
        return jnp.where(more, u, jnp.minimum(u + 1, n_units - 1)), jnp.where(more, k + 1, 0)

    steps = limits[1, 0, 0]
    for u in range(1, n_units):
        steps = steps + limits[1, u, 0]

    def place(u, k):
        return limits[0, u, 0] + k * per_step

    def features(p, u, k):
        t = place(u, k)
        for g in range(groups):
            base = pl.multiple_of(u * UNIT + g * GROUP, GROUP)
            qt = [q_terms[i, pl.ds(base, GROUP), :] for i in range(7)]
            columns = []
            for i in range(per_step):
                kt = [terms[j, pl.ds(t + i, 1), :] for j in range(7)]
                gap = qt[1] - kt[1]
                cos_gap = qt[2] * kt[2] + qt[3] * kt[3]
                dist = gap * gap + (2.0 - 2.0 * cos_gap)
                small = jnp.minimum(qt[0], kt[0])
                msq = (
                    qt[6]
                    + kt[6]
                    + (qt[4] * kt[5] + qt[5] * kt[4] - 2.0 * (qt[0] * kt[0] * cos_gap))
                )
                f = [
                    jnp.log(1.0 + dist),
                    jnp.log(1.0 + small * small * dist),
                    small / (qt[0] + kt[0]),
                    jnp.log(1.0 + msq),
                ]
                fh, fl = split_two(jnp.concatenate(f, axis=0))
                columns.append(
                    jnp.concatenate([fh, fl, fh, jnp.ones((2 * GROUP, 128), BF16)], axis=0)
                )
            fresh[p, g] = jnp.concatenate(columns, axis=1)

    def hiddens(p):
        for g in range(groups):
            z = jnp.dot(wfirst[...], fresh[p, g], preferred_element_type=F32)
            hidden[p, g] = z[0 : hid * GROUP].astype(BF16)
            linear[p, g] = z[hid * GROUP :]

    def gelus(p):
        for g in range(groups):
            inner = hidden[p, g]
            turned[p, g] = inner * jnp.tanh(inner * (ALPHA + inner * inner))

    def scores(p, u, k, away):
        t = place(u, k)
        start = pl.multiple_of(t * LANES, LANES)
        first_row = pl.multiple_of(u * rows_u, rows_u)
        products = jnp.dot(
            qm_ref[pl.ds(first_row, rows_u), :],
            kt_ref[:, pl.ds(start, TILE)],
            preferred_element_type=F32,
        )
        for g in range(groups):
            base = pl.multiple_of(u * UNIT + g * GROUP, GROUP)
            bias = jnp.dot(wsecond[...], turned[p, g], preferred_element_type=F32)
            s = products[g * rows_g : (g + 1) * rows_g] + (bias + linear[p, g])
            own = q_terms[7, pl.ds(base, GROUP), :] + away
            live = jnp.concatenate(
                [own == terms[7, pl.ds(t + i, 1), :] for i in range(per_step)], axis=1
            )
            s = jnp.where(live[None], s.reshape(heads, GROUP, TILE), -1e30).reshape(rows_g, TILE)
            at = pl.ds(pl.multiple_of(first_row + g * rows_g, rows_g), rows_g)
            s_ref[at, pl.ds(start, TILE)] = s
            run_max = top_ref[at, :]
            for i in range(0, TILE, 128):
                run_max = jnp.maximum(run_max, s[:, i : i + 128])
            top_ref[at, :] = run_max

    def score_steps(i, carry):
        for k in range(SCORE_STEPS):
            p = k % 2
            u0, t0, u1, t1, u2, t2, u3, t3 = carry
            scores(1 - p, u3, t3, jnp.where(SCORE_STEPS * i + k >= 3, 0.0, 100.0))
            hiddens(1 - p)
            gelus(p)
            features(p, u0, t0)
            carry = (*following(u0, t0), u0, t0, u1, t1, u2, t2)
        return carry

    zero = jnp.int32(0)
    lax.fori_loop(0, (steps + SCORE_STEPS + 2) // SCORE_STEPS, score_steps, (zero,) * 8)

    for u in range(n_units):
        at = slice(u * rows_u, (u + 1) * rows_u)
        top_ref[at, :] = jnp.broadcast_to(
            jnp.max(top_ref[at, :], axis=1, keepdims=True), (rows_u, 128)
        )

    weight_ref[...] = jnp.zeros_like(weight_ref)

    def apply(p, u, k):
        at = pl.ds(pl.multiple_of(u * rows_u, rows_u), rows_u)
        acc_ref[at, :] += jnp.dot(
            weight_ref[p],
            v_ref[pl.ds(pl.multiple_of(place(u, k) * LANES, LANES), TILE), :],
            preferred_element_type=F32,
        )

    def weigh(p, u, k, above):
        t = place(u, k)
        at = pl.ds(pl.multiple_of(u * rows_u, rows_u), rows_u)
        top = top_ref[at, :] + above
        total = total_ref[at, :]
        for i in range(0, TILE, 128):
            cols = pl.ds(pl.multiple_of(t * LANES + i, 128), 128)
            weight = jnp.exp2((s_ref[at, cols] - top) * (LOG2E / root))
            total = total + weight
            weight_ref[p, :, i : i + 128] = weight.astype(BF16)
        total_ref[at, :] = total

    def value_steps(i, carry):
        for k in range(VALUE_STEPS):
            u0, t0, u1, t1 = carry
            apply(1 - k % 2, u1, t1)
            weigh(k % 2, u0, t0, jnp.where(VALUE_STEPS * i + k < steps, 0.0, 1e32))
            carry = (*following(u0, t0), u0, t0)
        return carry

    lax.fori_loop(0, (steps + VALUE_STEPS) // VALUE_STEPS, value_steps, (zero,) * 4)

    lane = lax.broadcasted_iota(jnp.int32, (rows_g, slots), 1)
    row = lax.rem(lax.broadcasted_iota(jnp.int32, (rows_g, slots), 0), GROUP)
    for zz in range(nz):
        level = jnp.zeros((rows_g, slots), F32)
        weight = jnp.ones((rows_g, slots), F32)
        for base in range(0, slots, GROUP):
            at = (zz * slots + base) * heads
            total = jnp.sum(total_ref[at : at + rows_g, :], axis=1, keepdims=True)
            here = lane == base + row
            level = jnp.where(here, top_ref[at : at + rows_g, :], level)
            weight = jnp.where(here, total, weight)
            total = 1.0 / total
            sides = []
            for i in range(0, width, 128):
                out = jnp.zeros((GROUP, 128), F32)
                for h in range(i // head_size, (i + 128) // head_size):
                    rows = slice(at + h * GROUP, at + (h + 1) * GROUP)
                    scaled = acc_ref[rows, i : i + 128] * total[h * GROUP : (h + 1) * GROUP]
                    out = jnp.where(lane_head[:, i : i + 128] == h, scaled, out)
                sides.append(out)
            out = jnp.concatenate(sides, axis=1)
            acc_ref[base : base + GROUP, :] = out
        held_ref[zz, 0:slots, :] = acc_ref[0:slots, :].astype(BF16)
        there = lax.rem(lane, GROUP) == row
        level = jnp.where(there, level * (LOG2E / root) + jnp.log(weight) * LOG2E, 0.0)
        level = jnp.sum(level.reshape(heads, GROUP, slots), axis=1)
        high, middle = split_two(level)
        low = (level - high.astype(F32) - middle.astype(F32)).astype(BF16)
        held_ref[zz, slots : slots + 2 * heads, :] = jnp.concatenate(
            [
                jnp.concatenate([high, middle], axis=1),
                jnp.concatenate([low, jnp.zeros_like(low)], axis=1),
            ],
            axis=0,
        )
    stores = [
        pltpu.make_async_copy(held_ref.at[z], keep_hbm, load_sem.at[0]),
        pltpu.make_async_copy(held_ref.at[1 - z], send_hbm, load_sem.at[1]),
    ]
    for store in stores:
        store.start()
    for store in stores:
        store.wait()


def finish_kernel(
    heads,
    keep_ref,
    came_ref,
    wo_ref,
    gain_ref,
    out_ref,
):
    slots, width = out_ref.shape
    spread = (
        lax.broadcasted_iota(jnp.int32, (heads, width), 1) // (width // heads)
        == lax.broadcasted_iota(jnp.int32, (heads, width), 0)
    ).astype(F32)

    def level_of(ref):
        pieces = ref[slots : slots + 2 * heads, :].astype(F32)
        return pieces[0:heads, 0:slots] + pieces[0:heads, slots:] + pieces[heads:, 0:slots]

    share = 1.0 / (1.0 + jnp.exp2(level_of(came_ref) - level_of(keep_ref)))
    share = jnp.dot(share.T, spread, precision=HIGHEST, preferred_element_type=F32)
    theirs = came_ref[0:slots, :].astype(F32)
    attended = theirs + share * (keep_ref[0:slots, :].astype(F32) - theirs)
    mixed = jnp.dot(attended.astype(BF16), wo_ref[...], preferred_element_type=F32)
    out_ref[...] = layer_norm(mixed, gain_ref[...]).astype(BF16)


def shards(
    n_grp,
    cube,
    raw,
    raw_kin,
    reader,
    event_id,
    pre_gain,
    w_query,
    w_key,
    w_value,
    w_out,
    post_gain,
    pair_w1,
    pair_b1,
    pair_w2,
):
    slots, width = raw.shape[2], raw.shape[3]
    heads = pair_w2.shape[1]
    nz, ny, nx = cube
    vmem = pl.BlockSpec(memory_space=pltpu.VMEM)
    free = pl.BlockSpec(memory_space=pl.ANY)
    dma = pltpu.SemaphoreType.DMA
    tall = slots + KIN_ROWS
    part_rows = slots // nz * (width // 128) + KIN_ROWS
    feats, hid = pair_w1.shape
    mixing = (3 * feats + 2) * GROUP
    pair, keys, first, second = pl.pallas_call(
        functools.partial(exchange_kernel, n_grp, cube),
        out_shape=(
            jax.ShapeDtypeStruct((nz, tall, width), BF16),
            jax.ShapeDtypeStruct((ny, nx, nz, part_rows, 128), BF16),
            jax.ShapeDtypeStruct(((hid + heads) * GROUP, mixing), BF16),
            jax.ShapeDtypeStruct((heads * GROUP, hid * GROUP), BF16),
        ),
        in_specs=[free] * 8,
        out_specs=(free,) * 4,
        scratch_shapes=[
            pltpu.VMEM(raw_kin.shape, BF16),
            pltpu.VMEM(reader.shape, jnp.int32),
            pltpu.VMEM(event_id.shape, jnp.int32),
            pltpu.VMEM((1, width), F32),
            pltpu.VMEM((feats, hid), F32),
            pltpu.VMEM((1, hid), F32),
            pltpu.VMEM((heads, hid), F32),
            pltpu.VMEM(((hid + heads) * GROUP, mixing), BF16),
            pltpu.VMEM((heads * GROUP, hid * GROUP), BF16),
            dma((8,)),
            pltpu.VMEM((n_grp, slots, width), BF16),
            pltpu.VMEM((n_grp, 8, slots), F32),
            pltpu.VMEM((n_grp, 8, slots), F32),
            pltpu.VMEM((tall, width), BF16),
            pltpu.VMEM((part_rows - KIN_ROWS, 128), BF16),
            pltpu.VMEM((part_rows, 128), BF16),
            pltpu.VMEM((part_rows, 128), BF16),
            dma((n_grp,)),
            dma((n_grp,)),
            dma((n_grp,)),
            dma((n_grp,)),
            dma((32,)),
            dma((32,)),
            dma((3,)),
        ],
        compiler_params=pltpu.CompilerParams(collective_id=0, has_side_effects=True),
        name="exchange",
    )(
        raw,
        raw_kin,
        reader,
        event_id,
        pre_gain[None],
        pair_w1,
        pair_b1[None],
        pair_w2.T,
    )

    own_rows = nz * slots
    n_tiles = nz * ny
    groups = UNIT // GROUP
    rows_all = heads * own_rows
    keep, send = pl.pallas_call(
        functools.partial(attend_kernel, heads),
        out_shape=(jax.ShapeDtypeStruct((slots + 2 * heads, width), BF16),) * 2,
        in_specs=[free] * 7,
        out_specs=(free, free),
        scratch_shapes=[
            pltpu.VMEM((nz, tall, width), BF16),
            pltpu.VMEM((ny, nx, nz, part_rows, 128), BF16),
            pltpu.VMEM((width, width), BF16),
            pltpu.VMEM((width, width), BF16),
            pltpu.VMEM((width, width), BF16),
            pltpu.VMEM(((hid + heads) * GROUP, mixing), BF16),
            pltpu.VMEM((heads * GROUP, hid * GROUP), BF16),
            dma((8,)),
            pltpu.VMEM((width, n_tiles * TILE + LANES), BF16),
            pltpu.VMEM((n_tiles * TILE + LANES, width), BF16),
            pltpu.VMEM((8, n_tiles * TILE // LANES + 8, LANES), F32),
            pltpu.VMEM((8, own_rows, slots), F32),
            pltpu.VMEM((rows_all, width), BF16),
            pltpu.VMEM((rows_all, n_tiles * TILE + LANES), F32),
            pltpu.VMEM((rows_all, 128), F32),
            pltpu.VMEM((rows_all, 128), F32),
            pltpu.VMEM((rows_all, width), F32),
            pltpu.VMEM((2, groups, mixing, TILE), BF16),
            pltpu.VMEM((2, groups, hid * GROUP, TILE), BF16),
            pltpu.VMEM((2, groups, heads * GROUP, TILE), F32),
            pltpu.VMEM((2, groups, hid * GROUP, TILE), BF16),
            pltpu.VMEM((2, heads * UNIT, TILE), BF16),
            pltpu.VMEM((nz, slots + 2 * heads, width), BF16),
            pltpu.VMEM((2, own_rows // UNIT, 128), jnp.int32),
            pltpu.SMEM((2, own_rows // UNIT, 128), jnp.int32),
        ],
        compiler_params=pltpu.CompilerParams(vmem_limit_bytes=63 * 1024 * 1024),
        name="attend",
    )(pair, keys, w_query, w_key, w_value, first, second)

    n_blk = nz * ny * nx
    swap = [(i, (i + ny * nx) % n_blk) for i in range(n_blk)]
    came = lax.ppermute(send, "blk", swap)
    encoded = pl.pallas_call(
        functools.partial(finish_kernel, heads),
        out_shape=jax.ShapeDtypeStruct((slots, width), BF16),
        in_specs=[vmem] * 4,
        out_specs=vmem,
        compiler_params=pltpu.CompilerParams(vmem_limit_bytes=8 * 1024 * 1024),
        name="finish",
    )(keep.astype(F32), came, w_out, post_gain[None])
    return encoded[None]


def solution(mesh):
    in_specs = (
        P("grp", None, "blk", None),
        P("grp", None, None, "blk"),
        P("grp", "blk"),
        P("grp", "blk"),
        P(),
        P(),
        P(),
        P(),
        P(),
        P(),
        P(),
        P(),
        P(),
    )
    out_specs = P("grp", "blk", None)
    cube = (2, 4, mesh.shape["blk"] // 8)
    body = functools.partial(shards, mesh.shape["grp"], cube)
    return jax.shard_map(body, mesh=mesh, in_specs=in_specs, out_specs=out_specs, check_vma=False)
```
